32 devices in a mesh: section: 2 (over core), seq: 16 (over z, y, x).
Axes of the slice: x: 2, y: 2, z: 4, core: 2. Of those that a mesh axis runs over, the one named last changes fastest.
Arguments:
- inputs: bfloat16 [2, 4096, 1536], P(None, 'seq'), may hold values from -6 to 6
- cotangent: bfloat16 [2, 4096, 1536], P(None, 'seq'), may hold values from -6 to 6
- norm_gain: float32 [2, 1536], P('section'), may hold values from 0.5 to 1.5
- in_weight: bfloat16 [2, 1536, 6448], P('section'), may hold values from -0.15625 to 0.15625
- conv_weight: float32 [2, 3328, 4], P('section'), may hold values from -3 to 3
- conv_bias: float32 [2, 3328], P('section'), may hold values from -0.5 to 0.5
- dt_bias: float32 [2, 48], P('section'), may hold values from -4.5 to -3.5
- a_log: float32 [2, 48], P('section'), may hold values from -8 to 1, as said below
- d_skip: float32 [2, 48], P('section'), may hold values from 0.5 to 1.5
- gate_norm_gain: float32 [2, 3072], P('section'), may hold values from 0.5 to 1.5
- out_weight: bfloat16 [2, 3072, 1536], P('section'), may hold values from -0.109375 to 0.109375
Outputs:
- acts: bfloat16 [2, 2, 4096, 1536], P('section', None, 'seq')
- input_grads: float32 [2, 2, 4096, 1536], P('section', None, 'seq')
- grad_norm_gain: float32 [2, 1536], P('section', 'seq')
- grad_in_weight: float32 [2, 1536, 6448], P('section', 'seq')
- grad_conv_weight: float32 [2, 3328, 4], P('section', 'seq')
- grad_conv_bias: float32 [2, 3328], P('section', 'seq')
- grad_dt_bias: float32 [2, 48], P('section')
- grad_a_log: float32 [2, 48], P('section')
- grad_d_skip: float32 [2, 48], P('section')
- grad_gate_norm_gain: float32 [2, 3072], P('section', 'seq')
- grad_out_weight: float32 [2, 3072, 1536], P('section', 'seq')
The draws below stay inside these ranges and needn't reach their ends.
Inputs may be any that keep to these rules, and one draw needn't show every extreme that they name: Per layer and head, a_log is log(rate / 0.03) for a decay rate per unit step.
All inputs are finite; a program needn't handle non-finite values.
Results may differ from the reference program's by a relative error of at most 0.015.
The reference program's roundings to bfloat16 on the way (of `normed`) count: a program that leaves them out, or rounds other values in their place, can miss the bound.
Values may be sent and summed in bfloat16 or wider, within the bound.
A program may use at most 576 MiB of HBM per device.

```python
import jax
import jax.numpy as jnp
from jax import lax

D = 1536
INNER = 3072
STATE = 128
HEADDIM = 64
CONV = 4
GROUP = 256
MICRO = 2
HEADS = 48
CONVD = 3328
PROJ = 6448
LAYERS = 2
SEQ_LEN = 4096


def draw_a_log(key, part):
    key = jax.random.fold_in(key, 7)
    key_pick, key_slow, key_fast = jax.random.split(key, 3)
    slow_share = 0.5
    slow = jax.random.bernoulli(key_pick, slow_share, (LAYERS, HEADS))
    slow_rate = jnp.exp(jax.random.uniform(key_slow, (LAYERS, HEADS), jnp.float32, jnp.log(0.3), jnp.log(2.0))) / SEQ_LEN
    fast_rate = jnp.exp(jax.random.uniform(key_fast, (LAYERS, HEADS), jnp.float32, jnp.log(0.02), jnp.log(0.06)))
    rate = jnp.where(slow, slow_rate, fast_rate)
    return jnp.log(rate / 0.03).astype(jnp.float32)


def block_scale(key, dims, shards, least, top_value):
    factor_of, own = 1.0, jax.random.fold_in(key, 6)
    for dim, shards_of in shards:
        heights = jnp.exp(jax.random.uniform(jax.random.fold_in(own, dim), (shards_of,), jnp.float32, least / len(shards), top_value / len(shards)))
        factor_of = factor_of * jnp.repeat(heights, dims[dim] // shards_of).reshape([-1 if axis == dim else 1 for axis in range(len(dims))])
    return factor_of


def normal_values(key, shape, spread, most, cuts=(), held_as=jnp.bfloat16):
    values = spread * jax.random.normal(key, shape, jnp.float32)
    if cuts:
        values = values * block_scale(key, shape, cuts, -0.22, 0.18)
    return jnp.clip(values, -most, most).astype(held_as)


def setup_inputs(seed: int = 0) -> dict:
    splits = jax.random.split(jax.random.key(seed), 12)
    return {
        "inputs": normal_values(splits[0], (MICRO, SEQ_LEN, D), 1.0, 6.0, ((1, 16),)),
        "cotangent": normal_values(splits[1], (MICRO, SEQ_LEN, D), 1.0, 6.0, ((1, 16),)),
        "norm_gain": jnp.clip(1.0 + 0.1 * jax.random.normal(splits[2], (LAYERS, D), jnp.float32), 0.5, 1.5),
        "in_weight": normal_values(splits[3], (LAYERS, D, PROJ), D ** -0.5, 0.15625, ((0, 2),)),
        "conv_weight": normal_values(splits[4], (LAYERS, CONVD, CONV), CONV ** -0.5, 3.0, ((0, 2),), jnp.float32),
        "conv_bias": jnp.clip(jax.random.uniform(splits[5], (LAYERS, CONVD), jnp.float32, -0.5, 0.5) * block_scale(splits[5], (LAYERS, CONVD), ((0, 2),), -0.4, 0.0), -0.5, 0.5),
        "dt_bias": jnp.clip(-4.5 + 1.0 * jax.random.uniform(splits[6], (LAYERS, HEADS), jnp.float32) ** block_scale(splits[6], (LAYERS, HEADS), ((0, 2),), -0.2, 0.2), -4.5, -3.5),
        "a_log": draw_a_log(jax.random.fold_in(splits[11], 71), 0),
        "d_skip": jnp.clip(0.5 + 1.0 * jax.random.uniform(splits[8], (LAYERS, HEADS), jnp.float32) ** block_scale(splits[8], (LAYERS, HEADS), ((0, 2),), -0.2, 0.2), 0.5, 1.5),
        "gate_norm_gain": jnp.clip(1.0 + 0.1 * jax.random.normal(splits[9], (LAYERS, INNER), jnp.float32), 0.5, 1.5),
        "out_weight": normal_values(splits[10], (LAYERS, INNER, D), INNER ** -0.5, 0.109375, ((0, 2),)),
    }


HIGH = lax.Precision.HIGHEST
epsilon_norm = 1e-05

@jax.custom_vjp
def low(v):
    return lax.optimization_barrier(v.astype(jnp.bfloat16)).astype(jnp.float32)

@jax.custom_vjp
def low_back(v):
    return v

def low_keep(v):
    return (low(v), None)

def low_pass(kept, grad):
    return (grad,)

def back_keep(v):
    return (v, None)

def back_low(kept, grad):
    return (low(grad),)
low.defvjp(low_keep, low_pass)
low_back.defvjp(back_keep, back_low)

def rms_scale(value, gain):
    return value * lax.rsqrt(lax.optimization_barrier(jnp.mean(value * value, axis=-1, keepdims=True)) + epsilon_norm) * gain

def ssd_block(carry_state, pieces):
    scaled, decay_log, b_proj, c_proj = pieces
    size = decay_log.shape[0]
    cumulative = jnp.cumsum(decay_log, axis=0)
    by_head = cumulative.T
    row_ids = lax.broadcasted_iota(jnp.int32, (size, size), 0)
    col_ids = lax.broadcasted_iota(jnp.int32, (size, size), 1)
    lower_mask = (row_ids >= col_ids)[None, :, :]
    segment = by_head[:, :, None] - by_head[:, None, :]
    decay = jnp.exp(jnp.where(lower_mask, segment, -jnp.inf))
    intersection = jnp.dot(c_proj, b_proj.T, precision=HIGH)
    mixing = intersection[None, :, :] * decay
    intra_out = jnp.einsum('hts,shp->thp', mixing, scaled, precision=HIGH)
    state_out = jnp.exp(cumulative)[:, :, None] * jnp.einsum('tn,hpn->thp', c_proj, carry_state, precision=HIGH)
    to_end = jnp.exp(cumulative[-1][None, :] - cumulative)
    new_state = jnp.exp(cumulative[-1])[:, None, None] * carry_state + jnp.einsum('sh,shp,sn->hpn', to_end, scaled, b_proj, precision=HIGH)
    return (new_state, intra_out + state_out)

def layer(stream, params):
    norm_g, w_in, conv_w, conv_b, dt_b, a_lg, skip_w, gate_g, w_out = params
    seq_rows = stream.shape[0]
    normed = low(rms_scale(stream, norm_g))
    projected = low_back(jnp.dot(normed, w_in, precision=HIGH))
    gate_in = projected[:, :INNER]
    conv_in = projected[:, INNER:INNER + CONVD]
    step_raw = projected[:, INNER + CONVD:]
    extended = jnp.concatenate([jnp.zeros((CONV - 1, CONVD), jnp.float32), conv_in], axis=0)
    convolved = conv_b + jnp.zeros((seq_rows, CONVD), jnp.float32)
    for offset in range(CONV):
        convolved = convolved + extended[offset:offset + seq_rows] * conv_w[:, offset]
    activated = jax.nn.silu(convolved)
    values = activated[:, :INNER].reshape(seq_rows, HEADS, HEADDIM)
    b_proj = activated[:, INNER:INNER + STATE]
    c_proj = activated[:, INNER + STATE:]
    step_size = jax.nn.softplus(step_raw + dt_b)
    decay_log = -jnp.exp(a_lg) * step_size
    scaled = values * step_size[:, :, None]
    blocks = seq_rows // GROUP

    def by_block(value):
        return value.reshape((blocks, GROUP) + value.shape[1:])
    start = jnp.zeros((HEADS, HEADDIM, STATE), jnp.float32)
    _, outputs = lax.scan(jax.checkpoint(ssd_block), start, (by_block(scaled), by_block(decay_log), by_block(b_proj), by_block(c_proj)))
    mixed = outputs.reshape(seq_rows, HEADS, HEADDIM) + skip_w[:, None] * values
    gated = mixed.reshape(seq_rows, INNER) * jax.nn.silu(gate_in)
    gated_low = low(rms_scale(gated, gate_g))
    out = low_back(jnp.dot(gated_low, w_out, precision=HIGH))
    return stream + out

def reference(inputs, cotangent, norm_gain, in_weight, conv_weight, conv_bias, dt_bias, a_log, d_skip, gate_norm_gain, out_weight):
    stacked = tuple((value.astype(jnp.float32) for value in (norm_gain, in_weight, conv_weight, conv_bias, dt_bias, a_log, d_skip, gate_norm_gain, out_weight)))
    first_params = tuple((value[0] for value in stacked))
    second_params = tuple((value[1] for value in stacked))

    def forward(layer_input, probe_zero, params_one, params_two):
        middle = layer(layer_input, params_one)
        middle_low = low(middle)
        handed = low_back(middle_low) + probe_zero
        final_out = layer(handed, params_two)
        return (final_out, middle_low)
    acts_first, acts_second, grads_first, grads_second = ([], [], [], [])
    totals_one = None
    totals_two = None
    for index in range(MICRO):
        layer_input = inputs[index].astype(jnp.float32)
        probe_zero = jnp.zeros_like(layer_input)
        (final_out, middle_low), pull = jax.vjp(forward, layer_input, probe_zero, first_params, second_params)
        d_input, d_probe, d_one, d_two = pull((cotangent[index].astype(jnp.float32), jnp.zeros_like(middle_low)))
        acts_first.append(middle_low.astype(jnp.bfloat16))
        acts_second.append(final_out.astype(jnp.bfloat16))
        grads_first.append(d_input)
        grads_second.append(d_probe)
        if totals_one is None:
            totals_one, totals_two = (d_one, d_two)
        else:
            totals_one = jax.tree.map(jnp.add, totals_one, d_one)
            totals_two = jax.tree.map(jnp.add, totals_two, d_two)
    acts = jnp.stack([jnp.stack(acts_first), jnp.stack(acts_second)])
    input_grads = jnp.stack([jnp.stack(grads_first), jnp.stack(grads_second)])
    weight_grads = tuple((jnp.stack([left_value, right_value]) for left_value, right_value in zip(totals_one, totals_two)))
    return (acts, input_grads, weight_grads[0], weight_grads[1], weight_grads[2], weight_grads[3], weight_grads[4], weight_grads[5], weight_grads[6], weight_grads[7], weight_grads[8])
```

```python
import functools

import jax
import jax.numpy as jnp
from jax import lax
from jax.experimental import pallas as pl
from jax.experimental.pallas import tpu as pltpu
from jax.sharding import PartitionSpec as P

D = 1536
INNER = 3072
STATE = 128
HEADS = 48
HEADDIM = 64
CONV = 4
CONVD = 3328
PROJ = 6448
ROWS = 256
PAIRS = INNER // 128
PLANE = 4
LANES = INNER // PLANE
QUARTER = 1664
EPS = 1e-05
MIB = 2**20
MESH = pl.DeviceIdType.MESH
F32 = jnp.float32
BF16 = jnp.bfloat16


def dot_nn(a, b):
    return lax.dot_general(a, b, (((1,), (0,)), ((), ())), preferred_element_type=F32)


def dot_tn(a, b):
    return lax.dot_general(a, b, (((0,), (0,)), ((), ())), preferred_element_type=F32)


def dot_nt(a, b):
    return lax.dot_general(a, b, (((1,), (1,)), ((), ())), preferred_element_type=F32)


def split3(v):
    high = v.astype(BF16)
    rest = v - high.astype(F32)
    mid = rest.astype(BF16)
    return high, mid, (rest - mid.astype(F32)).astype(BF16)


def split2(v):
    high = v.astype(BF16)
    return high, (v - high.astype(F32)).astype(BF16)


def fine(dot, a, b):
    return dot(a[0], b[0]) + (dot(a[0], b[1]) + dot(a[1], b[0]))


def halves(ref):
    return ref[:, 0:128], ref[:, 128:256]


def exact_right(v, ones):
    a, b, c = split3(v)
    return dot_nn(a, ones) + (dot_nn(b, ones) + dot_nn(c, ones))


def exact_left(ones, v):
    a, b, c = split3(v)
    return dot_nn(ones, a) + (dot_nn(ones, b) + dot_nn(ones, c))


def iota(shape, dim):
    return lax.broadcasted_iota(jnp.int32, shape, dim)


def expander(pair):
    head_of = 2 * pair + (iota((128, 128), 1) >= HEADDIM).astype(jnp.int32)
    return (iota((128, 128), 0) == head_of).astype(F32).astype(BF16)


def collector(pair):
    head_of = 2 * pair + (iota((128, 128), 0) >= HEADDIM).astype(jnp.int32)
    return (iota((128, 128), 1) == head_of).astype(F32).astype(BF16)


def triangle(lower):
    rows, cols = iota((ROWS, ROWS), 0), iota((ROWS, ROWS), 1)
    return ((rows >= cols) if lower else (rows <= cols)).astype(F32).astype(BF16)


def sigmoid(v):
    return 1.0 / (1.0 + jnp.exp(-v))


def extended(block, halo):
    return jnp.concatenate([halo, block], axis=0)


def conv_pre(ext, taps):
    out = taps[4:5] + taps[0:1] * ext[5 : 5 + ROWS]
    for k in range(1, CONV):
        out = out + taps[k : k + 1] * ext[5 + k : 5 + k + ROWS]
    return out


def conv_back(d_pre, taps):
    ext = jnp.concatenate([d_pre, jnp.zeros((8, d_pre.shape[1]), F32)], axis=0)
    out = taps[3:4] * d_pre
    for k in range(CONV - 1):
        out = out + taps[k : k + 1] * ext[3 - k : 3 - k + ROWS]
    return out


def tap_grads(d_pre, ext):
    rows = [jnp.sum(d_pre * ext[5 + k : 5 + k + ROWS], axis=0, keepdims=True) for k in range(CONV)]
    rows.append(jnp.sum(d_pre, axis=0, keepdims=True))
    rows.append(jnp.zeros((3, d_pre.shape[1]), F32))
    return jnp.concatenate(rows, axis=0)


def step_parts(raw_ref, hp_ref):
    real = iota((ROWS, 128), 1) < HEADS
    raw = jnp.where(real, raw_ref[...], 0.0) + hp_ref[0:1, :]
    step = jnp.maximum(raw, 0.0) + jnp.log1p(jnp.exp(-jnp.abs(raw)))
    step = jnp.where(real, step, 0.0)
    rate = jnp.where(real[0:1], -jnp.exp(hp_ref[1:2, :]), 0.0)
    return raw, step, rate


def mm_kernel(flag_ref, x_ref, own_ref, other_ref, o_ref, *, nt):
    dot = dot_nt if nt else dot_nn

    @pl.when(flag_ref[0] == 1)
    def _():
        o_ref[...] = dot(x_ref[...], own_ref[...])

    @pl.when(flag_ref[0] == 0)
    def _():
        o_ref[...] = dot(x_ref[...], other_ref[...])


def mm(x, own, other, flag, nt, tile):
    rows, depth = x.shape
    width = own.shape[0] if nt else own.shape[1]
    block = (tile, depth) if nt else (depth, tile)

    def place(j, keep):
        return (j * keep, 0) if nt else (0, j * keep)

    return pl.pallas_call(
        functools.partial(mm_kernel, nt=nt),
        grid_spec=pltpu.PrefetchScalarGridSpec(
            num_scalar_prefetch=1,
            grid=(pl.cdiv(width, tile),),
            in_specs=[
                pl.BlockSpec((rows, depth), lambda j, f: (0, 0)),
                pl.BlockSpec(block, lambda j, f: place(j, f[0])),
                pl.BlockSpec(block, lambda j, f: place(j, 1 - f[0])),
            ],
            out_specs=pl.BlockSpec((rows, tile), lambda j, f: (0, j)),
        ),
        out_shape=jax.ShapeDtypeStruct((rows, width), F32),
        compiler_params=pltpu.CompilerParams(vmem_limit_bytes=48 * MIB),
        cost_estimate=pl.CostEstimate(
            flops=2 * rows * depth * width, bytes_accessed=2 * depth * width, transcendentals=0
        ),
    )(flag, x, own, other)


def front_kernel(
    x_ref, b_ref, c_ref, raw_ref, xh_ref, bh_ref, ch_ref, xw_ref, bw_ref, cw_ref, hp_ref,
    val_ref, state_ref, dec_ref, step_ref, cum_ref, cumt_ref, bo_ref, co_ref, g_ref,
):
    j = pl.program_id(0)

    @pl.when(j == 0)
    def _():
        _, step, rate = step_parts(raw_ref, hp_ref)
        step_ref[...] = step
        cum = exact_left(triangle(True), rate * step)
        cum_ref[...] = cum
        cumt_ref[...] = cum.T
        pre = conv_pre(extended(b_ref[...], bh_ref[...]), bw_ref[...])
        b_low = split2(pre * sigmoid(pre))
        bo_ref[...] = jnp.concatenate(b_low, axis=1)
        pre = conv_pre(extended(c_ref[...], ch_ref[...]), cw_ref[...])
        c_low = split2(pre * sigmoid(pre))
        co_ref[...] = jnp.concatenate(c_low, axis=1)
        seen = iota((ROWS, ROWS), 0) >= iota((ROWS, ROWS), 1)
        g_ref[...] = jnp.where(seen, fine(dot_nt, c_low, b_low), 0.0)

    pre = conv_pre(extended(x_ref[...], xh_ref[...]), xw_ref[...])
    values = pre * sigmoid(pre)
    heads = expander(j)
    step = exact_right(step_ref[...], heads)
    cum = exact_right(cum_ref[...], heads)
    last = cum[ROWS - 1 : ROWS]
    scaled = values * step
    val_ref[...] = values
    state_ref[...] = fine(dot_tn, halves(bo_ref), split2(scaled * jnp.exp(last - cum)))
    dec_ref[...] = jnp.broadcast_to(jnp.exp(last), (8, 128))


def whole(shape):
    return pl.BlockSpec(shape, lambda j: (0, 0))


def lanes(rows, first=0):
    return pl.BlockSpec((rows, 128), lambda j: (0, first + j))


def fixed(rows, at):
    return pl.BlockSpec((rows, 128), lambda j: (0, at))


def sds(rows, cols, dtype):
    return jax.ShapeDtypeStruct((rows, cols), dtype)


def grid_params():
    return pltpu.CompilerParams(vmem_limit_bytes=48 * MIB)


def front(proj, halo, taps, hp):
    return pl.pallas_call(
        front_kernel,
        grid=(PAIRS,),
        in_specs=[
            lanes(ROWS, 24), fixed(ROWS, 48), fixed(ROWS, 49), fixed(ROWS, 50),
            lanes(8), fixed(8, 24), fixed(8, 25),
            lanes(8), fixed(8, 24), fixed(8, 25),
            whole((8, 128)),
        ],
        out_specs=[
            lanes(ROWS), lanes(128), lanes(8),
            whole((ROWS, 128)), whole((ROWS, 128)), whole((128, ROWS)),
            whole((ROWS, 256)), whole((ROWS, 256)), whole((ROWS, ROWS)),
        ],
        out_shape=[
            sds(ROWS, INNER, F32), sds(128, INNER, F32), sds(8, INNER, F32),
            sds(ROWS, 128, F32), sds(ROWS, 128, F32), sds(128, ROWS, F32),
            sds(ROWS, 256, BF16), sds(ROWS, 256, BF16), sds(ROWS, ROWS, F32),
        ],
        compiler_params=grid_params(),
        cost_estimate=pl.CostEstimate(flops=2 * 10**9, bytes_accessed=10 * MIB, transcendentals=10**6),
    )(proj, proj, proj, proj, halo, halo, halo, taps, taps, taps, hp)


def exchange_kernel(
    n, rev, s_ref, d_ref, o_ref, inbox, dbox, parts, decs, total, chain_out, chain_in, outbox,
    send_a, recv_a, send_d, recv_d, send_c, recv_c, send_o, recv_o,
):
    planes = n // PLANE
    section = lax.axis_index("section")
    q = lax.axis_index("seq")
    u = n - 1 - q if rev else q
    spot, level = lax.rem(u, PLANE), u // PLANE

    def device(at):
        return (section, n - 1 - at if rev else at)

    peers = [lax.rem(spot + k, PLANE) for k in range(1, PLANE)]
    barrier = pltpu.get_barrier_semaphore()
    for peer in peers:
        pl.semaphore_signal(barrier, inc=1, device_id=device(level * PLANE + peer), device_id_type=MESH)

    @pl.when(level > 0)
    def _():
        pl.semaphore_signal(barrier, inc=1, device_id=device(u - PLANE), device_id_type=MESH)

    pl.semaphore_wait(barrier, PLANE - 1 + (level < planes - 1).astype(jnp.int32))

    def group(at):
        return pl.ds(pl.multiple_of(at * LANES, LANES), LANES)

    first = []
    for k, peer in enumerate(peers):
        to = device(level * PLANE + peer)
        first.append(
            pltpu.make_async_remote_copy(
                src_ref=d_ref.at[:, group(peer)], dst_ref=dbox.at[spot],
                send_sem=send_d.at[k], recv_sem=recv_d.at[k], device_id=to, device_id_type=MESH,
            )
        )
        first.append(
            pltpu.make_async_remote_copy(
                src_ref=s_ref.at[:, group(peer)], dst_ref=inbox.at[spot],
                send_sem=send_a.at[k], recv_sem=recv_a.at[k], device_id=to, device_id_type=MESH,
            )
        )
    for copy in first:
        copy.start()
    inbox[spot] = s_ref[:, group(spot)]
    dbox[spot] = d_ref[:, group(spot)]
    for copy in first:
        copy.wait()

    cuts = LANES // 256
    for b in range(cuts):
        at = slice(b * 256, b * 256 + 256)
        state = inbox[0, :, at].astype(F32)
        decay = dbox[0, 0:1, at]
        for p in range(1, PLANE):
            parts[p, :, at] = state
            decs[p, 0:1, at] = decay
            d = dbox[p, 0:1, at]
            state = d * state + inbox[p, :, at].astype(F32)
            decay = decay * d
        total[:, at] = state
        decs[0, 0:1, at] = decay

    def chain(b):
        return pltpu.make_async_remote_copy(
            src_ref=chain_out.at[b], dst_ref=chain_in.at[b],
            send_sem=send_c.at[b], recv_sem=recv_c.at[b],
            device_id=device(lax.rem(u + PLANE, n)), device_id_type=MESH,
        )

    last = []
    for b in range(cuts):
        at = slice(b * 256, b * 256 + 256)

        @pl.when(level > 0)
        def _():
            chain(b).wait_recv()

        @pl.when(level == 0)
        def _():
            chain_in[b] = jnp.zeros((128, 256), chain_in.dtype)

        enter = chain_in[b].astype(F32)

        @pl.when(level < planes - 1)
        def _():
            chain_out[b] = (decs[0, 0:1, at] * enter + total[:, at]).astype(chain_out.dtype)
            chain(b).start()

        outbox[0, :, at] = enter.astype(outbox.dtype)
        for p in range(1, PLANE):
            outbox[p, :, at] = (decs[p, 0:1, at] * enter + parts[p, :, at]).astype(outbox.dtype)
        mine = pl.ds(pl.multiple_of(spot * LANES + b * 256, 256), 256)
        o_ref[:, mine] = outbox[spot, :, at]
        for k, peer in enumerate(peers):
            copy = pltpu.make_async_remote_copy(
                src_ref=outbox.at[peer, :, pl.ds(b * 256, 256)], dst_ref=o_ref.at[:, mine],
                send_sem=send_o.at[b * 3 + k], recv_sem=recv_o.at[b * 3 + k],
                device_id=device(level * PLANE + peer), device_id_type=MESH,
            )
            copy.start()
            last.append(copy)
    for copy in last:
        copy.wait()

    @pl.when(level < planes - 1)
    def _():
        for b in range(cuts):
            chain(b).wait_send()


def exchange(state, decay, n, rev):
    vmem = pl.BlockSpec(memory_space=pltpu.VMEM)
    dma = pltpu.SemaphoreType.DMA
    cuts = LANES // 256
    return pl.pallas_call(
        functools.partial(exchange_kernel, n, rev),
        out_shape=sds(128, INNER, state.dtype),
        in_specs=[vmem, vmem],
        out_specs=vmem,
        scratch_shapes=[
            pltpu.VMEM((PLANE, 128, LANES), state.dtype),
            pltpu.VMEM((PLANE, 8, LANES), F32),
            pltpu.VMEM((PLANE, 128, LANES), F32),
            pltpu.VMEM((PLANE, 8, LANES), F32),
            pltpu.VMEM((128, LANES), F32),
            pltpu.VMEM((cuts, 128, 256), state.dtype),
            pltpu.VMEM((cuts, 128, 256), state.dtype),
            pltpu.VMEM((PLANE, 128, LANES), state.dtype),
            dma((3,)), dma((3,)), dma((3,)), dma((3,)),
            dma((cuts,)), dma((cuts,)), dma((3 * cuts,)), dma((3 * cuts,)),
        ],
        compiler_params=pltpu.CompilerParams(
            collective_id=2 if rev else 1, has_side_effects=True, vmem_limit_bytes=32 * MIB
        ),
    )(state, decay)


def decay_block(cum, row):
    return jnp.exp(jnp.minimum(cum - row, 0.0))


def mix_kernel(
    g_ref, step_ref, cum_ref, cumt_ref, val_ref, gate_ref, c_ref, car_ref, lp_ref, gain_ref,
    y_ref, low_ref, gated_ref, sum_ref,
):
    j = pl.program_id(0)
    heads = expander(j)
    cum = exact_right(cum_ref[...], heads)
    values = val_ref[...]
    scaled = split2(values * exact_right(step_ref[...], heads))
    early = iota((ROWS, 128), 1) < HEADDIM
    y = jnp.exp(cum) * fine(dot_nn, halves(c_ref), split2(car_ref[...])) + lp_ref[0:1, :] * values
    for i in range(2):
        row = cumt_ref[pl.ds(2 * j + i, 1), :]
        decay = decay_block(cum[:, i * HEADDIM : i * HEADDIM + 1], row)
        half = early if i == 0 else ~early
        part = [jnp.where(half, v, jnp.zeros((), BF16)) for v in scaled]
        y = y + fine(dot_nn, split2(g_ref[...] * decay), part)
    y_ref[...] = y
    gate = gate_ref[...]
    gated = y * (gate * sigmoid(gate))
    gated_ref[j] = gated

    @pl.when(j == 0)
    def _():
        sum_ref[...] = jnp.zeros_like(sum_ref)

    sum_ref[...] += gated * gated

    @pl.when(j == PAIRS - 1)
    def _():
        mean = jnp.sum(sum_ref[...], axis=1, keepdims=True) * (1.0 / INNER)
        scale = lax.rsqrt(mean + EPS)
        for k in range(PAIRS):
            at = slice(k * 128, k * 128 + 128)
            low_ref[:, at] = (gated_ref[k] * scale * gain_ref[1:2, at]).astype(BF16)


def mix(g, step, cum, cumt, values, proj, c, carried, lp):
    return pl.pallas_call(
        mix_kernel,
        grid=(PAIRS,),
        in_specs=[
            whole((ROWS, ROWS)), whole((ROWS, 128)), whole((ROWS, 128)), whole((128, ROWS)),
            lanes(ROWS), lanes(ROWS), whole((ROWS, 256)), lanes(128), lanes(8),
            whole((8, INNER)),
        ],
        out_specs=[lanes(ROWS), whole((ROWS, INNER))],
        out_shape=[sds(ROWS, INNER, F32), sds(ROWS, INNER, BF16)],
        scratch_shapes=[pltpu.VMEM((PAIRS, ROWS, 128), F32), pltpu.VMEM((ROWS, 128), F32)],
        compiler_params=grid_params(),
        cost_estimate=pl.CostEstimate(flops=3 * 10**9, bytes_accessed=14 * MIB, transcendentals=4 * 10**6),
    )(g, step, cum, cumt, values, proj, c, carried, lp, lp)


def gate_back_kernel(
    dg_ref, y_ref, gate_ref, cum_ref, c_ref, lp_ref, dy_ref, dgate_ref, gain_ref, dcar_ref
):
    def piece(k):
        at = pl.ds(pl.multiple_of(k * 128, 128), 128)
        gate = gate_ref[:, at]
        s = sigmoid(gate)
        y = y_ref[:, at]
        return at, gate, s, y, y * (gate * s)

    def first(k, sums):
        at, _, _, _, gated = piece(k)
        w = dg_ref[:, at] * lp_ref[1:2, at]
        return sums[0] + gated * gated, sums[1] + w * gated

    zero = jnp.zeros((ROWS, 128), F32)
    squares, cross = lax.fori_loop(0, PAIRS, first, (zero, zero))
    r = lax.rsqrt(jnp.sum(squares, axis=1, keepdims=True) * (1.0 / INNER) + EPS)
    m = jnp.sum(cross, axis=1, keepdims=True) * (1.0 / INNER) * r * r

    def second(k, carry):
        at, gate, s, y, gated = piece(k)
        dg = dg_ref[:, at]
        gain_ref[:, at] = jnp.broadcast_to(jnp.sum(dg * gated * r, axis=0, keepdims=True), (8, 128))
        d_gated = r * (dg * lp_ref[1:2, at] - gated * m)
        dy = d_gated * (gate * s)
        dy_ref[:, at] = dy
        dgate_ref[:, at] = (d_gated * y * (s * (1.0 + gate * (1.0 - s)))).astype(BF16)
        cum = exact_right(cum_ref[...], expander(k))
        dcar_ref[:, at] = fine(dot_tn, halves(c_ref), split2(dy * jnp.exp(cum))).astype(BF16)
        return carry

    lax.fori_loop(0, PAIRS, second, 0)


def gate_back(dg, y, proj, cum, c, lp):
    return pl.pallas_call(
        gate_back_kernel,
        grid=(1,),
        in_specs=[
            whole((ROWS, INNER)), whole((ROWS, INNER)), whole((ROWS, INNER)),
            whole((ROWS, 128)), whole((ROWS, 256)), whole((8, INNER)),
        ],
        out_specs=[whole((ROWS, INNER)), whole((ROWS, INNER)), whole((8, INNER)), whole((128, INNER))],
        out_shape=[sds(ROWS, INNER, F32), sds(ROWS, INNER, BF16), sds(8, INNER, F32), sds(128, INNER, BF16)],
        compiler_params=grid_params(),
        cost_estimate=pl.CostEstimate(flops=10**9, bytes_accessed=16 * MIB, transcendentals=2 * 10**6),
    )(dg, y, proj, cum, c, lp)


def core_back_kernel(
    x_ref, b_ref, c_ref, raw_ref, xh_ref, bh_ref, ch_ref, xw_ref, bw_ref, cw_ref, hp_ref,
    step_ref, cum_ref, cumt_ref, g_ref, bo_ref, co_ref, dy_ref, car_ref, late_ref, lp_ref,
    dx_ref, dbc_ref, tail_ref, tailbc_ref, head_ref, headbc_ref, taps_ref, tapsbc_ref, draw_ref, hg_ref,
    dg_acc, dc_acc, db_acc, dcum_acc, dstep_acc, rows_acc,
):
    j = pl.program_id(0)

    @pl.when(j == 0)
    def _():
        for acc in (dg_acc, dc_acc, db_acc, dcum_acc, dstep_acc, rows_acc):
            acc[...] = jnp.zeros_like(acc)

    ext = extended(x_ref[...], xh_ref[...])
    pre = conv_pre(ext, xw_ref[...])
    sig = sigmoid(pre)
    values = pre * sig
    heads, collect = expander(j), collector(j)
    step = exact_right(step_ref[...], heads)
    cum = exact_right(cum_ref[...], heads)
    last = cum[ROWS - 1 : ROWS]
    to_end, from_start = jnp.exp(last - cum), jnp.exp(cum)
    scaled = values * step
    scaled_parts = split2(scaled)
    scaled_low = scaled_parts[0]
    dy = dy_ref[...]
    dy_parts = split2(dy)
    dy_low = dy_parts[0]
    early = iota((ROWS, 128), 1) < HEADDIM
    y_in = jnp.zeros((ROWS, 128), F32)
    d_scaled = jnp.zeros((ROWS, 128), F32)
    for i in range(2):
        half = early if i == 0 else ~early
        row = cumt_ref[pl.ds(2 * j + i, 1), :]
        decay = decay_block(cum[:, i * HEADDIM : i * HEADDIM + 1], row)
        mixing = (g_ref[...] * decay).astype(BF16)
        dy_half = [jnp.where(half, part, jnp.zeros((), BF16)) for part in dy_parts]
        y_in = y_in + dot_nn(mixing, jnp.where(half, scaled_low, jnp.zeros((), BF16)))
        d_scaled = d_scaled + dot_tn(mixing, dy_half[0])
        dg_acc[...] += fine(dot_nt, dy_half, scaled_parts) * decay
    car, late = car_ref[...], late_ref[...]
    car_parts = split2(car)
    y_across = from_start * fine(dot_nn, halves(co_ref), car_parts)
    d_ended = dot_nn(bo_ref[:, 0:128], late)
    ended = scaled * to_end
    dc_acc[...] += fine(dot_nt, split2(dy * from_start), car_parts)
    ended_parts = split2(ended)
    db_acc[...] += dot_nt(ended_parts[0], late) + dot_nt(ended_parts[1], late)
    d_total = d_scaled + to_end * d_ended
    through_end = ended * d_ended
    d_cum = dy_low.astype(F32) * y_in + dy * y_across - scaled_low.astype(F32) * d_scaled - through_end
    dcum_acc[...] += exact_right(d_cum, collect)
    dstep_acc[...] += exact_right(d_total * values, collect)
    at_last = jnp.exp(last) * jnp.sum(late.astype(F32) * car, axis=0, keepdims=True)
    at_last = at_last + jnp.sum(through_end, axis=0, keepdims=True)
    skip = jnp.sum(dy * values, axis=0, keepdims=True)
    rows_acc[...] += exact_right(jnp.concatenate([at_last, skip, jnp.zeros((6, 128), F32)], axis=0), collect)
    d_values = lp_ref[0:1, :] * dy + step * d_total
    d_pre = d_values * (sig * (1.0 + pre * (1.0 - sig)))
    taps_ref[...] = tap_grads(d_pre, ext)
    head_ref[...] = d_pre[0:8]
    d_conv = conv_back(d_pre, xw_ref[...])
    dx_ref[...] = d_conv.astype(BF16)
    tail_ref[...] = d_conv[ROWS - 8 : ROWS]

    @pl.when(j == PAIRS - 1)
    def _():
        seen = iota((ROWS, ROWS), 0) >= iota((ROWS, ROWS), 1)
        d_g = split2(jnp.where(seen, dg_acc[...], 0.0))
        d_c = dc_acc[...] + fine(dot_nn, d_g, halves(bo_ref))
        d_b = db_acc[...] + fine(dot_tn, d_g, halves(co_ref))
        for k, (block, halo, taps, grad) in enumerate(
            ((b_ref, bh_ref, bw_ref, d_b), (c_ref, ch_ref, cw_ref, d_c))
        ):
            at = slice(k * 128, k * 128 + 128)
            ext_k = extended(block[...], halo[...])
            pre_k = conv_pre(ext_k, taps[...])
            sig_k = sigmoid(pre_k)
            d_pre_k = grad * (sig_k * (1.0 + pre_k * (1.0 - sig_k)))
            tapsbc_ref[:, at] = tap_grads(d_pre_k, ext_k)
            headbc_ref[:, at] = d_pre_k[0:8]
            d_conv_k = conv_back(d_pre_k, taps[...])
            dbc_ref[:, at] = d_conv_k.astype(BF16)
            tailbc_ref[:, at] = d_conv_k[ROWS - 8 : ROWS]
        raw, step_all, rate = step_parts(raw_ref, hp_ref)
        end = iota((ROWS, 128), 0) == ROWS - 1
        d_cum_all = dcum_acc[...] + jnp.where(end, rows_acc[0:1, :], 0.0)
        d_log = exact_left(triangle(False), d_cum_all)
        d_step = dstep_acc[...] + rate * d_log
        d_raw = jnp.where(iota((ROWS, 128), 1) < HEADS, d_step * sigmoid(raw), 0.0)
        draw_ref[...] = d_raw.astype(BF16)
        hg_ref[...] = jnp.concatenate(
            [
                jnp.sum(d_raw, axis=0, keepdims=True),
                jnp.sum(d_log * rate * step_all, axis=0, keepdims=True),
                rows_acc[1:2, :],
                jnp.zeros((5, 128), F32),
            ],
            axis=0,
        )


def core_back(proj, halo, taps, hp, step, cum, cumt, g, b, c, dy, carried, late, lp):
    return pl.pallas_call(
        core_back_kernel,
        grid=(PAIRS,),
        in_specs=[
            lanes(ROWS, 24), fixed(ROWS, 48), fixed(ROWS, 49), fixed(ROWS, 50),
            lanes(8), fixed(8, 24), fixed(8, 25),
            lanes(8), fixed(8, 24), fixed(8, 25),
            whole((8, 128)),
            whole((ROWS, 128)), whole((ROWS, 128)), whole((128, ROWS)), whole((ROWS, ROWS)),
            whole((ROWS, 256)), whole((ROWS, 256)),
            lanes(ROWS), lanes(128), lanes(128), lanes(8),
        ],
        out_specs=[
            lanes(ROWS), whole((ROWS, 256)), lanes(8), whole((8, 256)), lanes(8), whole((8, 256)),
            lanes(8), whole((8, 256)), whole((ROWS, 128)), whole((8, 128)),
        ],
        out_shape=[
            sds(ROWS, INNER, BF16), sds(ROWS, 256, BF16), sds(8, INNER, F32), sds(8, 256, F32),
            sds(8, INNER, F32), sds(8, 256, F32), sds(8, INNER, F32), sds(8, 256, F32),
            sds(ROWS, 128, BF16), sds(8, 128, F32),
        ],
        scratch_shapes=[
            pltpu.VMEM((ROWS, ROWS), F32),
            pltpu.VMEM((ROWS, 128), F32), pltpu.VMEM((ROWS, 128), F32), pltpu.VMEM((ROWS, 128), F32),
            pltpu.VMEM((ROWS, 128), F32), pltpu.VMEM((8, 128), F32),
        ],
        compiler_params=grid_params(),
        cost_estimate=pl.CostEstimate(flops=8 * 10**9, bytes_accessed=14 * MIB, transcendentals=5 * 10**6),
    )(
        proj, proj, proj, proj, halo, halo, halo, taps, taps, taps, hp,
        step, cum, cumt, g, b, c, dy, carried, late, lp,
    )


def swap(value):
    return lax.ppermute(value, "section", [(0, 1), (1, 0)])


def shifted(value, distance, n):
    return lax.ppermute(value, "seq", [(i, i + distance) for i in range(n) if 0 <= i + distance < n])


def plane_route(k, n):
    return [(i, i - i % PLANE + (i + k) % PLANE) for i in range(n)]


def rms(value):
    return lax.rsqrt(jnp.mean(value * value, axis=-1, keepdims=True) + EPS)


def split_small(flat):
    sizes = [D, CONVD * CONV, CONVD, HEADS, HEADS, HEADS, INNER]
    parts, at = [], 0
    for size in sizes:
        parts.append(flat[at : at + size])
        at += size
    return parts


def unpack_params(flat):
    norm_g, conv_w, conv_b, dt_b, a_lg, skip_w, gate_g = split_small(flat)
    taps = jnp.concatenate(
        [conv_w.reshape(CONVD, CONV).T, conv_b[None], jnp.zeros((3, CONVD), F32)], axis=0
    )
    hp = jnp.zeros((8, 128), F32).at[0, :HEADS].set(dt_b).at[1, :HEADS].set(a_lg)
    lp = jnp.concatenate(
        [jnp.repeat(skip_w, HEADDIM)[None], gate_g[None], jnp.zeros((6, INNER), F32)], axis=0
    )
    return norm_g, taps, hp, lp


def forward_layer(h, weights, params, n):
    own_in, other_in, own_out, other_out, flag = weights
    norm_g, taps, hp, lp = params
    normed = (h * rms(h) * norm_g).astype(BF16)
    proj = mm(normed, own_in, other_in, flag, False, 512)
    halo = shifted(proj[ROWS - 8 :, INNER : INNER + CONVD], 1, n)
    values, state, decay, step, cum, cumt, b, c, g = front(proj, halo, taps, hp)
    carried = exchange(state, decay, n, False)
    y, gated_low = mix(g, step, cum, cumt, values, proj, c, carried, lp)
    out = h + mm(gated_low, own_out, other_out, flag, False, 256)
    return out, (h, normed, proj, halo, decay, step, cum, cumt, b, c, g, carried, y, gated_low)


def backward_layer(stored, d_out, weights, params, n):
    own_in, other_in, own_out, other_out, flag = weights
    norm_g, taps, hp, lp = params
    h, normed, proj, halo, decay, step, cum, cumt, b, c, g, carried, y, gated_low = stored
    d_low = d_out.astype(BF16)
    d_gated_low = mm(d_low, own_out, other_out, flag, True, 512)
    dy, d_gate, gate_gain, d_carried = gate_back(d_gated_low, y, proj, cum, c, lp)
    late = exchange(d_carried, decay, n, True)
    dx, dbc, tail, tailbc, head, headbc, gtaps, gtapsbc, d_raw, heads = core_back(
        proj, halo, taps, hp, step, cum, cumt, g, b, c, dy, carried, late, lp
    )
    after = shifted(jnp.concatenate([head, headbc], axis=1), -1, n)
    fix = jnp.concatenate([tail, tailbc], axis=1)
    zero = jnp.zeros((8, CONVD), F32)
    for k in range(CONV - 1):
        fix = fix + zero.at[5 + k :].set(taps[k][None] * after[: 3 - k])
    low = jnp.concatenate([d_gate, dx, dbc, d_raw[:, :HEADS]], axis=1)
    d_proj = low.at[ROWS - 8 :, INNER : INNER + CONVD].set(fix.astype(BF16))
    d_normed = mm(d_proj, own_in, other_in, flag, True, 256)
    r = rms(h)
    v = d_normed * norm_g
    d_h = d_out + r * (v - h * (r * r * jnp.mean(v * h, axis=-1, keepdims=True)))
    norm_gain = jnp.sum(d_normed * h * r, axis=0)
    taps_all = jnp.concatenate([gtaps, gtapsbc], axis=1)
    small = jnp.concatenate(
        [
            norm_gain, taps_all[:CONV].T.reshape(-1), taps_all[CONV],
            heads[0, :HEADS], heads[1, :HEADS], heads[2, :HEADS], gate_gain[0],
        ]
    )
    return d_h, (normed, d_proj, gated_low, d_low), small


def pieces_of(value, count, n):
    spot = lax.axis_index("seq") % PLANE
    width = value.shape[1] // count
    got = [lax.dynamic_slice_in_dim(value, spot * width, width, 1)]
    for k in range(1, PLANE):
        part = lax.dynamic_slice_in_dim(value, (spot + k) % PLANE * width, width, 1)
        got.append(lax.ppermute(part, "seq", plane_route(k, n)))
    return jnp.concatenate(got, axis=0)


def copies_of(value, n):
    got = [value] + [lax.ppermute(value, "seq", plane_route(k, n)) for k in range(1, PLANE)]
    return jnp.concatenate(got, axis=0)


def matrix_grads(factors, n):
    normed, d_proj, gated_low, d_low = factors
    planes = n // PLANE
    columns = [[p + PLANE * z for z in range(planes)] for p in range(PLANE)]
    in_plane = [[PLANE * z + p for p in range(PLANE)] for z in range(planes)]

    def sum_rows(partial):
        return lax.psum_scatter(
            partial.astype(BF16), "seq", scatter_dimension=0, axis_index_groups=columns, tiled=True
        )

    by_owner = gated_low.reshape(ROWS, planes, PLANE, INNER // n).transpose(0, 2, 1, 3).reshape(ROWS, INNER)
    g_out = sum_rows(dot_tn(pieces_of(by_owner, PLANE, n), copies_of(d_low, n)))
    wide = jnp.concatenate([d_proj, jnp.zeros((ROWS, PLANE * QUARTER - PROJ), BF16)], axis=1)
    g_in = sum_rows(dot_tn(copies_of(normed, n), pieces_of(wide, PLANE, n)))
    g_in = lax.all_to_all(g_in, "seq", 0, 1, axis_index_groups=in_plane, tiled=True)
    return g_in[:, :PROJ].astype(F32), g_out.astype(F32)


def per_device(
    inputs, cotangent, norm_gain, in_weight, conv_weight, conv_bias, dt_bias, a_log, d_skip,
    gate_norm_gain, out_weight,
):
    n = lax.axis_size("seq")
    core = lax.axis_index("section")
    place = lax.axis_index("seq")
    first = core == 0
    own_in, own_out = in_weight[0], out_weight[0]
    other_in, other_out = swap(own_in), swap(own_out)
    own_small = jnp.concatenate(
        [
            norm_gain[0], conv_weight[0].reshape(-1), conv_bias[0], dt_bias[0], a_log[0], d_skip[0],
            gate_norm_gain[0],
        ]
    )
    other_small = swap(own_small)
    flags = [(core == layer).astype(jnp.int32)[None] for layer in range(2)]
    weights = [(own_in, other_in, own_out, other_out, flag) for flag in flags]
    params = [
        unpack_params(jnp.where(first, own_small, other_small)),
        unpack_params(jnp.where(first, other_small, own_small)),
    ]

    def mine(pair):
        return lax.dynamic_index_in_dim(pair, core, 0, keepdims=False)

    def settle(early, late):
        return jnp.where(first, early, late), swap(jnp.where(first, late, early))

    def both(early, late):
        own, other = settle(early, late)
        return jnp.stack([jnp.where(first, own, other), jnp.where(first, other, own)])[None]

    out_0, kept_0 = forward_layer(mine(inputs).astype(F32), weights[0], params[0], n)
    act_0 = out_0.astype(BF16)
    out_1, kept_1 = forward_layer(act_0.astype(F32), weights[1], params[1], n)
    acts = both(act_0, out_1.astype(BF16))

    d_1, factors_1, small_1 = backward_layer(kept_1, mine(cotangent).astype(F32), weights[1], params[1], n)
    in_1, outw_1 = matrix_grads(factors_1, n)
    d_0, factors_0, small_0 = backward_layer(kept_0, d_1.astype(BF16).astype(F32), weights[0], params[0], n)
    in_0, outw_0 = matrix_grads(factors_0, n)
    input_grads = both(d_0, d_1)

    def joined(early, late):
        own, other = settle(early, late)
        return own + other

    g_in, g_out, small = joined(in_0, in_1), joined(outw_0, outw_1), joined(small_0, small_1)
    reach = 1
    while reach < n:
        small = small + lax.ppermute(small, "seq", [(i, i ^ reach) for i in range(n)])
        reach *= 2
    norm_g, conv_w, conv_b, dt_b, a_lg, skip_w, gate_g = split_small(small)

    def share(value):
        rows = value.shape[0] // n
        return lax.dynamic_slice_in_dim(value, place * rows, rows, 0)[None]

    return (
        acts, input_grads, share(norm_g), g_in[None], share(conv_w.reshape(CONVD, CONV)), share(conv_b),
        dt_b[None], a_lg[None], skip_w[None], share(gate_g), g_out[None],
    )


def solution(mesh):
    in_specs = (
        P(None, "seq", None), P(None, "seq", None), P("section", None), P("section", None, None),
        P("section", None, None), P("section", None), P("section", None), P("section", None),
        P("section", None), P("section", None), P("section", None, None),
    )
    out_specs = (
        P("section", None, "seq", None), P("section", None, "seq", None), P("section", "seq"),
        P("section", "seq", None), P("section", "seq", None), P("section", "seq"), P("section", None),
        P("section", None), P("section", None), P("section", "seq"), P("section", "seq", None),
    )
    return jax.shard_map(per_device, mesh=mesh, in_specs=in_specs, out_specs=out_specs, check_vma=False)
```

```python
import functools

import jax
import jax.numpy as jnp
from jax import lax
from jax.experimental import pallas as pl
from jax.experimental.pallas import tpu as pltpu
from jax.sharding import PartitionSpec as P

D = 1536
INNER = 3072
STATE = 128
HEADS = 48
HEADDIM = 64
CONV = 4
CONVD = 3328
PROJ = 6448
ROWS = 256
WIDE = 256
STEPS = INNER // WIDE
HALF = ROWS // 2
PLANE = 4
LANES = INNER // PLANE
REST = 3584
EPS = 1e-05
MIB = 2**20
MESH = pl.DeviceIdType.MESH
F32 = jnp.float32
BF16 = jnp.bfloat16


def dot_nn(a, b):
    return lax.dot_general(a, b, (((1,), (0,)), ((), ())), preferred_element_type=F32)


def dot_tn(a, b):
    return lax.dot_general(a, b, (((0,), (0,)), ((), ())), preferred_element_type=F32)


def dot_nt(a, b):
    return lax.dot_general(a, b, (((1,), (1,)), ((), ())), preferred_element_type=F32)


def split3(v):
    high = v.astype(BF16)
    rest = v - high.astype(F32)
    mid = rest.astype(BF16)
    return high, mid, (rest - mid.astype(F32)).astype(BF16)


def split2(v):
    high = v.astype(BF16)
    return high, (v - high.astype(F32)).astype(BF16)


def fine(dot, a, b):
    return dot(a[0], b[0]) + (dot(a[0], b[1]) + dot(a[1], b[0]))


def halves(ref):
    return ref[:, 0:128], ref[:, 128:256]


def parts3(v):
    return jnp.concatenate(split3(v), axis=1)


def exact_left(ones, v):
    a, b, c = split3(v)
    return dot_nn(ones, a) + (dot_nn(ones, b) + dot_nn(ones, c))


def iota(shape, dim):
    return lax.broadcasted_iota(jnp.int32, shape, dim)


def expander(step):
    head_of = (WIDE // HEADDIM) * step + lax.shift_right_logical(iota((128, WIDE), 1), 6)
    ones = (iota((128, WIDE), 0) == head_of).astype(F32).astype(BF16)
    return jnp.concatenate([ones, ones, ones], axis=0)


def collector(step):
    head_of = (WIDE // HEADDIM) * step + lax.shift_right_logical(iota((WIDE, 128), 0), 6)
    return (iota((WIDE, 128), 1) == head_of).astype(F32).astype(BF16)


def collect(v, ones):
    a, b, c = split3(v)
    return dot_nn(a, ones) + (dot_nn(b, ones) + dot_nn(c, ones))


def triangle(lower):
    rows, cols = iota((ROWS, ROWS), 0), iota((ROWS, ROWS), 1)
    return ((rows >= cols) if lower else (rows <= cols)).astype(F32).astype(BF16)


def sigmoid(v):
    return 0.5 * jnp.tanh(0.5 * v) + 0.5


def extended(block, halo):
    return jnp.concatenate([halo, block], axis=0)


def conv_pre(ext, taps):
    out = taps[4:5] + taps[0:1] * ext[5 : 5 + ROWS]
    for k in range(1, CONV):
        out = out + taps[k : k + 1] * ext[5 + k : 5 + k + ROWS]
    return out


def conv_back(d_pre, taps):
    ext = jnp.concatenate([d_pre, jnp.zeros((8, d_pre.shape[1]), F32)], axis=0)
    out = taps[3:4] * d_pre
    for k in range(CONV - 1):
        out = out + taps[k : k + 1] * ext[3 - k : 3 - k + ROWS]
    return out


def tap_grads(d_pre, ext):
    rows = [jnp.sum(d_pre * ext[5 + k : 5 + k + ROWS], axis=0, keepdims=True) for k in range(CONV)]
    rows.append(jnp.sum(d_pre, axis=0, keepdims=True))
    rows.append(jnp.zeros((3, d_pre.shape[1]), F32))
    return jnp.concatenate(rows, axis=0)


def step_parts(raw_ref, hp_ref):
    real = iota((ROWS, 128), 1) < HEADS
    raw = jnp.where(real, raw_ref[...], 0.0) + hp_ref[0:1, :]
    step = jnp.maximum(raw, 0.0) + jnp.log1p(jnp.exp(-jnp.abs(raw)))
    step = jnp.where(real, step, 0.0)
    rate = jnp.where(real[0:1], -jnp.exp(hp_ref[1:2, :]), 0.0)
    return raw, step, rate


def mm_kernel(flag_ref, x_ref, own_ref, other_ref, o_ref, *, nt):
    dot = dot_nt if nt else dot_nn

    @pl.when(flag_ref[0] == 1)
    def _():
        o_ref[...] = dot(x_ref[...], own_ref[...])

    @pl.when(flag_ref[0] == 0)
    def _():
        o_ref[...] = dot(x_ref[...], other_ref[...])


def mm(x, own, other, flag, nt, tile):
    rows, depth = x.shape
    width = own.shape[0] if nt else own.shape[1]
    block = (tile, depth) if nt else (depth, tile)

    def place(j, keep):
        return (j * keep, 0) if nt else (0, j * keep)

    return pl.pallas_call(
        functools.partial(mm_kernel, nt=nt),
        grid_spec=pltpu.PrefetchScalarGridSpec(
            num_scalar_prefetch=1,
            grid=(pl.cdiv(width, tile),),
            in_specs=[
                pl.BlockSpec((rows, depth), lambda j, f: (0, 0)),
                pl.BlockSpec(block, lambda j, f: place(j, f[0])),
                pl.BlockSpec(block, lambda j, f: place(j, 1 - f[0])),
            ],
            out_specs=pl.BlockSpec((rows, tile), lambda j, f: (0, j)),
        ),
        out_shape=jax.ShapeDtypeStruct((rows, width), F32),
        compiler_params=pltpu.CompilerParams(vmem_limit_bytes=48 * MIB),
        cost_estimate=pl.CostEstimate(
            flops=2 * rows * depth * width, bytes_accessed=2 * depth * width, transcendentals=0
        ),
    )(flag, x, own, other)


def front_kernel(
    x_ref, bc_ref, raw_ref, xh_ref, bch_ref, xw_ref, bcw_ref, hp_ref,
    val_ref, state_ref, dec_ref, step_ref, cum_ref, cumt_ref, b_ref, c_ref, ct_ref, g_ref, gt_ref, bt_ref,
):
    j = pl.program_id(0)

    @pl.when(j == 0)
    def _():
        _, step, rate = step_parts(raw_ref, hp_ref)
        step_ref[...] = parts3(step)
        cum = exact_left(triangle(True), rate * step)
        cum_ref[...] = parts3(cum)
        cumt_ref[...] = cum.T
        pre = conv_pre(extended(bc_ref[...], bch_ref[...]), bcw_ref[...])
        both = pre * sigmoid(pre)
        b, c = both[:, 0:128], both[:, 128:256]
        b_low, c_low = split2(b), split2(c)
        b_ref[...] = jnp.concatenate(b_low, axis=1)
        c_ref[...] = jnp.concatenate([c_low[0], c_low[1], c_low[0]], axis=1)
        ct_ref[...] = c.T.astype(BF16)
        bt_ref[...] = jnp.concatenate(split2(b.T), axis=0)
        seen = iota((ROWS, ROWS), 0) >= iota((ROWS, ROWS), 1)
        g = jnp.where(seen, fine(dot_nt, c_low, b_low), 0.0)
        g_ref[...] = g
        gt_ref[...] = g.T

    pre = conv_pre(extended(x_ref[...], xh_ref[...]), xw_ref[...])
    values = pre * sigmoid(pre)
    val_ref[...] = values
    heads = expander(j)
    cum = dot_nn(cum_ref[...], heads)
    last = cum[ROWS - 1 : ROWS]
    high, rest = split2(values * dot_nn(step_ref[...], heads) * jnp.exp(last - cum))
    twice = dot_nn(bt_ref[...], high)
    state_ref[...] = twice[0:128] + twice[128:256] + dot_nn(bt_ref[0:128, :], rest)
    dec_ref[...] = jnp.broadcast_to(jnp.exp(last), (8, WIDE))


def whole(shape):
    return pl.BlockSpec(shape, lambda j: (0, 0))


def lanes(rows, first=0):
    return pl.BlockSpec((rows, WIDE), lambda j: (0, first + j))


def fixed(rows, at, width=WIDE):
    return pl.BlockSpec((rows, width), lambda j: (0, at))


def sds(rows, cols, dtype):
    return jax.ShapeDtypeStruct((rows, cols), dtype)


def grid_params():
    return pltpu.CompilerParams(vmem_limit_bytes=48 * MIB)


def front(proj, halo, taps, hp):
    square = (ROWS, ROWS)
    return pl.pallas_call(
        front_kernel,
        grid=(STEPS,),
        in_specs=[
            lanes(ROWS, STEPS), fixed(ROWS, 2 * STEPS), fixed(ROWS, 50, 128),
            lanes(8), fixed(8, STEPS), lanes(8), fixed(8, STEPS), whole((8, 128)),
        ],
        out_specs=[
            lanes(ROWS), lanes(128), lanes(8),
            whole((ROWS, 384)), whole((ROWS, 384)), whole((128, ROWS)),
            whole((ROWS, 256)), whole((ROWS, 384)), whole((128, ROWS)), whole(square), whole(square),
        ],
        out_shape=[
            sds(ROWS, INNER, F32), sds(128, INNER, F32), sds(8, INNER, F32),
            sds(ROWS, 384, BF16), sds(ROWS, 384, BF16), sds(128, ROWS, F32),
            sds(ROWS, 256, BF16), sds(ROWS, 384, BF16), sds(128, ROWS, BF16), sds(*square, F32), sds(*square, F32),
        ],
        scratch_shapes=[pltpu.VMEM((256, ROWS), BF16)],
        compiler_params=grid_params(),
        cost_estimate=pl.CostEstimate(flops=10**9, bytes_accessed=10 * MIB, transcendentals=10**6),
    )(proj, proj, proj, halo, halo, taps, taps, hp)


def exchange_kernel(
    n, rev, s_ref, d_ref, o_ref, inbox, dbox, parts, decs, total, chain_out, chain_in, outbox,
    send_a, recv_a, send_d, recv_d, send_c, recv_c, send_o, recv_o,
):
    planes = n // PLANE
    section = lax.axis_index("section")
    q = lax.axis_index("seq")
    u = n - 1 - q if rev else q
    spot, level = lax.rem(u, PLANE), u // PLANE

    def device(at):
        return (section, n - 1 - at if rev else at)

    peers = [lax.rem(spot + k, PLANE) for k in range(1, PLANE)]
    barrier = pltpu.get_barrier_semaphore()
    for peer in peers:
        pl.semaphore_signal(barrier, inc=1, device_id=device(level * PLANE + peer), device_id_type=MESH)

    @pl.when(level > 0)
    def _():
        pl.semaphore_signal(barrier, inc=1, device_id=device(u - PLANE), device_id_type=MESH)

    pl.semaphore_wait(barrier, PLANE - 1 + (level < planes - 1).astype(jnp.int32))

    def group(at):
        return pl.ds(pl.multiple_of(at * LANES, LANES), LANES)

    first = []
    for k, peer in enumerate(peers):
        to = device(level * PLANE + peer)
        first.append(
            pltpu.make_async_remote_copy(
                src_ref=d_ref.at[:, group(peer)], dst_ref=dbox.at[spot],
                send_sem=send_d.at[k], recv_sem=recv_d.at[k], device_id=to, device_id_type=MESH,
            )
        )
        first.append(
            pltpu.make_async_remote_copy(
                src_ref=s_ref.at[:, group(peer)], dst_ref=inbox.at[spot],
                send_sem=send_a.at[k], recv_sem=recv_a.at[k], device_id=to, device_id_type=MESH,
            )
        )
    for copy in first:
        copy.start()
    inbox[spot] = s_ref[:, group(spot)]
    dbox[spot] = d_ref[:, group(spot)]
    for copy in first:
        copy.wait()

    cuts = LANES // 256
    for b in range(cuts):
        at = slice(b * 256, b * 256 + 256)
        state = inbox[0, :, at].astype(F32)
        decay = dbox[0, 0:1, at]
        for p in range(1, PLANE):
            parts[p, :, at] = state
            decs[p, 0:1, at] = decay
            d = dbox[p, 0:1, at]
            state = d * state + inbox[p, :, at].astype(F32)
            decay = decay * d
        total[:, at] = state
        decs[0, 0:1, at] = decay

    def chain(b):
        return pltpu.make_async_remote_copy(
            src_ref=chain_out.at[b], dst_ref=chain_in.at[b],
            send_sem=send_c.at[b], recv_sem=recv_c.at[b],
            device_id=device(lax.rem(u + PLANE, n)), device_id_type=MESH,
        )

    last = []
    for b in range(cuts):
        at = slice(b * 256, b * 256 + 256)

        @pl.when(level > 0)
        def _():
            chain(b).wait_recv()

        @pl.when(level == 0)
        def _():
            chain_in[b] = jnp.zeros((128, 256), chain_in.dtype)

        enter = chain_in[b].astype(F32)

        @pl.when(level < planes - 1)
        def _():
            chain_out[b] = (decs[0, 0:1, at] * enter + total[:, at]).astype(chain_out.dtype)
            chain(b).start()

        outbox[0, :, at] = enter.astype(outbox.dtype)
        for p in range(1, PLANE):
            outbox[p, :, at] = (decs[p, 0:1, at] * enter + parts[p, :, at]).astype(outbox.dtype)
        mine = pl.ds(pl.multiple_of(spot * LANES + b * 256, 256), 256)
        o_ref[:, mine] = outbox[spot, :, at]
        for k, peer in enumerate(peers):
            copy = pltpu.make_async_remote_copy(
                src_ref=outbox.at[peer, :, pl.ds(b * 256, 256)], dst_ref=o_ref.at[:, mine],
                send_sem=send_o.at[b * 3 + k], recv_sem=recv_o.at[b * 3 + k],
                device_id=device(level * PLANE + peer), device_id_type=MESH,
            )
            copy.start()
            last.append(copy)
    for copy in last:
        copy.wait()

    @pl.when(level < planes - 1)
    def _():
        for b in range(cuts):
            chain(b).wait_send()


def exchange(state, decay, n, rev):
    vmem = pl.BlockSpec(memory_space=pltpu.VMEM)
    dma = pltpu.SemaphoreType.DMA
    cuts = LANES // 256
    return pl.pallas_call(
        functools.partial(exchange_kernel, n, rev),
        out_shape=sds(128, INNER, state.dtype),
        in_specs=[vmem, vmem],
        out_specs=vmem,
        scratch_shapes=[
            pltpu.VMEM((PLANE, 128, LANES), state.dtype),
            pltpu.VMEM((PLANE, 8, LANES), F32),
            pltpu.VMEM((PLANE, 128, LANES), F32),
            pltpu.VMEM((PLANE, 8, LANES), F32),
            pltpu.VMEM((128, LANES), F32),
            pltpu.VMEM((cuts, 128, 256), state.dtype),
            pltpu.VMEM((cuts, 128, 256), state.dtype),
            pltpu.VMEM((PLANE, 128, LANES), state.dtype),
            dma((3,)), dma((3,)), dma((3,)), dma((3,)),
            dma((cuts,)), dma((cuts,)), dma((3 * cuts,)), dma((3 * cuts,)),
        ],
        compiler_params=pltpu.CompilerParams(
            collective_id=2 if rev else 1, has_side_effects=True, vmem_limit_bytes=32 * MIB
        ),
    )(state, decay)


def decay_block(later, earlier):
    return jnp.exp(jnp.minimum(later - earlier, 0.0))


def head_lanes(parts, i):
    at = (i // 2) * 128
    here = (iota((ROWS, 128), 1) < HEADDIM) if i % 2 == 0 else (iota((ROWS, 128), 1) >= HEADDIM)
    return [jnp.where(here, part[:, at : at + 128], jnp.zeros((), BF16)) for part in parts]


def mix_kernel(
    g_ref, step_ref, cum_ref, cumt_ref, val_ref, gate_ref, c_ref, car_ref, lp_ref, gain_ref,
    y_ref, low_ref, gated_ref, sum_ref,
):
    j = pl.program_id(0)
    heads = expander(j)
    cum = dot_nn(cum_ref[...], heads)
    values = val_ref[...]
    scaled = split2(values * dot_nn(step_ref[...], heads))
    car_high, car_rest = split2(car_ref[...])
    across = dot_nn(c_ref[...], jnp.concatenate([car_high, car_high, car_rest], axis=0))
    y = jnp.exp(cum) * across + lp_ref[0:1, :] * values
    sides = []
    for pair in range(WIDE // 128):
        top = jnp.zeros((HALF, 128), F32)
        bottom = jnp.zeros((HALF, 128), F32)
        for i in (2 * pair, 2 * pair + 1):
            row = cumt_ref[pl.ds((WIDE // HEADDIM) * j + i, 1), :]
            column = cum[:, i * HEADDIM : i * HEADDIM + 1]
            part = head_lanes(scaled, i)
            upper = split2(g_ref[0:HALF, 0:HALF] * decay_block(column[0:HALF], row[:, 0:HALF]))
            top = top + fine(dot_nn, upper, [v[0:HALF] for v in part])
            lower = split2(g_ref[HALF:ROWS, :] * decay_block(column[HALF:ROWS], row))
            bottom = bottom + fine(dot_nn, lower, part)
        sides.append(jnp.concatenate([top, bottom], axis=0))
    y = y + jnp.concatenate(sides, axis=1)
    y_ref[...] = y
    gate = gate_ref[...]
    gated = y * (gate * sigmoid(gate))
    gated_ref[j] = gated

    @pl.when(j == 0)
    def _():
        sum_ref[...] = jnp.zeros_like(sum_ref)

    sum_ref[...] += gated * gated

    @pl.when(j == STEPS - 1)
    def _():
        mean = jnp.sum(sum_ref[...], axis=1, keepdims=True) * (1.0 / INNER)
        scale = lax.rsqrt(mean + EPS)
        for k in range(STEPS):
            at = slice(k * WIDE, k * WIDE + WIDE)
            low_ref[:, at] = (gated_ref[k] * scale * gain_ref[1:2, at]).astype(BF16)


def mix(g, step, cum, cumt, values, proj, c, carried, lp):
    return pl.pallas_call(
        mix_kernel,
        grid=(STEPS,),
        in_specs=[
            whole((ROWS, ROWS)), whole((ROWS, 384)), whole((ROWS, 384)), whole((128, ROWS)),
            lanes(ROWS), lanes(ROWS), whole((ROWS, 384)), lanes(128), lanes(8),
            whole((8, INNER)),
        ],
        out_specs=[lanes(ROWS), whole((ROWS, INNER))],
        out_shape=[sds(ROWS, INNER, F32), sds(ROWS, INNER, BF16)],
        scratch_shapes=[pltpu.VMEM((STEPS, ROWS, WIDE), F32), pltpu.VMEM((ROWS, WIDE), F32)],
        compiler_params=grid_params(),
        cost_estimate=pl.CostEstimate(flops=3 * 10**9, bytes_accessed=14 * MIB, transcendentals=4 * 10**6),
    )(g, step, cum, cumt, values, proj, c, carried, lp, lp)


def gate_back_kernel(
    dg_ref, y_ref, gate_ref, cum_ref, ct_ref, lp_ref, dy_ref, dgate_ref, gain_ref, dcar_ref,
    dg_all, y_all, gate_all, square_acc, cross_acc,
):
    phase, j = pl.program_id(0), pl.program_id(1)

    @pl.when(jnp.logical_and(phase == 0, j == 0))
    def _():
        square_acc[...] = jnp.zeros_like(square_acc)
        cross_acc[...] = jnp.zeros_like(cross_acc)

    @pl.when(phase == 0)
    def _():
        dg, y, gate = dg_ref[...], y_ref[...], gate_ref[...]
        dg_all[j], y_all[j], gate_all[j] = dg, y, gate
        gated = y * (gate * sigmoid(gate))
        square_acc[...] += gated * gated
        cross_acc[...] += dg * lp_ref[1:2, :] * gated

    @pl.when(phase == 1)
    def _():
        r = lax.rsqrt(jnp.sum(square_acc[...], axis=1, keepdims=True) * (1.0 / INNER) + EPS)
        m = jnp.sum(cross_acc[...], axis=1, keepdims=True) * (1.0 / INNER) * r * r
        dg, y, gate = dg_all[j], y_all[j], gate_all[j]
        s = sigmoid(gate)
        silu = gate * s
        gated = y * silu
        gain_ref[...] = jnp.broadcast_to(jnp.sum(dg * gated * r, axis=0, keepdims=True), (8, WIDE))
        d_gated = r * (dg * lp_ref[1:2, :] - gated * m)
        dy = d_gated * silu
        dy_ref[...] = dy
        dgate_ref[...] = (d_gated * y * (s + silu * (1.0 - s))).astype(BF16)
        cum = dot_nn(cum_ref[...], expander(j))
        dcar_ref[...] = dot_nn(ct_ref[...], (dy * jnp.exp(cum)).astype(BF16)).astype(BF16)


def gate_back(dg, y, proj, cum, ct, lp):
    def first(rows):
        return pl.BlockSpec((rows, WIDE), lambda p, j: (0, j * (1 - p) + (STEPS - 1) * p))

    def second(rows):
        return pl.BlockSpec((rows, WIDE), lambda p, j: (0, j * p))

    def both(shape):
        return pl.BlockSpec(shape, lambda p, j: (0, 0))

    kept = pltpu.VMEM((STEPS, ROWS, WIDE), F32)
    return pl.pallas_call(
        gate_back_kernel,
        grid=(2, STEPS),
        in_specs=[
            first(ROWS), first(ROWS), first(ROWS), both((ROWS, 384)), both((128, ROWS)),
            pl.BlockSpec((8, WIDE), lambda p, j: (0, j)),
        ],
        out_specs=[second(ROWS), second(ROWS), second(8), second(128)],
        out_shape=[sds(ROWS, INNER, F32), sds(ROWS, INNER, BF16), sds(8, INNER, F32), sds(128, INNER, BF16)],
        scratch_shapes=[kept, kept, kept, pltpu.VMEM((ROWS, WIDE), F32), pltpu.VMEM((ROWS, WIDE), F32)],
        compiler_params=grid_params(),
        cost_estimate=pl.CostEstimate(flops=10**9, bytes_accessed=16 * MIB, transcendentals=2 * 10**6),
    )(dg, y, proj, cum, ct, lp)


def core_back_kernel(
    x_ref, bc_ref, raw_ref, xh_ref, bch_ref, xw_ref, bcw_ref, hp_ref,
    step_ref, cum_ref, cumt_ref, gt_ref, b_ref, c_ref, y_ref, dy_ref, car_ref, late_ref, lp_ref,
    dx_ref, dbc_ref, tail_ref, tailbc_ref, head_ref, headbc_ref, taps_ref, tapsbc_ref, draw_ref, hg_ref,
    dgt_acc, dc_acc, db_acc, dcum_acc, dstep_acc, rows_acc,
):
    j = pl.program_id(0)

    @pl.when(j == 0)
    def _():
        for acc in (dgt_acc, dc_acc, db_acc, dcum_acc, dstep_acc, rows_acc):
            acc[...] = jnp.zeros_like(acc)

    ext = extended(x_ref[...], xh_ref[...])
    pre = conv_pre(ext, xw_ref[...])
    sig = sigmoid(pre)
    values = pre * sig
    heads, to_heads = expander(j), collector(j)
    step = dot_nn(step_ref[...], heads)
    cum = dot_nn(cum_ref[...], heads)
    last = cum[ROWS - 1 : ROWS]
    scaled = values * step
    scaled_parts = split2(scaled)
    dy = dy_ref[...]
    dy_parts = split2(dy)
    sides = []
    for pair in range(WIDE // 128):
        top = jnp.zeros((HALF, 128), F32)
        bottom = jnp.zeros((HALF, 128), F32)
        at = slice(pair * 128, pair * 128 + 128)
        own = [part[:, at] for part in scaled_parts]
        for i in (2 * pair, 2 * pair + 1):
            row = cumt_ref[pl.ds((WIDE // HEADDIM) * j + i, 1), :]
            column = cum[:, i * HEADDIM : i * HEADDIM + 1]
            part = head_lanes(dy_parts, i)
            decay = decay_block(row, column[0:HALF])
            top = top + fine(dot_nn, split2(gt_ref[0:HALF, :] * decay), part)
            dgt_acc[0:HALF, :] += fine(dot_nt, [v[0:HALF] for v in own], part) * decay
            decay = decay_block(row[:, HALF:ROWS], column[HALF:ROWS])
            late_part = [v[HALF:ROWS] for v in part]
            bottom = bottom + fine(dot_nn, split2(gt_ref[HALF:ROWS, HALF:ROWS] * decay), late_part)
            dgt_acc[HALF:ROWS, HALF:ROWS] += fine(dot_nt, [v[HALF:ROWS] for v in own], late_part) * decay
        sides.append(jnp.concatenate([top, bottom], axis=0))
    car, late = car_ref[...], late_ref[...]
    to_end = jnp.exp(last - cum)
    d_ended = dot_nn(b_ref[:, 0:128], late)
    ended = scaled * to_end
    dc_acc[...] += fine(dot_nt, split2(dy * jnp.exp(cum)), split2(car))
    db_acc[...] += dot_nt(ended.astype(BF16), late)
    d_total = jnp.concatenate(sides, axis=1) + to_end * d_ended
    skip_w = lp_ref[0:1, :]
    dcum_acc[...] += collect(dy * (y_ref[...] - skip_w * values) - scaled * d_total, to_heads)
    dstep_acc[...] += collect(d_total * values, to_heads)
    at_last = jnp.exp(last) * jnp.sum(late.astype(F32) * car, axis=0, keepdims=True)
    at_last = at_last + jnp.sum(ended * d_ended, axis=0, keepdims=True)
    skip = jnp.sum(dy * values, axis=0, keepdims=True)
    rows_acc[...] += collect(jnp.concatenate([at_last, skip, jnp.zeros((6, WIDE), F32)], axis=0), to_heads)
    d_pre = (skip_w * dy + step * d_total) * (sig + values * (1.0 - sig))
    taps_ref[...] = tap_grads(d_pre, ext)
    head_ref[...] = d_pre[0:8]
    d_conv = conv_back(d_pre, xw_ref[...])
    dx_ref[...] = d_conv.astype(BF16)
    tail_ref[...] = d_conv[ROWS - 8 : ROWS]

    @pl.when(j == STEPS - 1)
    def _():
        seen = iota((ROWS, ROWS), 1) >= iota((ROWS, ROWS), 0)
        d_gt = split2(jnp.where(seen, dgt_acc[...], 0.0))
        d_c = dc_acc[...] + fine(dot_tn, d_gt, halves(b_ref))
        d_b = db_acc[...] + fine(dot_nn, d_gt, halves(c_ref))
        ext_bc = extended(bc_ref[...], bch_ref[...])
        pre_bc = conv_pre(ext_bc, bcw_ref[...])
        sig_bc = sigmoid(pre_bc)
        d_pre_bc = jnp.concatenate([d_b, d_c], axis=1) * (sig_bc + pre_bc * sig_bc * (1.0 - sig_bc))
        tapsbc_ref[...] = tap_grads(d_pre_bc, ext_bc)
        headbc_ref[...] = d_pre_bc[0:8]
        d_conv_bc = conv_back(d_pre_bc, bcw_ref[...])
        dbc_ref[...] = d_conv_bc.astype(BF16)
        tailbc_ref[...] = d_conv_bc[ROWS - 8 : ROWS]
        raw, step_all, rate = step_parts(raw_ref, hp_ref)
        end = iota((ROWS, 128), 0) == ROWS - 1
        d_cum_all = dcum_acc[...] + jnp.where(end, rows_acc[0:1, :], 0.0)
        d_log = exact_left(triangle(False), d_cum_all)
        d_step = dstep_acc[...] + rate * d_log
        d_raw = jnp.where(iota((ROWS, 128), 1) < HEADS, d_step * sigmoid(raw), 0.0)
        draw_ref[...] = d_raw.astype(BF16)
        hg_ref[...] = jnp.concatenate(
            [
                jnp.sum(d_raw, axis=0, keepdims=True),
                jnp.sum(d_log * rate * step_all, axis=0, keepdims=True),
                rows_acc[1:2, :],
                jnp.zeros((5, 128), F32),
            ],
            axis=0,
        )


def core_back(proj, halo, taps, hp, step, cum, cumt, gt, b, c, y, dy, carried, late, lp):
    acc = pltpu.VMEM((ROWS, 128), F32)
    return pl.pallas_call(
        core_back_kernel,
        grid=(STEPS,),
        in_specs=[
            lanes(ROWS, STEPS), fixed(ROWS, 2 * STEPS), fixed(ROWS, 50, 128),
            lanes(8), fixed(8, STEPS), lanes(8), fixed(8, STEPS), whole((8, 128)),
            whole((ROWS, 384)), whole((ROWS, 384)), whole((128, ROWS)), whole((ROWS, ROWS)),
            whole((ROWS, 256)), whole((ROWS, 384)),
            lanes(ROWS), lanes(ROWS), lanes(128), lanes(128), lanes(8),
        ],
        out_specs=[
            lanes(ROWS), whole((ROWS, 256)), lanes(8), whole((8, 256)), lanes(8), whole((8, 256)),
            lanes(8), whole((8, 256)), whole((ROWS, 128)), whole((8, 128)),
        ],
        out_shape=[
            sds(ROWS, INNER, BF16), sds(ROWS, 256, BF16), sds(8, INNER, F32), sds(8, 256, F32),
            sds(8, INNER, F32), sds(8, 256, F32), sds(8, INNER, F32), sds(8, 256, F32),
            sds(ROWS, 128, BF16), sds(8, 128, F32),
        ],
        scratch_shapes=[pltpu.VMEM((ROWS, ROWS), F32), acc, acc, acc, acc, pltpu.VMEM((8, 128), F32)],
        compiler_params=grid_params(),
        cost_estimate=pl.CostEstimate(flops=8 * 10**9, bytes_accessed=14 * MIB, transcendentals=5 * 10**6),
    )(
        proj, proj, proj, halo, halo, taps, taps, hp,
        step, cum, cumt, gt, b, c, y, dy, carried, late, lp,
    )


def swap(value):
    return lax.ppermute(value, "section", [(0, 1), (1, 0)])


def shifted(value, distance, n):
    return lax.ppermute(value, "seq", [(i, i + distance) for i in range(n) if 0 <= i + distance < n])


def plane_route(k, n):
    return [(i, i - i % PLANE + (i + k) % PLANE) for i in range(n)]


def rms(value):
    return lax.rsqrt(jnp.mean(value * value, axis=-1, keepdims=True) + EPS)


def tied(value, *others):
    return lax.optimization_barrier((value, *others))[0]


def copies_of(value, n):
    return [value] + [lax.ppermute(value, "seq", plane_route(k, n)) for k in range(1, PLANE)]


def pieces_of(value, n):
    spot = lax.axis_index("seq") % PLANE
    width = value.shape[1] // PLANE
    got = [lax.dynamic_slice_in_dim(value, spot * width, width, 1)]
    for k in range(1, PLANE):
        part = lax.dynamic_slice_in_dim(value, (spot + k) % PLANE * width, width, 1)
        got.append(lax.ppermute(part, "seq", plane_route(k, n)))
    return got


def partial_grad(left, right):
    core = lax.axis_index("section")
    left, right = jnp.concatenate(left, axis=0), jnp.concatenate(right, axis=0)
    half = right.shape[1] // 2
    away = dot_tn(left, lax.dynamic_slice_in_dim(right, (1 - core) * half, half, 1)).astype(BF16)
    mine = dot_tn(left, lax.dynamic_slice_in_dim(right, core * half, half, 1))
    return (mine + swap(away).astype(F32)).astype(BF16)


def plane_rows(partials, n):
    planes = n // PLANE
    columns = [[p + PLANE * z for z in range(planes)] for p in range(PLANE)]
    joined = jnp.concatenate([part.reshape(planes, D // planes, -1) for part in partials], axis=2)
    joined = lax.psum_scatter(joined, "seq", scatter_dimension=0, axis_index_groups=columns)
    return jnp.split(joined, [sum(p.shape[1] for p in partials[:k]) for k in range(1, len(partials))], axis=1)


def stacked_halves(value, n):
    planes = n // PLANE
    value = value.reshape(planes, -1, D // 2)
    return jnp.concatenate([value[:, :, : D // 4], value[:, :, D // 4 :]], axis=1).reshape(D, D // 4)


def unstacked_halves(value):
    rows = value.shape[0] // 2
    return jnp.concatenate([value[:rows], value[rows:]], axis=1)


def by_row(value, n):
    in_plane = [[PLANE * z + p for p in range(PLANE)] for z in range(n // PLANE)]
    rows = value.shape[0] // PLANE
    value = value.reshape(PLANE, rows, value.shape[1])
    return lax.all_to_all(value, "seq", 0, 0, axis_index_groups=in_plane).transpose(1, 0, 2)


SIZES = [D, CONVD * CONV, CONVD, HEADS, HEADS, HEADS, INNER]


def split_small(flat):
    parts, at = [], 0
    for size in SIZES:
        parts.append(flat[at : at + size])
        at += size
    return parts


def unpack_params(flat):
    norm_g, conv_w, conv_b, dt_b, a_lg, skip_w, gate_g = split_small(flat)
    taps = jnp.concatenate(
        [conv_w.reshape(CONV, CONVD), conv_b[None], jnp.zeros((3, CONVD), F32)], axis=0
    )
    pad = jnp.zeros((128 - HEADS,), F32)
    hp = jnp.concatenate([dt_b, pad, a_lg, pad, jnp.zeros((6 * 128,), F32)]).reshape(8, 128)
    lp = jnp.concatenate(
        [jnp.repeat(skip_w, HEADDIM)[None], gate_g[None], jnp.zeros((6, INNER), F32)], axis=0
    )
    return norm_g, taps, hp, lp


def per_device(
    inputs, cotangent, norm_gain, in_weight, conv_weight, conv_bias, dt_bias, a_log, d_skip,
    gate_norm_gain, out_weight,
):
    n = lax.axis_size("seq")
    planes = n // PLANE
    core = lax.axis_index("section")
    place = lax.axis_index("seq")
    first = core == 0
    own_in, own_out = in_weight[0].T, out_weight[0]
    other_in, other_out = swap(own_in), swap(own_out)
    own_small = jnp.concatenate(
        [
            norm_gain[0], conv_weight[0].T.reshape(-1), conv_bias[0], dt_bias[0], a_log[0], d_skip[0],
            gate_norm_gain[0],
        ]
    )
    other_small = swap(own_small)
    flags = [(core == layer).astype(jnp.int32)[None] for layer in range(2)]
    params = [
        unpack_params(jnp.where(first, own_small, other_small)),
        unpack_params(jnp.where(first, other_small, own_small)),
    ]

    def mine(pair):
        return lax.dynamic_index_in_dim(pair, core, 0, keepdims=False)

    def project(layer, h):
        normed = (h * rms(h) * params[layer][0]).astype(BF16)
        return normed, mm(normed, own_in, other_in, flags[layer], True, 1664)

    def blocks(layer, proj):
        _, taps, hp, _ = params[layer]
        halo = shifted(proj[ROWS - 8 :, INNER : INNER + CONVD], 1, n)
        return halo, front(proj, halo, taps, hp)

    def finish(layer, h, proj, parts, carried):
        values, _, _, step, cum, cumt, _, c, _, g, _ = parts
        y, gated_low = mix(g, step, cum, cumt, values, proj, c, carried, params[layer][3])
        return y, gated_low, h + mm(gated_low, own_out, other_out, flags[layer], False, 768)

    def by_owner(gated_low):
        width = INNER // n
        return gated_low.reshape(ROWS, planes, PLANE, width).transpose(0, 2, 1, 3).reshape(ROWS, INNER)

    d_out_1 = mine(cotangent)
    lows_1 = copies_of(d_out_1, n)
    h_0 = mine(inputs).astype(F32)
    normed_0, proj_0 = project(0, h_0)
    proj_0 = tied(proj_0, *lows_1)
    halo_0, parts_0 = blocks(0, proj_0)
    carried_0 = exchange(parts_0[1], parts_0[2], n, False)
    normeds_0 = copies_of(tied(normed_0, carried_0), n)
    y_0, gated_0, out_0 = finish(0, h_0, proj_0, parts_0, carried_0)
    act_0 = out_0.astype(BF16)

    h_1 = act_0.astype(F32)
    normed_1, proj_1 = project(1, h_1)
    proj_1 = tied(proj_1, *normeds_0)
    halo_1, parts_1 = blocks(1, proj_1)
    gateds_0 = pieces_of(by_owner(tied(gated_0, halo_1)), n)
    carried_1 = exchange(tied(parts_1[1], *gateds_0), parts_1[2], n, False)
    normeds_1 = copies_of(tied(normed_1, carried_1), n)
    y_1, gated_1, out_1 = finish(1, h_1, proj_1, parts_1, carried_1)
    act_1 = out_1.astype(BF16)

    def gate_side(layer, d_low, y, proj, parts):
        d_gated_low = mm(d_low, own_out, other_out, flags[layer], True, 1024)
        return gate_back(d_gated_low, y, proj, parts[4], parts[8], params[layer][3])

    def core_side(layer, proj, halo, parts, y, dy, carried, late):
        _, taps, hp, lp = params[layer]
        _, _, _, step, cum, cumt, b, c, _, _, gt = parts
        return core_back(proj, halo, taps, hp, step, cum, cumt, gt, b, c, y, dy, carried, late, lp)

    def conv_side(layer, back):
        dx, dbc, tail, tailbc, head, headbc, gtaps, gtapsbc, d_raw, heads = back
        w = params[layer][1]
        a = shifted(jnp.concatenate([head, headbc], axis=1), -1, n)
        fix = jnp.concatenate(
            [
                jnp.zeros((5, CONVD), F32),
                w[0:1] * a[0:1],
                w[0:1] * a[1:2] + w[1:2] * a[0:1],
                w[0:1] * a[2:3] + w[1:2] * a[1:2] + w[2:3] * a[0:1],
            ],
            axis=0,
        )
        low = (jnp.concatenate([tail, tailbc], axis=1) + fix).astype(BF16)
        main = jnp.concatenate([dx[: ROWS - 8], dbc[: ROWS - 8]], axis=1)
        d_conv = jnp.concatenate([main, low], axis=0)
        return d_conv, d_raw[:, :HEADS]

    def norm_side(layer, h, d_out, d_proj):
        norm_g = params[layer][0]
        d_normed = mm(d_proj, own_in, other_in, flags[layer], False, 512)
        r = rms(h)
        v = d_normed * norm_g
        d_h = d_out + r * (v - h * (r * r * jnp.mean(v * h, axis=-1, keepdims=True)))
        return d_h, jnp.sum(d_normed * h * r, axis=0)

    def small_of(norm_gain_grad, back, gate_gain):
        taps_all = jnp.concatenate([back[6], back[7]], axis=1)
        heads = back[9]
        return jnp.concatenate(
            [
                norm_gain_grad, taps_all[:CONV].reshape(-1), taps_all[CONV],
                heads[0, :HEADS], heads[1, :HEADS], heads[2, :HEADS], gate_gain[0],
            ]
        )

    def padded(d_conv, d_raw):
        pad = jnp.zeros((ROWS, REST - CONVD - HEADS), BF16)
        return jnp.concatenate([d_conv, d_raw, pad], axis=1)

    dy_1, d_gate_1, gain_1, d_carried_1 = gate_side(1, d_out_1, y_1, proj_1, parts_1)
    late_1 = exchange(tied(d_carried_1, *normeds_1), parts_1[2], n, True)
    gates_1 = pieces_of(tied(d_gate_1, late_1), n)
    gateds_1 = pieces_of(by_owner(tied(gated_1, late_1)), n)
    back_1 = core_side(1, proj_1, halo_1, parts_1, y_1, dy_1, carried_1, late_1)
    back_1 = [tied(back_1[0], *gates_1, *gateds_1)] + list(back_1[1:])
    d_conv_1, d_raw_1 = conv_side(1, back_1)
    rests_1 = pieces_of(padded(d_conv_1, d_raw_1), n)
    d_1, ng_1 = norm_side(1, h_1, d_out_1.astype(F32), jnp.concatenate([d_gate_1, d_conv_1, d_raw_1], axis=1))

    d_out_0 = d_1.astype(BF16)
    lows_0 = copies_of(tied(d_out_0, *rests_1), n)
    dy_0, d_gate_0, gain_0, d_carried_0 = gate_side(0, d_out_0, y_0, proj_0, parts_0)
    outw_1 = stacked_halves(partial_grad(gateds_1, lows_1), n)
    grads_1 = [outw_1, partial_grad(normeds_1, gates_1), partial_grad(normeds_1, rests_1)]
    late_0 = exchange(tied(d_carried_0, *grads_1), parts_0[2], n, True)
    outw_1, gatew_1, restw_1 = plane_rows(grads_1, n)
    gates_0 = pieces_of(tied(d_gate_0, late_0, *lows_0), n)
    outw_0 = stacked_halves(partial_grad(gateds_0, lows_0), n)
    back_0 = core_side(0, proj_0, halo_0, parts_0, y_0, dy_0, carried_0, tied(late_0, *lows_0, outw_0))
    (outw_0,) = plane_rows([outw_0], n)
    back_0 = [tied(back_0[0], *gates_0, outw_1, gatew_1, restw_1)] + list(back_0[1:])
    d_conv_0, d_raw_0 = conv_side(0, back_0)
    rests_0 = pieces_of(padded(d_conv_0, d_raw_0), n)
    (gatew_0,) = plane_rows([partial_grad(normeds_0, gates_0)], n)
    d_0, ng_0 = norm_side(0, h_0, d_out_0.astype(F32), jnp.concatenate([d_gate_0, d_conv_0, d_raw_0], axis=1))
    (restw_0,) = plane_rows([partial_grad(normeds_0, rests_0)], n)

    def joined(early, late):
        own = jnp.where(first, early, late)
        other = swap(jnp.where(first, late, early))
        return jnp.where(first, own, other), jnp.where(first, other, own)

    def both(early, late):
        return jnp.stack(joined(early, late))[None]

    acts = both(act_0, act_1)
    input_grads = both(d_0, d_1)
    gate_w = jnp.stack(joined(by_row(gatew_0, n), by_row(gatew_1, n)), axis=2)
    rest_w = jnp.stack(joined(by_row(restw_0, n), by_row(restw_1, n)), axis=2)
    rows = D // n
    g_in = jnp.concatenate(
        [gate_w.reshape(rows, INNER), rest_w.reshape(rows, REST)[:, : PROJ - INNER]], axis=1
    ).astype(F32)
    g_out = jnp.concatenate(joined(unstacked_halves(outw_0), unstacked_halves(outw_1)), axis=1).astype(F32)
    small_0, small_1 = small_of(ng_0, back_0, gain_0), small_of(ng_1, back_1, gain_1)
    small = jnp.where(first, small_0, small_1) + swap(jnp.where(first, small_1, small_0))
    reach = 1
    while reach < n:
        small = small + lax.ppermute(small, "seq", [(i, i ^ reach) for i in range(n)])
        reach *= 2
    norm_g, conv_w, conv_b, dt_b, a_lg, skip_w, gate_g = split_small(small)

    def share(value):
        rows = value.shape[0] // n
        return lax.dynamic_slice_in_dim(value, place * rows, rows, 0)[None]

    conv_rows = CONVD // n
    conv_w = lax.dynamic_slice_in_dim(conv_w.reshape(CONV, CONVD), place * conv_rows, conv_rows, 1).T
    return (
        acts, input_grads, share(norm_g), g_in[None], conv_w[None], share(conv_b),
        dt_b[None], a_lg[None], skip_w[None], share(gate_g), g_out[None],
    )


def solution(mesh):
    in_specs = (
        P(None, "seq", None), P(None, "seq", None), P("section", None), P("section", None, None),
        P("section", None, None), P("section", None), P("section", None), P("section", None),
        P("section", None), P("section", None), P("section", None, None),
    )
    out_specs = (
        P("section", None, "seq", None), P("section", None, "seq", None), P("section", "seq"),
        P("section", "seq", None), P("section", "seq", None), P("section", "seq"), P("section", None),
        P("section", None), P("section", None), P("section", "seq"), P("section", "seq", None),
    )
    return jax.shard_map(per_device, mesh=mesh, in_specs=in_specs, out_specs=out_specs, check_vma=False)
```

```python
import functools

import jax
import jax.numpy as jnp
from jax import lax
from jax.experimental import pallas as pl
from jax.experimental.pallas import tpu as pltpu
from jax.sharding import PartitionSpec as P

D = 1536
INNER = 3072
STATE = 128
HEADS = 48
HEADDIM = 64
CONV = 4
CONVD = 3328
PROJ = 6448
ROWS = 256
WIDE = 256
STEPS = INNER // WIDE
HALF = ROWS // 2
PLANE = 4
LANES = INNER // PLANE
REST = 3584
EPS = 1e-05
MIB = 2**20
MESH = pl.DeviceIdType.MESH
F32 = jnp.float32
BF16 = jnp.bfloat16


def dot_nn(a, b):
    return lax.dot_general(a, b, (((1,), (0,)), ((), ())), preferred_element_type=F32)


def dot_tn(a, b):
    return lax.dot_general(a, b, (((0,), (0,)), ((), ())), preferred_element_type=F32)


def dot_nt(a, b):
    return lax.dot_general(a, b, (((1,), (1,)), ((), ())), preferred_element_type=F32)


def split3(v):
    high = v.astype(BF16)
    rest = v - high.astype(F32)
    mid = rest.astype(BF16)
    return high, mid, (rest - mid.astype(F32)).astype(BF16)


def split2(v):
    high = v.astype(BF16)
    return high, (v - high.astype(F32)).astype(BF16)


def fine(dot, a, b):
    return dot(a[0], b[0]) + (dot(a[0], b[1]) + dot(a[1], b[0]))


def halves(ref):
    return ref[:, 0:128], ref[:, 128:256]


def parts3(v):
    return jnp.concatenate(split3(v), axis=1)


def exact_left(ones, v):
    a, b, c = split3(v)
    return dot_nn(ones, a) + (dot_nn(ones, b) + dot_nn(ones, c))


def iota(shape, dim):
    return lax.broadcasted_iota(jnp.int32, shape, dim)


def expander(step):
    head_of = (WIDE // HEADDIM) * step + lax.shift_right_logical(iota((128, WIDE), 1), 6)
    ones = (iota((128, WIDE), 0) == head_of).astype(F32).astype(BF16)
    return jnp.concatenate([ones, ones, ones], axis=0)


def collector(step):
    head_of = (WIDE // HEADDIM) * step + lax.shift_right_logical(iota((WIDE, 128), 0), 6)
    return (iota((WIDE, 128), 1) == head_of).astype(F32).astype(BF16)


def collect(v, ones):
    a, b, c = split3(v)
    return dot_nn(a, ones) + (dot_nn(b, ones) + dot_nn(c, ones))


def triangle(lower):
    rows, cols = iota((ROWS, ROWS), 0), iota((ROWS, ROWS), 1)
    return ((rows >= cols) if lower else (rows <= cols)).astype(F32).astype(BF16)


def sigmoid(v):
    return 0.5 * jnp.tanh(0.5 * v) + 0.5


def extended(block, halo):
    return jnp.concatenate([halo, block], axis=0)


def conv_pre(ext, taps):
    out = taps[4:5] + taps[0:1] * ext[5 : 5 + ROWS]
    for k in range(1, CONV):
        out = out + taps[k : k + 1] * ext[5 + k : 5 + k + ROWS]
    return out


def conv_back(d_pre, taps):
    ext = jnp.concatenate([d_pre, jnp.zeros((8, d_pre.shape[1]), F32)], axis=0)
    out = taps[3:4] * d_pre
    for k in range(CONV - 1):
        out = out + taps[k : k + 1] * ext[3 - k : 3 - k + ROWS]
    return out


def tap_grads(d_pre, ext):
    rows = [jnp.sum(d_pre * ext[5 + k : 5 + k + ROWS], axis=0, keepdims=True) for k in range(CONV)]
    rows.append(jnp.sum(d_pre, axis=0, keepdims=True))
    rows.append(jnp.zeros((3, d_pre.shape[1]), F32))
    return jnp.concatenate(rows, axis=0)


def step_parts(raw_ref, hp_ref):
    real = iota((ROWS, 128), 1) < HEADS
    raw = jnp.where(real, raw_ref[...], 0.0) + hp_ref[0:1, :]
    step = jnp.maximum(raw, 0.0) + jnp.log1p(jnp.exp(-jnp.abs(raw)))
    step = jnp.where(real, step, 0.0)
    rate = jnp.where(real[0:1], -jnp.exp(hp_ref[1:2, :]), 0.0)
    return raw, step, rate


def mm_kernel(flag_ref, x_ref, own_ref, other_ref, o_ref, *, nt):
    dot = dot_nt if nt else dot_nn

    @pl.when(flag_ref[0] == 1)
    def _():
        o_ref[...] = dot(x_ref[...], own_ref[...])

    @pl.when(flag_ref[0] == 0)
    def _():
        o_ref[...] = dot(x_ref[...], other_ref[...])


def mm(x, own, other, flag, nt, tile):
    rows, depth = x.shape
    width = own.shape[0] if nt else own.shape[1]
    block = (tile, depth) if nt else (depth, tile)

    def place(j, keep):
        return (j * keep, 0) if nt else (0, j * keep)

    return pl.pallas_call(
        functools.partial(mm_kernel, nt=nt),
        grid_spec=pltpu.PrefetchScalarGridSpec(
            num_scalar_prefetch=1,
            grid=(pl.cdiv(width, tile),),
            in_specs=[
                pl.BlockSpec((rows, depth), lambda j, f: (0, 0)),
                pl.BlockSpec(block, lambda j, f: place(j, f[0])),
                pl.BlockSpec(block, lambda j, f: place(j, 1 - f[0])),
            ],
            out_specs=pl.BlockSpec((rows, tile), lambda j, f: (0, j)),
        ),
        out_shape=jax.ShapeDtypeStruct((rows, width), F32),
        compiler_params=pltpu.CompilerParams(vmem_limit_bytes=48 * MIB),
        cost_estimate=pl.CostEstimate(
            flops=2 * rows * depth * width, bytes_accessed=2 * depth * width, transcendentals=0
        ),
    )(flag, x, own, other)


def front_kernel(
    x_ref, bc_ref, raw_ref, xh_ref, bch_ref, xw_ref, bcw_ref, hp_ref,
    val_ref, state_ref, dec_ref, step_ref, cum_ref, cumt_ref, b_ref, c_ref, ct_ref, g_ref, gt_ref, bt_ref,
):
    j = pl.program_id(0)

    @pl.when(j == 0)
    def _():
        _, step, rate = step_parts(raw_ref, hp_ref)
        step_ref[...] = parts3(step)
        cum = exact_left(triangle(True), rate * step)
        cum_ref[...] = parts3(cum)
        cumt_ref[...] = cum.T
        pre = conv_pre(extended(bc_ref[...], bch_ref[...]), bcw_ref[...])
        both = pre * sigmoid(pre)
        b, c = both[:, 0:128], both[:, 128:256]
        b_low, c_low = split2(b), split2(c)
        b_ref[...] = jnp.concatenate(b_low, axis=1)
        c_ref[...] = jnp.concatenate([c_low[0], c_low[1], c_low[0]], axis=1)
        ct_ref[...] = c.T.astype(BF16)
        bt_ref[...] = jnp.concatenate(split2(b.T), axis=0)
        seen = iota((ROWS, ROWS), 0) >= iota((ROWS, ROWS), 1)
        g = jnp.where(seen, fine(dot_nt, c_low, b_low), 0.0)
        g_ref[...] = g
        gt_ref[...] = g.T

    pre = conv_pre(extended(x_ref[...], xh_ref[...]), xw_ref[...])
    values = pre * sigmoid(pre)
    val_ref[...] = values
    heads = expander(j)
    cum = dot_nn(cum_ref[...], heads)
    last = cum[ROWS - 1 : ROWS]
    high, rest = split2(values * dot_nn(step_ref[...], heads) * jnp.exp(last - cum))
    twice = dot_nn(bt_ref[...], high)
    state_ref[...] = twice[0:128] + twice[128:256] + dot_nn(bt_ref[0:128, :], rest)
    dec_ref[...] = jnp.broadcast_to(jnp.exp(last), (8, WIDE))


def whole(shape):
    return pl.BlockSpec(shape, lambda j: (0, 0))


def lanes(rows, first=0):
    return pl.BlockSpec((rows, WIDE), lambda j: (0, first + j))


def fixed(rows, at, width=WIDE):
    return pl.BlockSpec((rows, width), lambda j: (0, at))


def sds(rows, cols, dtype):
    return jax.ShapeDtypeStruct((rows, cols), dtype)


def grid_params():
    return pltpu.CompilerParams(vmem_limit_bytes=48 * MIB)


def front(proj, halo, taps, hp):
    square = (ROWS, ROWS)
    return pl.pallas_call(
        front_kernel,
        grid=(STEPS,),
        in_specs=[
            lanes(ROWS, STEPS), fixed(ROWS, 2 * STEPS), fixed(ROWS, 50, 128),
            lanes(8), fixed(8, STEPS), lanes(8), fixed(8, STEPS), whole((8, 128)),
        ],
        out_specs=[
            lanes(ROWS), lanes(128), lanes(8),
            whole((ROWS, 384)), whole((ROWS, 384)), whole((128, ROWS)),
            whole((ROWS, 256)), whole((ROWS, 384)), whole((128, ROWS)), whole(square), whole(square),
        ],
        out_shape=[
            sds(ROWS, INNER, F32), sds(128, INNER, F32), sds(8, INNER, F32),
            sds(ROWS, 384, BF16), sds(ROWS, 384, BF16), sds(128, ROWS, F32),
            sds(ROWS, 256, BF16), sds(ROWS, 384, BF16), sds(128, ROWS, BF16), sds(*square, F32), sds(*square, F32),
        ],
        scratch_shapes=[pltpu.VMEM((256, ROWS), BF16)],
        compiler_params=grid_params(),
        cost_estimate=pl.CostEstimate(flops=10**9, bytes_accessed=10 * MIB, transcendentals=10**6),
    )(proj, proj, proj, halo, halo, taps, taps, hp)


def exchange_kernel(
    n, rev, s_ref, d_ref, o_ref, inbox, dbox, parts, decs, total, chain_out, chain_in, outbox,
    send_a, recv_a, send_d, recv_d, send_c, recv_c, send_o, recv_o,
):
    planes = n // PLANE
    section = lax.axis_index("section")
    q = lax.axis_index("seq")
    u = n - 1 - q if rev else q
    spot, level = lax.rem(u, PLANE), u // PLANE

    def device(at):
        return (section, n - 1 - at if rev else at)

    peers = [lax.rem(spot + k, PLANE) for k in range(1, PLANE)]
    barrier = pltpu.get_barrier_semaphore()
    for peer in peers:
        pl.semaphore_signal(barrier, inc=1, device_id=device(level * PLANE + peer), device_id_type=MESH)

    @pl.when(level > 0)
    def _():
        pl.semaphore_signal(barrier, inc=1, device_id=device(u - PLANE), device_id_type=MESH)

    pl.semaphore_wait(barrier, PLANE - 1 + (level < planes - 1).astype(jnp.int32))

    def group(at):
        return pl.ds(pl.multiple_of(at * LANES, LANES), LANES)

    first = []
    for k, peer in enumerate(peers):
        to = device(level * PLANE + peer)
        first.append(
            pltpu.make_async_remote_copy(
                src_ref=d_ref.at[:, group(peer)], dst_ref=dbox.at[spot],
                send_sem=send_d.at[k], recv_sem=recv_d.at[k], device_id=to, device_id_type=MESH,
            )
        )
        first.append(
            pltpu.make_async_remote_copy(
                src_ref=s_ref.at[:, group(peer)], dst_ref=inbox.at[spot],
                send_sem=send_a.at[k], recv_sem=recv_a.at[k], device_id=to, device_id_type=MESH,
            )
        )
    for copy in first:
        copy.start()
    inbox[spot] = s_ref[:, group(spot)]
    dbox[spot] = d_ref[:, group(spot)]
    for copy in first:
        copy.wait()

    cuts = LANES // 256
    for b in range(cuts):
        at = slice(b * 256, b * 256 + 256)
        state = inbox[0, :, at].astype(F32)
        decay = dbox[0, 0:1, at]
        for p in range(1, PLANE):
            parts[p, :, at] = state
            decs[p, 0:1, at] = decay
            d = dbox[p, 0:1, at]
            state = d * state + inbox[p, :, at].astype(F32)
            decay = decay * d
        total[:, at] = state
        decs[0, 0:1, at] = decay

    def chain(b):
        return pltpu.make_async_remote_copy(
            src_ref=chain_out.at[b], dst_ref=chain_in.at[b],
            send_sem=send_c.at[b], recv_sem=recv_c.at[b],
            device_id=device(lax.rem(u + PLANE, n)), device_id_type=MESH,
        )

    last = []
    for b in range(cuts):
        at = slice(b * 256, b * 256 + 256)

        @pl.when(level > 0)
        def _():
            chain(b).wait_recv()

        @pl.when(level == 0)
        def _():
            chain_in[b] = jnp.zeros((128, 256), chain_in.dtype)

        enter = chain_in[b].astype(F32)

        @pl.when(level < planes - 1)
        def _():
            chain_out[b] = (decs[0, 0:1, at] * enter + total[:, at]).astype(chain_out.dtype)
            chain(b).start()

        outbox[0, :, at] = enter.astype(outbox.dtype)
        for p in range(1, PLANE):
            outbox[p, :, at] = (decs[p, 0:1, at] * enter + parts[p, :, at]).astype(outbox.dtype)
        mine = pl.ds(pl.multiple_of(spot * LANES + b * 256, 256), 256)
        o_ref[:, mine] = outbox[spot, :, at]
        for k, peer in enumerate(peers):
            copy = pltpu.make_async_remote_copy(
                src_ref=outbox.at[peer, :, pl.ds(b * 256, 256)], dst_ref=o_ref.at[:, mine],
                send_sem=send_o.at[b * 3 + k], recv_sem=recv_o.at[b * 3 + k],
                device_id=device(level * PLANE + peer), device_id_type=MESH,
            )
            copy.start()
            last.append(copy)
    for copy in last:
        copy.wait()

    @pl.when(level < planes - 1)
    def _():
        for b in range(cuts):
            chain(b).wait_send()


def exchange(state, decay, n, rev):
    vmem = pl.BlockSpec(memory_space=pltpu.VMEM)
    dma = pltpu.SemaphoreType.DMA
    cuts = LANES // 256
    return pl.pallas_call(
        functools.partial(exchange_kernel, n, rev),
        out_shape=sds(128, INNER, state.dtype),
        in_specs=[vmem, vmem],
        out_specs=vmem,
        scratch_shapes=[
            pltpu.VMEM((PLANE, 128, LANES), state.dtype),
            pltpu.VMEM((PLANE, 8, LANES), F32),
            pltpu.VMEM((PLANE, 128, LANES), F32),
            pltpu.VMEM((PLANE, 8, LANES), F32),
            pltpu.VMEM((128, LANES), F32),
            pltpu.VMEM((cuts, 128, 256), state.dtype),
            pltpu.VMEM((cuts, 128, 256), state.dtype),
            pltpu.VMEM((PLANE, 128, LANES), state.dtype),
            dma((3,)), dma((3,)), dma((3,)), dma((3,)),
            dma((cuts,)), dma((cuts,)), dma((3 * cuts,)), dma((3 * cuts,)),
        ],
        compiler_params=pltpu.CompilerParams(
            collective_id=2 if rev else 1, has_side_effects=True, vmem_limit_bytes=32 * MIB
        ),
    )(state, decay)


def decay_block(later, earlier):
    return jnp.exp(jnp.minimum(later - earlier, 0.0))


def head_lanes(parts, i):
    at = (i // 2) * 128
    here = (iota((ROWS, 128), 1) < HEADDIM) if i % 2 == 0 else (iota((ROWS, 128), 1) >= HEADDIM)
    return [jnp.where(here, part[:, at : at + 128], jnp.zeros((), BF16)) for part in parts]


def mix_kernel(
    g_ref, step_ref, cum_ref, cumt_ref, val_ref, gate_ref, c_ref, car_ref, lp_ref, gain_ref,
    y_ref, low_ref, gated_ref, sum_ref,
):
    j = pl.program_id(0)
    heads = expander(j)
    cum = dot_nn(cum_ref[...], heads)
    values = val_ref[...]
    scaled = split2(values * dot_nn(step_ref[...], heads))
    car_high, car_rest = split2(car_ref[...])
    across = dot_nn(c_ref[...], jnp.concatenate([car_high, car_high, car_rest], axis=0))
    y = jnp.exp(cum) * across + lp_ref[0:1, :] * values
    sides = []
    for pair in range(WIDE // 128):
        top = jnp.zeros((HALF, 128), F32)
        bottom = jnp.zeros((HALF, 128), F32)
        for i in (2 * pair, 2 * pair + 1):
            row = cumt_ref[pl.ds((WIDE // HEADDIM) * j + i, 1), :]
            column = cum[:, i * HEADDIM : i * HEADDIM + 1]
            part = head_lanes(scaled, i)
            upper = split2(g_ref[0:HALF, 0:HALF] * decay_block(column[0:HALF], row[:, 0:HALF]))
            top = top + fine(dot_nn, upper, [v[0:HALF] for v in part])
            lower = split2(g_ref[HALF:ROWS, :] * decay_block(column[HALF:ROWS], row))
            bottom = bottom + fine(dot_nn, lower, part)
        sides.append(jnp.concatenate([top, bottom], axis=0))
    y = y + jnp.concatenate(sides, axis=1)
    y_ref[...] = y
    gate = gate_ref[...]
    gated = y * (gate * sigmoid(gate))
    gated_ref[j] = gated

    @pl.when(j == 0)
    def _():
        sum_ref[...] = jnp.zeros_like(sum_ref)

    sum_ref[...] += gated * gated

    @pl.when(j == STEPS - 1)
    def _():
        mean = jnp.sum(sum_ref[...], axis=1, keepdims=True) * (1.0 / INNER)
        scale = lax.rsqrt(mean + EPS)
        for k in range(STEPS):
            at = slice(k * WIDE, k * WIDE + WIDE)
            low_ref[:, at] = (gated_ref[k] * scale * gain_ref[1:2, at]).astype(BF16)


def mix(g, step, cum, cumt, values, proj, c, carried, lp):
    return pl.pallas_call(
        mix_kernel,
        grid=(STEPS,),
        in_specs=[
            whole((ROWS, ROWS)), whole((ROWS, 384)), whole((ROWS, 384)), whole((128, ROWS)),
            lanes(ROWS), lanes(ROWS), whole((ROWS, 384)), lanes(128), lanes(8),
            whole((8, INNER)),
        ],
        out_specs=[lanes(ROWS), whole((ROWS, INNER))],
        out_shape=[sds(ROWS, INNER, F32), sds(ROWS, INNER, BF16)],
        scratch_shapes=[pltpu.VMEM((STEPS, ROWS, WIDE), F32), pltpu.VMEM((ROWS, WIDE), F32)],
        compiler_params=grid_params(),
        cost_estimate=pl.CostEstimate(flops=3 * 10**9, bytes_accessed=14 * MIB, transcendentals=4 * 10**6),
    )(g, step, cum, cumt, values, proj, c, carried, lp, lp)


def gate_back_kernel(
    dg_ref, y_ref, gate_ref, cum_ref, ct_ref, lp_ref, dy_ref, dgate_ref, gain_ref, dcar_ref,
    dg_all, y_all, gate_all, square_acc, cross_acc,
):
    phase, j = pl.program_id(0), pl.program_id(1)

    @pl.when(jnp.logical_and(phase == 0, j == 0))
    def _():
        square_acc[...] = jnp.zeros_like(square_acc)
        cross_acc[...] = jnp.zeros_like(cross_acc)

    @pl.when(phase == 0)
    def _():
        dg, y, gate = dg_ref[...], y_ref[...], gate_ref[...]
        dg_all[j], y_all[j], gate_all[j] = dg, y, gate
        gated = y * (gate * sigmoid(gate))
        square_acc[...] += gated * gated
        cross_acc[...] += dg * lp_ref[1:2, :] * gated

    @pl.when(phase == 1)
    def _():
        r = lax.rsqrt(jnp.sum(square_acc[...], axis=1, keepdims=True) * (1.0 / INNER) + EPS)
        m = jnp.sum(cross_acc[...], axis=1, keepdims=True) * (1.0 / INNER) * r * r
        dg, y, gate = dg_all[j], y_all[j], gate_all[j]
        s = sigmoid(gate)
        silu = gate * s
        gated = y * silu
        gain_ref[...] = jnp.broadcast_to(jnp.sum(dg * gated * r, axis=0, keepdims=True), (8, WIDE))
        d_gated = r * (dg * lp_ref[1:2, :] - gated * m)
        dy = d_gated * silu
        dy_ref[...] = dy
        dgate_ref[...] = (d_gated * y * (s + silu * (1.0 - s))).astype(BF16)
        cum = dot_nn(cum_ref[...], expander(j))
        dcar_ref[...] = dot_nn(ct_ref[...], (dy * jnp.exp(cum)).astype(BF16)).astype(BF16)


def gate_back(dg, y, proj, cum, ct, lp):
    def first(rows):
        return pl.BlockSpec((rows, WIDE), lambda p, j: (0, j * (1 - p) + (STEPS - 1) * p))

    def second(rows):
        return pl.BlockSpec((rows, WIDE), lambda p, j: (0, j * p))

    def both(shape):
        return pl.BlockSpec(shape, lambda p, j: (0, 0))

    kept = pltpu.VMEM((STEPS, ROWS, WIDE), F32)
    return pl.pallas_call(
        gate_back_kernel,
        grid=(2, STEPS),
        in_specs=[
            first(ROWS), first(ROWS), first(ROWS), both((ROWS, 384)), both((128, ROWS)),
            pl.BlockSpec((8, WIDE), lambda p, j: (0, j)),
        ],
        out_specs=[second(ROWS), second(ROWS), second(8), second(128)],
        out_shape=[sds(ROWS, INNER, F32), sds(ROWS, INNER, BF16), sds(8, INNER, F32), sds(128, INNER, BF16)],
        scratch_shapes=[kept, kept, kept, pltpu.VMEM((ROWS, WIDE), F32), pltpu.VMEM((ROWS, WIDE), F32)],
        compiler_params=grid_params(),
        cost_estimate=pl.CostEstimate(flops=10**9, bytes_accessed=16 * MIB, transcendentals=2 * 10**6),
    )(dg, y, proj, cum, ct, lp)


def core_back_kernel(
    x_ref, bc_ref, raw_ref, xh_ref, bch_ref, xw_ref, bcw_ref, hp_ref,
    step_ref, cum_ref, cumt_ref, gt_ref, b_ref, c_ref, y_ref, dy_ref, car_ref, late_ref, lp_ref,
    dx_ref, dbc_ref, tail_ref, tailbc_ref, head_ref, headbc_ref, taps_ref, tapsbc_ref, draw_ref, hg_ref,
    dgt_acc, dc_acc, db_acc, dcum_acc, dstep_acc, rows_acc,
):
    j = pl.program_id(0)

    @pl.when(j == 0)
    def _():
        for acc in (dgt_acc, dc_acc, db_acc, dcum_acc, dstep_acc, rows_acc):
            acc[...] = jnp.zeros_like(acc)

    ext = extended(x_ref[...], xh_ref[...])
    pre = conv_pre(ext, xw_ref[...])
    sig = sigmoid(pre)
    values = pre * sig
    heads, to_heads = expander(j), collector(j)
    step = dot_nn(step_ref[...], heads)
    cum = dot_nn(cum_ref[...], heads)
    last = cum[ROWS - 1 : ROWS]
    scaled = values * step
    scaled_parts = split2(scaled)
    dy = dy_ref[...]
    dy_parts = split2(dy)
    sides = []
    for pair in range(WIDE // 128):
        top = jnp.zeros((HALF, 128), F32)
        bottom = jnp.zeros((HALF, 128), F32)
        at = slice(pair * 128, pair * 128 + 128)
        own = [part[:, at] for part in scaled_parts]
        for i in (2 * pair, 2 * pair + 1):
            row = cumt_ref[pl.ds((WIDE // HEADDIM) * j + i, 1), :]
            column = cum[:, i * HEADDIM : i * HEADDIM + 1]
            part = head_lanes(dy_parts, i)
            decay = decay_block(row, column[0:HALF])
            top = top + fine(dot_nn, split2(gt_ref[0:HALF, :] * decay), part)
            dgt_acc[0:HALF, :] += fine(dot_nt, [v[0:HALF] for v in own], part) * decay
            decay = decay_block(row[:, HALF:ROWS], column[HALF:ROWS])
            late_part = [v[HALF:ROWS] for v in part]
            bottom = bottom + fine(dot_nn, split2(gt_ref[HALF:ROWS, HALF:ROWS] * decay), late_part)
            dgt_acc[HALF:ROWS, HALF:ROWS] += fine(dot_nt, [v[HALF:ROWS] for v in own], late_part) * decay
        sides.append(jnp.concatenate([top, bottom], axis=0))
    car, late = car_ref[...], late_ref[...]
    to_end = jnp.exp(last - cum)
    d_ended = dot_nn(b_ref[:, 0:128], late)
    ended = scaled * to_end
    dc_acc[...] += fine(dot_nt, split2(dy * jnp.exp(cum)), split2(car))
    db_acc[...] += dot_nt(ended.astype(BF16), late)
    d_total = jnp.concatenate(sides, axis=1) + to_end * d_ended
    skip_w = lp_ref[0:1, :]
    dcum_acc[...] += collect(dy * (y_ref[...] - skip_w * values) - scaled * d_total, to_heads)
    dstep_acc[...] += collect(d_total * values, to_heads)
    at_last = jnp.exp(last) * jnp.sum(late.astype(F32) * car, axis=0, keepdims=True)
    at_last = at_last + jnp.sum(ended * d_ended, axis=0, keepdims=True)
    skip = jnp.sum(dy * values, axis=0, keepdims=True)
    rows_acc[...] += collect(jnp.concatenate([at_last, skip, jnp.zeros((6, WIDE), F32)], axis=0), to_heads)
    d_pre = (skip_w * dy + step * d_total) * (sig + values * (1.0 - sig))
    taps_ref[...] = tap_grads(d_pre, ext)
    head_ref[...] = d_pre[0:8]
    d_conv = conv_back(d_pre, xw_ref[...])
    dx_ref[...] = d_conv.astype(BF16)
    tail_ref[...] = d_conv[ROWS - 8 : ROWS]

    @pl.when(j == STEPS - 1)
    def _():
        seen = iota((ROWS, ROWS), 1) >= iota((ROWS, ROWS), 0)
        d_gt = split2(jnp.where(seen, dgt_acc[...], 0.0))
        d_c = dc_acc[...] + fine(dot_tn, d_gt, halves(b_ref))
        d_b = db_acc[...] + fine(dot_nn, d_gt, halves(c_ref))
        ext_bc = extended(bc_ref[...], bch_ref[...])
        pre_bc = conv_pre(ext_bc, bcw_ref[...])
        sig_bc = sigmoid(pre_bc)
        d_pre_bc = jnp.concatenate([d_b, d_c], axis=1) * (sig_bc + pre_bc * sig_bc * (1.0 - sig_bc))
        tapsbc_ref[...] = tap_grads(d_pre_bc, ext_bc)
        headbc_ref[...] = d_pre_bc[0:8]
        d_conv_bc = conv_back(d_pre_bc, bcw_ref[...])
        dbc_ref[...] = d_conv_bc.astype(BF16)
        tailbc_ref[...] = d_conv_bc[ROWS - 8 : ROWS]
        raw, step_all, rate = step_parts(raw_ref, hp_ref)
        end = iota((ROWS, 128), 0) == ROWS - 1
        d_cum_all = dcum_acc[...] + jnp.where(end, rows_acc[0:1, :], 0.0)
        d_log = exact_left(triangle(False), d_cum_all)
        d_step = dstep_acc[...] + rate * d_log
        d_raw = jnp.where(iota((ROWS, 128), 1) < HEADS, d_step * sigmoid(raw), 0.0)
        draw_ref[...] = d_raw.astype(BF16)
        hg_ref[...] = jnp.concatenate(
            [
                jnp.sum(d_raw, axis=0, keepdims=True),
                jnp.sum(d_log * rate * step_all, axis=0, keepdims=True),
                rows_acc[1:2, :],
                jnp.zeros((5, 128), F32),
            ],
            axis=0,
        )


def core_back(proj, halo, taps, hp, step, cum, cumt, gt, b, c, y, dy, carried, late, lp):
    acc = pltpu.VMEM((ROWS, 128), F32)
    return pl.pallas_call(
        core_back_kernel,
        grid=(STEPS,),
        in_specs=[
            lanes(ROWS, STEPS), fixed(ROWS, 2 * STEPS), fixed(ROWS, 50, 128),
            lanes(8), fixed(8, STEPS), lanes(8), fixed(8, STEPS), whole((8, 128)),
            whole((ROWS, 384)), whole((ROWS, 384)), whole((128, ROWS)), whole((ROWS, ROWS)),
            whole((ROWS, 256)), whole((ROWS, 384)),
            lanes(ROWS), lanes(ROWS), lanes(128), lanes(128), lanes(8),
        ],
        out_specs=[
            lanes(ROWS), whole((ROWS, 256)), lanes(8), whole((8, 256)), lanes(8), whole((8, 256)),
            lanes(8), whole((8, 256)), whole((ROWS, 128)), whole((8, 128)),
        ],
        out_shape=[
            sds(ROWS, INNER, BF16), sds(ROWS, 256, BF16), sds(8, INNER, F32), sds(8, 256, F32),
            sds(8, INNER, F32), sds(8, 256, F32), sds(8, INNER, F32), sds(8, 256, F32),
            sds(ROWS, 128, BF16), sds(8, 128, F32),
        ],
        scratch_shapes=[pltpu.VMEM((ROWS, ROWS), F32), acc, acc, acc, acc, pltpu.VMEM((8, 128), F32)],
        compiler_params=grid_params(),
        cost_estimate=pl.CostEstimate(flops=8 * 10**9, bytes_accessed=14 * MIB, transcendentals=5 * 10**6),
    )(
        proj, proj, proj, halo, halo, taps, taps, hp,
        step, cum, cumt, gt, b, c, y, dy, carried, late, lp,
    )


def settle_kernel(
    n, ga0, re0, ga1, re1, ow0, ow1, a0, a1, d0, d1, gin_ref, gout_ref, acts_ref, grads_ref,
    gate_in, rest_in, out_in, send_g, recv_g, send_r, recv_r, send_o, recv_o, send_x, recv_x, keep_x,
):
    core = lax.axis_index("section")
    q = lax.axis_index("seq")
    spot = lax.rem(q, PLANE)
    base = q - spot
    rows = gin_ref.shape[0]
    barrier = pltpu.get_barrier_semaphore()
    for k in range(PLANE):
        for flip in range(2):
            if k or flip:
                to = (core ^ flip, base + lax.rem(spot + k, PLANE))
                pl.semaphore_signal(barrier, inc=1, device_id=to, device_id_type=MESH)
    pl.semaphore_wait(barrier, 2 * PLANE - 1)

    def run(layer, gate, rest, outw, act, grad, away_act, away_grad, away_outw, away_gate, away_rest):
        copies = []

        def send(src, dst, sems, at, to):
            copy = pltpu.make_async_remote_copy(
                src_ref=src, dst_ref=dst, send_sem=sems[0].at[at], recv_sem=sems[1].at[at],
                device_id=to, device_id_type=MESH,
            )
            copy.start()
            copies.append(copy)

        across = (1 - layer, q)
        kept = []
        for at, (own, away, dst) in enumerate(((grad, away_grad, grads_ref), (act, away_act, acts_ref))):
            send(away, dst.at[layer], (send_x, recv_x), at, across)
            kept.append(pltpu.make_async_copy(own, dst.at[layer], keep_x.at[at]))
            kept[-1].start()
        send(away_outw, out_in, (send_o, recv_o), 0, across)
        for k in range(PLANE):
            peer = lax.rem(spot + k, PLANE)
            block = pl.ds(pl.multiple_of(peer * rows, rows), rows)
            for flip in range(2):
                if not (k or flip):
                    continue
                at = 2 * k + flip
                to = (1 - layer if flip else layer, base + peer)
                slot = 2 * spot + layer
                send((away_gate if flip else gate).at[block], gate_in.at[slot], (send_g, recv_g), at, to)
                send((away_rest if flip else rest).at[block], rest_in.at[slot], (send_r, recv_r), at, to)
        mine = pl.ds(pl.multiple_of(spot * rows, rows), rows)
        gate_in[2 * spot + layer] = gate[mine, :]
        rest_in[2 * spot + layer] = rest[mine, :]
        half = D // 2
        gout_ref[:, layer * half : layer * half + half] = outw[...].astype(F32)
        for copy in copies + kept:
            copy.wait()
        gout_ref[:, (1 - layer) * half : (1 - layer) * half + half] = out_in[...].astype(F32)

    @pl.when(core == 0)
    def _():
        run(0, ga0, re0, ow0, a0, d0, a1, d1, ow1, ga1, re1)

    @pl.when(core == 1)
    def _():
        run(1, ga1, re1, ow1, a1, d1, a0, d0, ow0, ga0, re0)

    for p in range(2 * PLANE):
        wide = gate_in.shape[2]
        gin_ref[:, p * wide : p * wide + wide] = gate_in[p].astype(F32)
        wide = rest_in.shape[2]
        at = INNER + p * wide
        width = min(wide, PROJ - at)
        gin_ref[:, at : at + width] = rest_in[p].astype(F32)[:, :width]


def settle(gates, rests, outs, acts, grads, n):
    vmem = pl.BlockSpec(memory_space=pltpu.VMEM)
    anywhere = pl.BlockSpec(memory_space=pl.ANY)
    dma = pltpu.SemaphoreType.DMA
    rows = D // n
    eight = 2 * PLANE
    return pl.pallas_call(
        functools.partial(settle_kernel, n),
        out_shape=[
            sds(rows, PROJ, F32), sds(INNER // n, D, F32),
            jax.ShapeDtypeStruct((2, ROWS, D), BF16), jax.ShapeDtypeStruct((2, ROWS, D), F32),
        ],
        in_specs=[vmem] * 6 + [anywhere] * 4,
        out_specs=[vmem, vmem, anywhere, anywhere],
        scratch_shapes=[
            pltpu.VMEM((eight, rows, gates[0].shape[1]), BF16),
            pltpu.VMEM((eight, rows, rests[0].shape[1]), BF16),
            pltpu.VMEM((INNER // n, D // 2), BF16),
            dma((eight,)), dma((eight,)), dma((eight,)), dma((eight,)),
            dma((1,)), dma((1,)), dma((2,)), dma((2,)), dma((2,)),
        ],
        compiler_params=pltpu.CompilerParams(collective_id=3, has_side_effects=True, vmem_limit_bytes=40 * MIB),
    )(gates[0], rests[0], gates[1], rests[1], outs[0], outs[1], acts[0], acts[1], grads[0], grads[1])


def swap(value):
    return lax.ppermute(value, "section", [(0, 1), (1, 0)])


def shifted(value, distance, n):
    return lax.ppermute(value, "seq", [(i, i + distance) for i in range(n) if 0 <= i + distance < n])


def plane_route(k, n):
    return [(i, i - i % PLANE + (i + k) % PLANE) for i in range(n)]


def rms(value):
    return lax.rsqrt(jnp.mean(value * value, axis=-1, keepdims=True) + EPS)


def tied(value, *others):
    return lax.optimization_barrier((value, *others))[0]


def tied_list(values, other):
    return list(lax.optimization_barrier((*values, other))[:-1])


def copies_of(value, n):
    return [value] + [lax.ppermute(value, "seq", plane_route(k, n)) for k in range(1, PLANE)]


def pieces_of(value, n):
    spot = lax.axis_index("seq") % PLANE
    width = value.shape[1] // PLANE
    got = [lax.dynamic_slice_in_dim(value, spot * width, width, 1)]
    for k in range(1, PLANE):
        part = lax.dynamic_slice_in_dim(value, (spot + k) % PLANE * width, width, 1)
        got.append(lax.ppermute(part, "seq", plane_route(k, n)))
    return got


def partial_grad(left, right):
    core = lax.axis_index("section")
    left, right = jnp.concatenate(left, axis=0), jnp.concatenate(right, axis=0)
    half = right.shape[1] // 2
    away = dot_tn(left, lax.dynamic_slice_in_dim(right, (1 - core) * half, half, 1)).astype(BF16)
    mine = dot_tn(left, lax.dynamic_slice_in_dim(right, core * half, half, 1))
    return (mine + swap(away).astype(F32)).astype(BF16)


def plane_rows(partial, n):
    columns = [[p + PLANE * z for z in range(n // PLANE)] for p in range(PLANE)]
    return lax.psum_scatter(partial, "seq", scatter_dimension=0, axis_index_groups=columns, tiled=True)


SIZES = [D, CONVD * CONV, CONVD, HEADS, HEADS, HEADS, INNER]


def split_small(flat):
    parts, at = [], 0
    for size in SIZES:
        parts.append(flat[at : at + size])
        at += size
    return parts


def unpack_params(flat):
    norm_g, conv_w, conv_b, dt_b, a_lg, skip_w, gate_g = split_small(flat)
    taps = jnp.concatenate(
        [conv_w.reshape(CONV, CONVD), conv_b[None], jnp.zeros((3, CONVD), F32)], axis=0
    )
    pad = jnp.zeros((128 - HEADS,), F32)
    hp = jnp.concatenate([dt_b, pad, a_lg, pad, jnp.zeros((6 * 128,), F32)]).reshape(8, 128)
    lp = jnp.concatenate(
        [jnp.repeat(skip_w, HEADDIM)[None], gate_g[None], jnp.zeros((6, INNER), F32)], axis=0
    )
    return norm_g, taps, hp, lp


def per_device(
    inputs, cotangent, norm_gain, in_weight, conv_weight, conv_bias, dt_bias, a_log, d_skip,
    gate_norm_gain, out_weight,
):
    n = lax.axis_size("seq")
    planes = n // PLANE
    core = lax.axis_index("section")
    place = lax.axis_index("seq")
    first = core == 0
    own_in, own_out = in_weight[0].T, out_weight[0]
    other_in, other_out = swap(own_in), swap(own_out)
    own_small = jnp.concatenate(
        [
            norm_gain[0], conv_weight[0].T.reshape(-1), conv_bias[0], dt_bias[0], a_log[0], d_skip[0],
            gate_norm_gain[0],
        ]
    )
    other_small = swap(own_small)
    flags = [(core == layer).astype(jnp.int32)[None] for layer in range(2)]
    params = [
        unpack_params(jnp.where(first, own_small, other_small)),
        unpack_params(jnp.where(first, other_small, own_small)),
    ]

    def mine(pair):
        return lax.dynamic_index_in_dim(pair, core, 0, keepdims=False)

    def project(layer, h):
        normed = (h * rms(h) * params[layer][0]).astype(BF16)
        return normed, mm(normed, own_in, other_in, flags[layer], True, 1664)

    def blocks(layer, proj):
        _, taps, hp, _ = params[layer]
        halo = shifted(proj[ROWS - 8 :, INNER : INNER + CONVD], 1, n)
        return halo, front(proj, halo, taps, hp)

    def finish(layer, h, proj, parts, carried):
        values, _, _, step, cum, cumt, _, c, _, g, _ = parts
        y, gated_low = mix(g, step, cum, cumt, values, proj, c, carried, params[layer][3])
        return y, gated_low, h + mm(gated_low, own_out, other_out, flags[layer], False, 768)

    def by_owner(gated_low):
        width = INNER // n
        return gated_low.reshape(ROWS, planes, PLANE, width).transpose(0, 2, 1, 3).reshape(ROWS, INNER)

    d_out_1 = mine(cotangent)
    lows_1 = copies_of(d_out_1, n)
    h_0 = mine(inputs).astype(F32)
    normed_0, proj_0 = project(0, h_0)
    proj_0 = tied(proj_0, *lows_1)
    halo_0, parts_0 = blocks(0, proj_0)
    carried_0 = exchange(parts_0[1], parts_0[2], n, False)
    normeds_0 = copies_of(tied(normed_0, carried_0), n)
    y_0, gated_0, out_0 = finish(0, h_0, proj_0, parts_0, carried_0)
    act_0 = out_0.astype(BF16)

    h_1 = act_0.astype(F32)
    normed_1, proj_1 = project(1, h_1)
    proj_1 = tied(proj_1, *normeds_0)
    halo_1, parts_1 = blocks(1, proj_1)
    gateds_0 = pieces_of(by_owner(tied(gated_0, halo_1)), n)
    carried_1 = exchange(tied(parts_1[1], *gateds_0), parts_1[2], n, False)
    normeds_1 = copies_of(tied(normed_1, carried_1), n)
    y_1, gated_1, out_1 = finish(1, h_1, proj_1, parts_1, carried_1)
    act_1 = out_1.astype(BF16)

    def gate_side(layer, d_low, y, proj, parts):
        d_gated_low = mm(d_low, own_out, other_out, flags[layer], True, 1024)
        return gate_back(d_gated_low, y, proj, parts[4], parts[8], params[layer][3])

    def core_side(layer, proj, halo, parts, y, dy, carried, late):
        _, taps, hp, lp = params[layer]
        _, _, _, step, cum, cumt, b, c, _, _, gt = parts
        return core_back(proj, halo, taps, hp, step, cum, cumt, gt, b, c, y, dy, carried, late, lp)

    def conv_side(layer, back):
        dx, dbc, tail, tailbc, head, headbc, gtaps, gtapsbc, d_raw, heads = back
        w = params[layer][1]
        a = shifted(jnp.concatenate([head, headbc], axis=1), -1, n)
        fix = jnp.concatenate(
            [
                jnp.zeros((5, CONVD), F32),
                w[0:1] * a[0:1],
                w[0:1] * a[1:2] + w[1:2] * a[0:1],
                w[0:1] * a[2:3] + w[1:2] * a[1:2] + w[2:3] * a[0:1],
            ],
            axis=0,
        )
        low = (jnp.concatenate([tail, tailbc], axis=1) + fix).astype(BF16)
        main = jnp.concatenate([dx[: ROWS - 8], dbc[: ROWS - 8]], axis=1)
        d_conv = jnp.concatenate([main, low], axis=0)
        return d_conv, d_raw[:, :HEADS]

    def norm_side(layer, h, d_out, d_proj):
        norm_g = params[layer][0]
        d_normed = mm(d_proj, own_in, other_in, flags[layer], False, 512)
        r = rms(h)
        v = d_normed * norm_g
        d_h = d_out + r * (v - h * (r * r * jnp.mean(v * h, axis=-1, keepdims=True)))
        return d_h, jnp.sum(d_normed * h * r, axis=0)

    def small_of(norm_gain_grad, back, gate_gain):
        taps_all = jnp.concatenate([back[6], back[7]], axis=1)
        heads = back[9]
        return jnp.concatenate(
            [
                norm_gain_grad, taps_all[:CONV].reshape(-1), taps_all[CONV],
                heads[0, :HEADS], heads[1, :HEADS], heads[2, :HEADS], gate_gain[0],
            ]
        )

    def padded(d_conv, d_raw):
        pad = jnp.zeros((ROWS, REST - CONVD - HEADS), BF16)
        return jnp.concatenate([d_conv, d_raw, pad], axis=1)

    dy_1, d_gate_1, gain_1, d_carried_1 = gate_side(1, d_out_1, y_1, proj_1, parts_1)
    late_1 = exchange(tied(d_carried_1, *normeds_1), parts_1[2], n, True)
    gates_1 = pieces_of(tied(d_gate_1, late_1), n)
    gateds_1 = pieces_of(by_owner(tied(gated_1, late_1)), n)
    back_1 = core_side(1, proj_1, halo_1, parts_1, y_1, dy_1, carried_1, late_1)
    outw_1 = partial_grad(tied_list(gateds_1, back_1[0]), lows_1)
    outw_1 = plane_rows(outw_1, n)
    gatew_1 = partial_grad(normeds_1, tied_list(gates_1, back_1[0]))
    d_conv_1, d_raw_1 = conv_side(1, back_1)
    rests_1 = pieces_of(padded(d_conv_1, d_raw_1), n)
    d_proj_1 = jnp.concatenate([tied(d_gate_1, gatew_1), d_conv_1, d_raw_1], axis=1)
    gatew_1 = plane_rows(gatew_1, n)
    d_1, ng_1 = norm_side(1, h_1, d_out_1.astype(F32), d_proj_1)

    d_out_0 = d_1.astype(BF16)
    lows_0 = copies_of(tied(d_out_0, *rests_1), n)
    dy_0, d_gate_0, gain_0, d_carried_0 = gate_side(0, d_out_0, y_0, proj_0, parts_0)
    restw_1 = partial_grad(normeds_1, rests_1)
    late_0 = exchange(tied(d_carried_0, restw_1), parts_0[2], n, True)
    restw_1 = plane_rows(restw_1, n)
    gates_0 = pieces_of(tied(d_gate_0, late_0, *lows_0), n)
    outw_0 = partial_grad(gateds_0, tied_list(lows_0, late_0))
    back_0 = core_side(0, proj_0, halo_0, parts_0, y_0, dy_0, carried_0, tied(late_0, outw_0))
    outw_0 = plane_rows(outw_0, n)
    gatew_0 = partial_grad(normeds_0, tied_list(gates_0, back_0[0]))
    d_conv_0, d_raw_0 = conv_side(0, back_0)
    rests_0 = pieces_of(padded(d_conv_0, d_raw_0), n)
    d_proj_0 = jnp.concatenate([tied(d_gate_0, gatew_0), d_conv_0, d_raw_0], axis=1)
    gatew_0 = plane_rows(gatew_0, n)
    d_0, ng_0 = norm_side(0, h_0, d_out_0.astype(F32), d_proj_0)
    restw_0 = plane_rows(partial_grad(normeds_0, rests_0), n)

    g_in, g_out, acts, input_grads = settle(
        (gatew_0, gatew_1), (restw_0, restw_1), (outw_0, outw_1), (act_0, act_1), (d_0, d_1), n
    )
    small_0, small_1 = small_of(ng_0, back_0, gain_0), small_of(ng_1, back_1, gain_1)
    small = jnp.where(first, small_0, small_1) + swap(jnp.where(first, small_1, small_0))
    reach = 1
    while reach < n:
        small = small + lax.ppermute(small, "seq", [(i, i ^ reach) for i in range(n)])
        reach *= 2
    norm_g, conv_w, conv_b, dt_b, a_lg, skip_w, gate_g = split_small(small)

    def share(value):
        rows = value.shape[0] // n
        return lax.dynamic_slice_in_dim(value, place * rows, rows, 0)[None]

    conv_rows = CONVD // n
    conv_w = lax.dynamic_slice_in_dim(conv_w.reshape(CONV, CONVD), place * conv_rows, conv_rows, 1).T
    return (
        acts[None], input_grads[None], share(norm_g), g_in[None], conv_w[None], share(conv_b),
        dt_b[None], a_lg[None], skip_w[None], share(gate_g), g_out[None],
    )


def solution(mesh):
    in_specs = (
        P(None, "seq", None), P(None, "seq", None), P("section", None), P("section", None, None),
        P("section", None, None), P("section", None), P("section", None), P("section", None),
        P("section", None), P("section", None), P("section", None, None),
    )
    out_specs = (
        P("section", None, "seq", None), P("section", None, "seq", None), P("section", "seq"),
        P("section", "seq", None), P("section", "seq", None), P("section", "seq"), P("section", None),
        P("section", None), P("section", None), P("section", "seq"), P("section", "seq", None),
    )
    return jax.shard_map(per_device, mesh=mesh, in_specs=in_specs, out_specs=out_specs, check_vma=False)
```

```python
import functools

import jax
import jax.numpy as jnp
from jax import lax
from jax.experimental import pallas as pl
from jax.experimental.pallas import tpu as pltpu
from jax.sharding import PartitionSpec as P

D = 1536
INNER = 3072
STATE = 128
HEADS = 48
HEADDIM = 64
CONV = 4
CONVD = 3328
PROJ = 6448
ROWS = 256
WIDE = 256
STEPS = INNER // WIDE
HALF = ROWS // 2
PLANE = 4
LANES = INNER // PLANE
REST = 3584
EPS = 1e-05
MIB = 2**20
MESH = pl.DeviceIdType.MESH
F32 = jnp.float32
BF16 = jnp.bfloat16


def dot_nn(a, b):
    return lax.dot_general(a, b, (((1,), (0,)), ((), ())), preferred_element_type=F32)


def dot_tn(a, b):
    return lax.dot_general(a, b, (((0,), (0,)), ((), ())), preferred_element_type=F32)


def dot_nt(a, b):
    return lax.dot_general(a, b, (((1,), (1,)), ((), ())), preferred_element_type=F32)


def split3(v):
    high = v.astype(BF16)
    rest = v - high.astype(F32)
    mid = rest.astype(BF16)
    return high, mid, (rest - mid.astype(F32)).astype(BF16)


def split2(v):
    high = v.astype(BF16)
    return high, (v - high.astype(F32)).astype(BF16)


def fine(dot, a, b):
    return dot(a[0], b[0]) + (dot(a[0], b[1]) + dot(a[1], b[0]))


def halves(ref):
    return ref[:, 0:128], ref[:, 128:256]


def parts3(v):
    return jnp.concatenate(split3(v), axis=1)


def exact_left(ones, v):
    a, b, c = split3(v)
    return dot_nn(ones, a) + (dot_nn(ones, b) + dot_nn(ones, c))


def iota(shape, dim):
    return lax.broadcasted_iota(jnp.int32, shape, dim)


def expander(step):
    head_of = (WIDE // HEADDIM) * step + lax.shift_right_logical(iota((128, WIDE), 1), 6)
    ones = (iota((128, WIDE), 0) == head_of).astype(F32).astype(BF16)
    return jnp.concatenate([ones, ones, ones], axis=0)


def collector(step):
    head_of = (WIDE // HEADDIM) * step + lax.shift_right_logical(iota((WIDE, 128), 0), 6)
    return (iota((WIDE, 128), 1) == head_of).astype(F32).astype(BF16)


def collect(v, ones):
    a, b, c = split3(v)
    return dot_nn(a, ones) + (dot_nn(b, ones) + dot_nn(c, ones))


def triangle(lower):
    rows, cols = iota((ROWS, ROWS), 0), iota((ROWS, ROWS), 1)
    return ((rows >= cols) if lower else (rows <= cols)).astype(F32).astype(BF16)


def sigmoid(v):
    return 0.5 * jnp.tanh(0.5 * v) + 0.5


def extended(block, halo):
    return jnp.concatenate([halo, block], axis=0)


def conv_pre(ext, taps):
    out = taps[4:5] + taps[0:1] * ext[5 : 5 + ROWS]
    for k in range(1, CONV):
        out = out + taps[k : k + 1] * ext[5 + k : 5 + k + ROWS]
    return out


def conv_back(d_pre, taps):
    ext = jnp.concatenate([d_pre, jnp.zeros((8, d_pre.shape[1]), F32)], axis=0)
    out = taps[3:4] * d_pre
    for k in range(CONV - 1):
        out = out + taps[k : k + 1] * ext[3 - k : 3 - k + ROWS]
    return out


def tap_grads(d_pre, ext):
    rows = [jnp.sum(d_pre * ext[5 + k : 5 + k + ROWS], axis=0, keepdims=True) for k in range(CONV)]
    rows.append(jnp.sum(d_pre, axis=0, keepdims=True))
    rows.append(jnp.zeros((3, d_pre.shape[1]), F32))
    return jnp.concatenate(rows, axis=0)


def step_parts(raw_ref, hp_ref):
    real = iota((ROWS, 128), 1) < HEADS
    raw = jnp.where(real, raw_ref[...], 0.0) + hp_ref[0:1, :]
    step = jnp.maximum(raw, 0.0) + jnp.log1p(jnp.exp(-jnp.abs(raw)))
    step = jnp.where(real, step, 0.0)
    rate = jnp.where(real[0:1], -jnp.exp(hp_ref[1:2, :]), 0.0)
    return raw, step, rate


def mm_kernel(flag_ref, x_ref, own_ref, other_ref, o_ref, *, nt):
    dot = dot_nt if nt else dot_nn

    @pl.when(flag_ref[0] == 1)
    def _():
        o_ref[...] = dot(x_ref[...], own_ref[...])

    @pl.when(flag_ref[0] == 0)
    def _():
        o_ref[...] = dot(x_ref[...], other_ref[...])


def mm(x, own, other, flag, nt, tile):
    rows, depth = x.shape
    width = own.shape[0] if nt else own.shape[1]
    block = (tile, depth) if nt else (depth, tile)

    def place(j, keep):
        return (j * keep, 0) if nt else (0, j * keep)

    return pl.pallas_call(
        functools.partial(mm_kernel, nt=nt),
        grid_spec=pltpu.PrefetchScalarGridSpec(
            num_scalar_prefetch=1,
            grid=(pl.cdiv(width, tile),),
            in_specs=[
                pl.BlockSpec((rows, depth), lambda j, f: (0, 0)),
                pl.BlockSpec(block, lambda j, f: place(j, f[0])),
                pl.BlockSpec(block, lambda j, f: place(j, 1 - f[0])),
            ],
            out_specs=pl.BlockSpec((rows, tile), lambda j, f: (0, j)),
        ),
        out_shape=jax.ShapeDtypeStruct((rows, width), F32),
        compiler_params=pltpu.CompilerParams(vmem_limit_bytes=48 * MIB),
        cost_estimate=pl.CostEstimate(
            flops=2 * rows * depth * width, bytes_accessed=2 * depth * width, transcendentals=0
        ),
    )(flag, x, own, other)


def spread_copies(pairs, sems):
    send, recv, keep = sems
    section, q = lax.axis_index("section"), lax.axis_index("seq")
    spot = lax.rem(q, PLANE)
    base = q - spot
    away, own = [], []
    for at, (src, dst) in enumerate(pairs):
        width = dst.shape[2]
        for k in range(PLANE):
            peer = lax.rem(spot + k, PLANE)
            part = src.at[:, pl.ds(pl.multiple_of(peer * width, 128), width)]
            if k:
                away.append(
                    pltpu.make_async_remote_copy(
                        src_ref=part, dst_ref=dst.at[k], send_sem=send.at[3 * at + k - 1],
                        recv_sem=recv.at[3 * at + k - 1], device_id=(section, base + peer), device_id_type=MESH,
                    )
                )
            else:
                own.append(pltpu.make_async_copy(part, dst.at[0], keep.at[at]))
    return away, own


def spread_start(pairs, sems):
    section, q = lax.axis_index("section"), lax.axis_index("seq")
    spot = lax.rem(q, PLANE)
    barrier = pltpu.get_barrier_semaphore()
    for k in range(1, PLANE):
        peer = q - spot + lax.rem(spot + k, PLANE)
        pl.semaphore_signal(barrier, inc=1, device_id=(section, peer), device_id_type=MESH)
    pl.semaphore_wait(barrier, PLANE - 1)
    away, own = spread_copies(pairs, sems)
    for copy in away + own:
        copy.start()


def spread_wait(pairs, sems):
    away, own = spread_copies(pairs, sems)
    for copy in away + own:
        copy.wait()


def spread_specs(sources):
    anywhere = pl.BlockSpec(memory_space=pl.ANY)
    shapes = [jax.ShapeDtypeStruct((PLANE, v.shape[0], v.shape[1] // PLANE), v.dtype) for v in sources]
    dma = pltpu.SemaphoreType.DMA
    sems = [dma((3 * len(sources),)), dma((3 * len(sources),)), dma((len(sources),))] if sources else []
    return [anywhere] * len(sources), shapes, sems


def spreading(body, n_in, n_out, count, first, last):
    if not count:
        return body

    def kernel(*refs):
        ins, rest = refs[: n_in + count], refs[n_in + count :]
        outs, scratch = rest[: n_out + count], rest[n_out + count :]
        pairs = list(zip(ins[n_in:], outs[n_out:]))
        sems = scratch[-3:]

        @pl.when(first())
        def _():
            spread_start(pairs, sems)

        body(*ins[:n_in], *outs[:n_out], *scratch[:-3])

        @pl.when(last())
        def _():
            spread_wait(pairs, sems)

    return kernel


def call_params(collective_id):
    if collective_id is None:
        return grid_params()
    return pltpu.CompilerParams(
        vmem_limit_bytes=48 * MIB, collective_id=collective_id, has_side_effects=True
    )


def project_kernel(flag_ref, x_ref, before_ref, own_ref, other_ref, o_ref, halo_ref):
    def product(w_ref):
        o_ref[...] = dot_nt(x_ref[...], w_ref[...])
        halo_ref[...] = dot_nt(before_ref[...], w_ref[...])

    @pl.when(flag_ref[0] == 1)
    def _():
        product(own_ref)

    @pl.when(flag_ref[0] == 0)
    def _():
        product(other_ref)


def project_mm(x, before, own, other, flag, tile):
    rows, depth = x.shape
    width = own.shape[0]
    return pl.pallas_call(
        project_kernel,
        grid_spec=pltpu.PrefetchScalarGridSpec(
            num_scalar_prefetch=1,
            grid=(pl.cdiv(width, tile),),
            in_specs=[
                pl.BlockSpec((rows, depth), lambda j, f: (0, 0)),
                pl.BlockSpec((16, depth), lambda j, f: (0, 0)),
                pl.BlockSpec((tile, depth), lambda j, f: (j * f[0], 0)),
                pl.BlockSpec((tile, depth), lambda j, f: (j * (1 - f[0]), 0)),
            ],
            out_specs=[
                pl.BlockSpec((rows, tile), lambda j, f: (0, j)),
                pl.BlockSpec((16, tile), lambda j, f: (0, j)),
            ],
        ),
        out_shape=[sds(rows, width, F32), sds(16, width, F32)],
        compiler_params=pltpu.CompilerParams(vmem_limit_bytes=48 * MIB),
        cost_estimate=pl.CostEstimate(
            flops=2 * rows * depth * width, bytes_accessed=2 * depth * width, transcendentals=0
        ),
    )(flag, x, before, own, other)


def back_kernel(flag_ref, gate_ref, rest_ref, own_ref, other_ref, o_ref):
    def product(w_ref):
        o_ref[...] = dot_nn(gate_ref[...], w_ref[0:INNER, :]) + dot_nn(
            rest_ref[:, 0 : PROJ - INNER], w_ref[INNER:PROJ, :]
        )

    @pl.when(flag_ref[0] == 1)
    def _():
        product(own_ref)

    @pl.when(flag_ref[0] == 0)
    def _():
        product(other_ref)


def back_mm(gate, rest, own, other, flag, tile):
    return pl.pallas_call(
        back_kernel,
        grid_spec=pltpu.PrefetchScalarGridSpec(
            num_scalar_prefetch=1,
            grid=(D // tile,),
            in_specs=[
                pl.BlockSpec((ROWS, INNER), lambda j, f: (0, 0)),
                pl.BlockSpec((ROWS, REST), lambda j, f: (0, 0)),
                pl.BlockSpec((PROJ, tile), lambda j, f: (0, j * f[0])),
                pl.BlockSpec((PROJ, tile), lambda j, f: (0, j * (1 - f[0]))),
            ],
            out_specs=pl.BlockSpec((ROWS, tile), lambda j, f: (0, j)),
        ),
        out_shape=sds(ROWS, D, F32),
        compiler_params=pltpu.CompilerParams(vmem_limit_bytes=48 * MIB),
        cost_estimate=pl.CostEstimate(
            flops=2 * ROWS * D * PROJ, bytes_accessed=2 * D * PROJ, transcendentals=0
        ),
    )(flag, gate, rest, own, other)


def front_kernel(
    x_ref, bc_ref, raw_ref, xh_ref, bch_ref, xw_ref, bcw_ref, hp_ref,
    val_ref, state_ref, dec_ref, step_ref, cum_ref, cumt_ref, b_ref, c_ref, ct_ref, g_ref, gt_ref, bt_ref,
):
    j = pl.program_id(0)

    @pl.when(j == 0)
    def _():
        _, step, rate = step_parts(raw_ref, hp_ref)
        step_ref[...] = parts3(step)
        cum = exact_left(triangle(True), rate * step)
        cum_ref[...] = parts3(cum)
        cumt_ref[...] = cum.T
        pre = conv_pre(extended(bc_ref[...], bch_ref[...]), bcw_ref[...])
        both = pre * sigmoid(pre)
        b, c = both[:, 0:128], both[:, 128:256]
        b_low, c_low = split2(b), split2(c)
        b_ref[...] = jnp.concatenate(b_low, axis=1)
        c_ref[...] = jnp.concatenate([c_low[0], c_low[1], c_low[0]], axis=1)
        ct_ref[...] = c.T.astype(BF16)
        bt_ref[...] = jnp.concatenate(split2(b.T), axis=0)
        seen = iota((ROWS, ROWS), 0) >= iota((ROWS, ROWS), 1)
        g = jnp.where(seen, fine(dot_nt, c_low, b_low), 0.0)
        g_ref[...] = g
        gt_ref[...] = g.T

    pre = conv_pre(extended(x_ref[...], xh_ref[...]), xw_ref[...])
    values = pre * sigmoid(pre)
    val_ref[...] = values
    heads = expander(j)
    cum = dot_nn(cum_ref[...], heads)
    last = cum[ROWS - 1 : ROWS]
    high, rest = split2(values * dot_nn(step_ref[...], heads) * jnp.exp(last - cum))
    twice = dot_nn(bt_ref[...], high)
    state_ref[...] = twice[0:128] + twice[128:256] + dot_nn(bt_ref[0:128, :], rest)
    dec_ref[...] = jnp.broadcast_to(jnp.exp(last), (8, WIDE))


def whole(shape):
    return pl.BlockSpec(shape, lambda j: (0, 0))


def lanes(rows, first=0):
    return pl.BlockSpec((rows, WIDE), lambda j: (0, first + j))


def fixed(rows, at, width=WIDE):
    return pl.BlockSpec((rows, width), lambda j: (0, at))


def sds(rows, cols, dtype):
    return jax.ShapeDtypeStruct((rows, cols), dtype)


def grid_params():
    return pltpu.CompilerParams(vmem_limit_bytes=48 * MIB)


def front(proj, halo, taps, hp, sources=(), collective_id=None):
    square = (ROWS, ROWS)
    specs, shapes, sems = spread_specs(sources)
    body = spreading(
        front_kernel, 8, 11, len(sources), lambda: pl.program_id(0) == 0, lambda: pl.program_id(0) == STEPS - 1
    )
    return pl.pallas_call(
        body,
        grid=(STEPS,),
        in_specs=[
            lanes(ROWS, STEPS), fixed(ROWS, 2 * STEPS), fixed(ROWS, 50, 128),
            lanes(8), fixed(8, STEPS), lanes(8), fixed(8, STEPS), whole((8, 128)), *specs,
        ],
        out_specs=[
            lanes(ROWS), lanes(128), lanes(8),
            whole((ROWS, 384)), whole((ROWS, 384)), whole((128, ROWS)),
            whole((ROWS, 256)), whole((ROWS, 384)), whole((128, ROWS)), whole(square), whole(square), *specs,
        ],
        out_shape=[
            sds(ROWS, INNER, F32), sds(128, INNER, F32), sds(8, INNER, F32),
            sds(ROWS, 384, BF16), sds(ROWS, 384, BF16), sds(128, ROWS, F32),
            sds(ROWS, 256, BF16), sds(ROWS, 384, BF16), sds(128, ROWS, BF16), sds(*square, F32), sds(*square, F32),
            *shapes,
        ],
        scratch_shapes=[pltpu.VMEM((256, ROWS), BF16), *sems],
        compiler_params=call_params(collective_id),
        cost_estimate=pl.CostEstimate(flops=10**9, bytes_accessed=10 * MIB, transcendentals=10**6),
    )(proj, proj, proj, halo, halo, taps, taps, hp, *sources)


def exchange_kernel(
    n, rev, s_ref, d_ref, o_ref, inbox, dbox, parts, decs, total, chain_out, chain_in, outbox,
    send_a, recv_a, send_d, recv_d, send_c, recv_c, send_o, recv_o,
):
    planes = n // PLANE
    section = lax.axis_index("section")
    q = lax.axis_index("seq")
    u = n - 1 - q if rev else q
    spot, level = lax.rem(u, PLANE), u // PLANE

    def device(at):
        return (section, n - 1 - at if rev else at)

    peers = [lax.rem(spot + k, PLANE) for k in range(1, PLANE)]
    barrier = pltpu.get_barrier_semaphore()
    for peer in peers:
        pl.semaphore_signal(barrier, inc=1, device_id=device(level * PLANE + peer), device_id_type=MESH)

    @pl.when(level > 0)
    def _():
        pl.semaphore_signal(barrier, inc=1, device_id=device(u - PLANE), device_id_type=MESH)

    pl.semaphore_wait(barrier, PLANE - 1 + (level < planes - 1).astype(jnp.int32))

    def group(at):
        return pl.ds(pl.multiple_of(at * LANES, LANES), LANES)

    first = []
    for k, peer in enumerate(peers):
        to = device(level * PLANE + peer)
        first.append(
            pltpu.make_async_remote_copy(
                src_ref=d_ref.at[:, group(peer)], dst_ref=dbox.at[spot],
                send_sem=send_d.at[k], recv_sem=recv_d.at[k], device_id=to, device_id_type=MESH,
            )
        )
        first.append(
            pltpu.make_async_remote_copy(
                src_ref=s_ref.at[:, group(peer)], dst_ref=inbox.at[spot],
                send_sem=send_a.at[k], recv_sem=recv_a.at[k], device_id=to, device_id_type=MESH,
            )
        )
    for copy in first:
        copy.start()
    inbox[spot] = s_ref[:, group(spot)]
    dbox[spot] = d_ref[:, group(spot)]
    for copy in first:
        copy.wait()

    cuts = LANES // 256
    for b in range(cuts):
        at = slice(b * 256, b * 256 + 256)
        state = inbox[0, :, at].astype(F32)
        decay = dbox[0, 0:1, at]
        for p in range(1, PLANE):
            parts[p, :, at] = state
            decs[p, 0:1, at] = decay
            d = dbox[p, 0:1, at]
            state = d * state + inbox[p, :, at].astype(F32)
            decay = decay * d
        total[:, at] = state
        decs[0, 0:1, at] = decay

    def chain(b):
        return pltpu.make_async_remote_copy(
            src_ref=chain_out.at[b], dst_ref=chain_in.at[b],
            send_sem=send_c.at[b], recv_sem=recv_c.at[b],
            device_id=device(lax.rem(u + PLANE, n)), device_id_type=MESH,
        )

    last = []
    for b in range(cuts):
        at = slice(b * 256, b * 256 + 256)

        @pl.when(level > 0)
        def _():
            chain(b).wait_recv()

        @pl.when(level == 0)
        def _():
            chain_in[b] = jnp.zeros((128, 256), chain_in.dtype)

        enter = chain_in[b].astype(F32)

        @pl.when(level < planes - 1)
        def _():
            chain_out[b] = (decs[0, 0:1, at] * enter + total[:, at]).astype(chain_out.dtype)
            chain(b).start()

        outbox[0, :, at] = enter.astype(outbox.dtype)
        for p in range(1, PLANE):
            outbox[p, :, at] = (decs[p, 0:1, at] * enter + parts[p, :, at]).astype(outbox.dtype)
        mine = pl.ds(pl.multiple_of(spot * LANES + b * 256, 256), 256)
        o_ref[:, mine] = outbox[spot, :, at]
        for k, peer in enumerate(peers):
            copy = pltpu.make_async_remote_copy(
                src_ref=outbox.at[peer, :, pl.ds(b * 256, 256)], dst_ref=o_ref.at[:, mine],
                send_sem=send_o.at[b * 3 + k], recv_sem=recv_o.at[b * 3 + k],
                device_id=device(level * PLANE + peer), device_id_type=MESH,
            )
            copy.start()
            last.append(copy)
    for copy in last:
        copy.wait()

    @pl.when(level < planes - 1)
    def _():
        for b in range(cuts):
            chain(b).wait_send()


def exchange(state, decay, n, rev):
    vmem = pl.BlockSpec(memory_space=pltpu.VMEM)
    dma = pltpu.SemaphoreType.DMA
    cuts = LANES // 256
    return pl.pallas_call(
        functools.partial(exchange_kernel, n, rev),
        out_shape=sds(128, INNER, state.dtype),
        in_specs=[vmem, vmem],
        out_specs=vmem,
        scratch_shapes=[
            pltpu.VMEM((PLANE, 128, LANES), state.dtype),
            pltpu.VMEM((PLANE, 8, LANES), F32),
            pltpu.VMEM((PLANE, 128, LANES), F32),
            pltpu.VMEM((PLANE, 8, LANES), F32),
            pltpu.VMEM((128, LANES), F32),
            pltpu.VMEM((cuts, 128, 256), state.dtype),
            pltpu.VMEM((cuts, 128, 256), state.dtype),
            pltpu.VMEM((PLANE, 128, LANES), state.dtype),
            dma((3,)), dma((3,)), dma((3,)), dma((3,)),
            dma((cuts,)), dma((cuts,)), dma((3 * cuts,)), dma((3 * cuts,)),
        ],
        compiler_params=pltpu.CompilerParams(
            collective_id=2 if rev else 1, has_side_effects=True, vmem_limit_bytes=32 * MIB
        ),
    )(state, decay)


def decay_block(later, earlier):
    return jnp.exp(jnp.minimum(later - earlier, 0.0))


def head_lanes(parts, i):
    at = (i // 2) * 128
    here = (iota((ROWS, 128), 1) < HEADDIM) if i % 2 == 0 else (iota((ROWS, 128), 1) >= HEADDIM)
    return [jnp.where(here, part[:, at : at + 128], jnp.zeros((), BF16)) for part in parts]


def mix_kernel(
    n, g_ref, step_ref, cum_ref, cumt_ref, val_ref, gate_ref, c_ref, car_ref, lp_ref, gain_ref,
    y_ref, low_ref, owned_ref, gated_ref, sum_ref,
):
    j = pl.program_id(0)
    heads = expander(j)
    cum = dot_nn(cum_ref[...], heads)
    values = val_ref[...]
    scaled = split2(values * dot_nn(step_ref[...], heads))
    car_high, car_rest = split2(car_ref[...])
    across = dot_nn(c_ref[...], jnp.concatenate([car_high, car_high, car_rest], axis=0))
    y = jnp.exp(cum) * across + lp_ref[0:1, :] * values
    sides = []
    for pair in range(WIDE // 128):
        top = jnp.zeros((HALF, 128), F32)
        bottom = jnp.zeros((HALF, 128), F32)
        for i in (2 * pair, 2 * pair + 1):
            row = cumt_ref[pl.ds((WIDE // HEADDIM) * j + i, 1), :]
            column = cum[:, i * HEADDIM : i * HEADDIM + 1]
            part = head_lanes(scaled, i)
            upper = split2(g_ref[0:HALF, 0:HALF] * decay_block(column[0:HALF], row[:, 0:HALF]))
            top = top + fine(dot_nn, upper, [v[0:HALF] for v in part])
            lower = split2(g_ref[HALF:ROWS, :] * decay_block(column[HALF:ROWS], row))
            bottom = bottom + fine(dot_nn, lower, part)
        sides.append(jnp.concatenate([top, bottom], axis=0))
    y = y + jnp.concatenate(sides, axis=1)
    y_ref[...] = y
    gate = gate_ref[...]
    gated = y * (gate * sigmoid(gate))
    gated_ref[j] = gated

    @pl.when(j == 0)
    def _():
        sum_ref[...] = jnp.zeros_like(sum_ref)

    sum_ref[...] += gated * gated

    @pl.when(j == STEPS - 1)
    def _():
        mean = jnp.sum(sum_ref[...], axis=1, keepdims=True) * (1.0 / INNER)
        scale = lax.rsqrt(mean + EPS)
        for k in range(STEPS):
            at = slice(k * WIDE, k * WIDE + WIDE)
            low_ref[:, at] = (gated_ref[k] * scale * gain_ref[1:2, at]).astype(BF16)
        width = INNER // n
        for q in range(n):
            to = (q % PLANE) * LANES + (q // PLANE) * width
            owned_ref[:, to : to + width] = low_ref[:, q * width : (q + 1) * width]


def mix(g, step, cum, cumt, values, proj, c, carried, lp, n):
    return pl.pallas_call(
        functools.partial(mix_kernel, n),
        grid=(STEPS,),
        in_specs=[
            whole((ROWS, ROWS)), whole((ROWS, 384)), whole((ROWS, 384)), whole((128, ROWS)),
            lanes(ROWS), lanes(ROWS), whole((ROWS, 384)), lanes(128), lanes(8),
            whole((8, INNER)),
        ],
        out_specs=[lanes(ROWS), whole((ROWS, INNER)), whole((ROWS, INNER))],
        out_shape=[sds(ROWS, INNER, F32), sds(ROWS, INNER, BF16), sds(ROWS, INNER, BF16)],
        scratch_shapes=[pltpu.VMEM((STEPS, ROWS, WIDE), F32), pltpu.VMEM((ROWS, WIDE), F32)],
        compiler_params=grid_params(),
        cost_estimate=pl.CostEstimate(flops=3 * 10**9, bytes_accessed=14 * MIB, transcendentals=4 * 10**6),
    )(g, step, cum, cumt, values, proj, c, carried, lp, lp)


def gate_back_kernel(
    dg_ref, y_ref, gate_ref, cum_ref, ct_ref, lp_ref, dy_ref, dgate_ref, gain_ref, dcar_ref,
    dg_all, y_all, gate_all, square_acc, cross_acc,
):
    phase, j = pl.program_id(0), pl.program_id(1)

    @pl.when(jnp.logical_and(phase == 0, j == 0))
    def _():
        square_acc[...] = jnp.zeros_like(square_acc)
        cross_acc[...] = jnp.zeros_like(cross_acc)

    @pl.when(phase == 0)
    def _():
        dg, y, gate = dg_ref[...], y_ref[...], gate_ref[...]
        dg_all[j], y_all[j], gate_all[j] = dg, y, gate
        gated = y * (gate * sigmoid(gate))
        square_acc[...] += gated * gated
        cross_acc[...] += dg * lp_ref[1:2, :] * gated

    @pl.when(phase == 1)
    def _():
        r = lax.rsqrt(jnp.sum(square_acc[...], axis=1, keepdims=True) * (1.0 / INNER) + EPS)
        m = jnp.sum(cross_acc[...], axis=1, keepdims=True) * (1.0 / INNER) * r * r
        dg, y, gate = dg_all[j], y_all[j], gate_all[j]
        s = sigmoid(gate)
        silu = gate * s
        gated = y * silu
        gain_ref[...] = jnp.broadcast_to(jnp.sum(dg * gated * r, axis=0, keepdims=True), (8, WIDE))
        d_gated = r * (dg * lp_ref[1:2, :] - gated * m)
        dy = d_gated * silu
        dy_ref[...] = dy
        dgate_ref[...] = (d_gated * y * (s + silu * (1.0 - s))).astype(BF16)
        cum = dot_nn(cum_ref[...], expander(j))
        dcar_ref[...] = dot_nn(ct_ref[...], (dy * jnp.exp(cum)).astype(BF16)).astype(BF16)


def gate_back(dg, y, proj, cum, ct, lp, sources=(), collective_id=None):
    def first(rows):
        return pl.BlockSpec((rows, WIDE), lambda p, j: (0, j * (1 - p) + (STEPS - 1) * p))

    def second(rows):
        return pl.BlockSpec((rows, WIDE), lambda p, j: (0, j * p))

    def both(shape):
        return pl.BlockSpec(shape, lambda p, j: (0, 0))

    def at_step(phase, j):
        return jnp.logical_and(pl.program_id(0) == phase, pl.program_id(1) == j)

    kept = pltpu.VMEM((STEPS, ROWS, WIDE), F32)
    specs, shapes, sems = spread_specs(sources)
    body = spreading(
        gate_back_kernel, 6, 4, len(sources), lambda: at_step(0, 0), lambda: at_step(1, STEPS - 1)
    )
    return pl.pallas_call(
        body,
        grid=(2, STEPS),
        in_specs=[
            first(ROWS), first(ROWS), first(ROWS), both((ROWS, 384)), both((128, ROWS)),
            pl.BlockSpec((8, WIDE), lambda p, j: (0, j)), *specs,
        ],
        out_specs=[second(ROWS), second(ROWS), second(8), second(128), *specs],
        out_shape=[
            sds(ROWS, INNER, F32), sds(ROWS, INNER, BF16), sds(8, INNER, F32), sds(128, INNER, BF16), *shapes,
        ],
        scratch_shapes=[kept, kept, kept, pltpu.VMEM((ROWS, WIDE), F32), pltpu.VMEM((ROWS, WIDE), F32), *sems],
        compiler_params=call_params(collective_id),
        cost_estimate=pl.CostEstimate(flops=10**9, bytes_accessed=16 * MIB, transcendentals=2 * 10**6),
    )(dg, y, proj, cum, ct, lp, *sources)


def core_back_kernel(
    x_ref, bc_ref, raw_ref, xh_ref, bch_ref, xw_ref, bcw_ref, hp_ref,
    step_ref, cum_ref, cumt_ref, gt_ref, b_ref, c_ref, y_ref, dy_ref, car_ref, late_ref, lp_ref,
    dx_ref, tail_ref, head_ref, taps_ref, hg_ref,
    dgt_acc, dc_acc, db_acc, dcum_acc, dstep_acc, rows_acc,
):
    j = pl.program_id(0)

    @pl.when(j == 0)
    def _():
        for acc in (dgt_acc, dc_acc, db_acc, dcum_acc, dstep_acc, rows_acc):
            acc[...] = jnp.zeros_like(acc)

    @pl.when(j < STEPS)
    def _():
        ext = extended(x_ref[...], xh_ref[...])
        pre = conv_pre(ext, xw_ref[...])
        sig = sigmoid(pre)
        values = pre * sig
        heads, to_heads = expander(j), collector(j)
        step = dot_nn(step_ref[...], heads)
        cum = dot_nn(cum_ref[...], heads)
        last = cum[ROWS - 1 : ROWS]
        scaled = values * step
        scaled_parts = split2(scaled)
        dy = dy_ref[...]
        dy_parts = split2(dy)
        sides = []
        for pair in range(WIDE // 128):
            top = jnp.zeros((HALF, 128), F32)
            bottom = jnp.zeros((HALF, 128), F32)
            at = slice(pair * 128, pair * 128 + 128)
            own = [part[:, at] for part in scaled_parts]
            for i in (2 * pair, 2 * pair + 1):
                row = cumt_ref[pl.ds((WIDE // HEADDIM) * j + i, 1), :]
                column = cum[:, i * HEADDIM : i * HEADDIM + 1]
                part = head_lanes(dy_parts, i)
                decay = decay_block(row, column[0:HALF])
                top = top + fine(dot_nn, split2(gt_ref[0:HALF, :] * decay), part)
                dgt_acc[0:HALF, :] += fine(dot_nt, [v[0:HALF] for v in own], part) * decay
                decay = decay_block(row[:, HALF:ROWS], column[HALF:ROWS])
                late_part = [v[HALF:ROWS] for v in part]
                bottom = bottom + fine(dot_nn, split2(gt_ref[HALF:ROWS, HALF:ROWS] * decay), late_part)
                dgt_acc[HALF:ROWS, HALF:ROWS] += fine(dot_nt, [v[HALF:ROWS] for v in own], late_part) * decay
            sides.append(jnp.concatenate([top, bottom], axis=0))
        car, late = car_ref[...], late_ref[...]
        to_end = jnp.exp(last - cum)
        d_ended = dot_nn(b_ref[:, 0:128], late)
        ended = scaled * to_end
        dc_acc[...] += fine(dot_nt, split2(dy * jnp.exp(cum)), split2(car))
        db_acc[...] += dot_nt(ended.astype(BF16), late)
        d_total = jnp.concatenate(sides, axis=1) + to_end * d_ended
        skip_w = lp_ref[0:1, :]
        dcum_acc[...] += collect(dy * (y_ref[...] - skip_w * values) - scaled * d_total, to_heads)
        dstep_acc[...] += collect(d_total * values, to_heads)
        at_last = jnp.exp(last) * jnp.sum(late.astype(F32) * car, axis=0, keepdims=True)
        at_last = at_last + jnp.sum(ended * d_ended, axis=0, keepdims=True)
        skip = jnp.sum(dy * values, axis=0, keepdims=True)
        rows_acc[...] += collect(jnp.concatenate([at_last, skip, jnp.zeros((6, WIDE), F32)], axis=0), to_heads)
        d_pre = (skip_w * dy + step * d_total) * (sig + values * (1.0 - sig))
        taps_ref[...] = tap_grads(d_pre, ext)
        head_ref[...] = d_pre[0:8]
        d_conv = conv_back(d_pre, xw_ref[...])
        dx_ref[...] = d_conv.astype(BF16)
        tail_ref[...] = d_conv[ROWS - 16 : ROWS]

    @pl.when(j == STEPS)
    def _():
        seen = iota((ROWS, ROWS), 1) >= iota((ROWS, ROWS), 0)
        d_gt = split2(jnp.where(seen, dgt_acc[...], 0.0))
        d_c = dc_acc[...] + fine(dot_tn, d_gt, halves(b_ref))
        d_b = db_acc[...] + fine(dot_nn, d_gt, halves(c_ref))
        ext_bc = extended(bc_ref[...], bch_ref[...])
        pre_bc = conv_pre(ext_bc, bcw_ref[...])
        sig_bc = sigmoid(pre_bc)
        d_pre_bc = jnp.concatenate([d_b, d_c], axis=1) * (sig_bc + pre_bc * sig_bc * (1.0 - sig_bc))
        taps_ref[...] = tap_grads(d_pre_bc, ext_bc)
        head_ref[...] = d_pre_bc[0:8]
        d_conv_bc = conv_back(d_pre_bc, bcw_ref[...])
        dx_ref[...] = d_conv_bc.astype(BF16)
        tail_ref[...] = d_conv_bc[ROWS - 16 : ROWS]

    @pl.when(j == STEPS + 1)
    def _():
        raw, step_all, rate = step_parts(raw_ref, hp_ref)
        end = iota((ROWS, 128), 0) == ROWS - 1
        d_cum_all = dcum_acc[...] + jnp.where(end, rows_acc[0:1, :], 0.0)
        d_log = exact_left(triangle(False), d_cum_all)
        d_step = dstep_acc[...] + rate * d_log
        d_raw = jnp.where(iota((ROWS, 128), 1) < HEADS, d_step * sigmoid(raw), 0.0)
        dx_ref[...] = jnp.concatenate([d_raw, jnp.zeros((ROWS, WIDE - 128), F32)], axis=1).astype(BF16)
        tail_ref[...] = dx_ref[ROWS - 16 : ROWS, :].astype(F32)
        head_ref[...] = jnp.zeros_like(head_ref)
        taps_ref[...] = jnp.zeros_like(taps_ref)
        hg_ref[...] = jnp.concatenate(
            [
                jnp.sum(d_raw, axis=0, keepdims=True),
                jnp.sum(d_log * rate * step_all, axis=0, keepdims=True),
                rows_acc[1:2, :],
                jnp.zeros((5, 128), F32),
            ],
            axis=0,
        )


def core_back(proj, halo, taps, hp, step, cum, cumt, gt, b, c, y, dy, carried, late, lp, sources=(), collective_id=None):
    acc = pltpu.VMEM((ROWS, 128), F32)

    def lanes(rows, first=0):
        return pl.BlockSpec((rows, WIDE), lambda j: (0, first + jnp.minimum(j, STEPS - 1)))

    def out(rows):
        return pl.BlockSpec((rows, WIDE), lambda j: (0, j))

    specs, shapes, sems = spread_specs(sources)
    body = spreading(
        core_back_kernel, 19, 5, len(sources),
        lambda: pl.program_id(0) == 0, lambda: pl.program_id(0) == STEPS + 1,
    )
    return pl.pallas_call(
        body,
        grid=(STEPS + 2,),
        in_specs=[
            lanes(ROWS, STEPS), fixed(ROWS, 2 * STEPS), fixed(ROWS, 50, 128),
            lanes(8), fixed(8, STEPS), lanes(8), fixed(8, STEPS), whole((8, 128)),
            whole((ROWS, 384)), whole((ROWS, 384)), whole((128, ROWS)), whole((ROWS, ROWS)),
            whole((ROWS, 256)), whole((ROWS, 384)),
            lanes(ROWS), lanes(ROWS), lanes(128), lanes(128), lanes(8), *specs,
        ],
        out_specs=[out(ROWS), out(16), out(8), out(8), whole((8, 128)), *specs],
        out_shape=[
            sds(ROWS, REST, BF16), sds(16, REST, F32), sds(8, REST, F32), sds(8, REST, F32), sds(8, 128, F32), *shapes,
        ],
        scratch_shapes=[pltpu.VMEM((ROWS, ROWS), F32), acc, acc, acc, acc, pltpu.VMEM((8, 128), F32), *sems],
        compiler_params=call_params(collective_id),
        cost_estimate=pl.CostEstimate(flops=8 * 10**9, bytes_accessed=14 * MIB, transcendentals=5 * 10**6),
    )(
        proj, proj, proj, halo, halo, taps, taps, hp,
        step, cum, cumt, gt, b, c, y, dy, carried, late, lp, *sources,
    )


def settle_kernel(
    n, ga0, re0, ga1, re1, ow0, ow1, a0, a1, d0, d1, gin_ref, gout_ref, acts_ref, grads_ref,
    gate_in, rest_in, out_in, send_g, recv_g, send_r, recv_r, send_o, recv_o, send_x, recv_x, keep_x,
):
    core = lax.axis_index("section")
    q = lax.axis_index("seq")
    spot = lax.rem(q, PLANE)
    base = q - spot
    rows = gin_ref.shape[0]
    barrier = pltpu.get_barrier_semaphore()
    for k in range(PLANE):
        for flip in range(2):
            if k or flip:
                to = (core ^ flip, base + lax.rem(spot + k, PLANE))
                pl.semaphore_signal(barrier, inc=1, device_id=to, device_id_type=MESH)
    pl.semaphore_wait(barrier, 2 * PLANE - 1)

    def run(layer, gate, rest, outw, act, grad, away_act, away_grad, away_outw, away_gate, away_rest):
        copies = []

        def send(src, dst, sems, at, to):
            copy = pltpu.make_async_remote_copy(
                src_ref=src, dst_ref=dst, send_sem=sems[0].at[at], recv_sem=sems[1].at[at],
                device_id=to, device_id_type=MESH,
            )
            copy.start()
            copies.append(copy)

        across = (1 - layer, q)
        kept = []
        for at, (own, away, dst) in enumerate(((grad, away_grad, grads_ref), (act, away_act, acts_ref))):
            send(away, dst.at[layer], (send_x, recv_x), at, across)
            kept.append(pltpu.make_async_copy(own, dst.at[layer], keep_x.at[at]))
            kept[-1].start()
        send(away_outw, out_in, (send_o, recv_o), 0, across)
        for k in range(PLANE):
            peer = lax.rem(spot + k, PLANE)
            block = pl.ds(pl.multiple_of(peer * rows, rows), rows)
            for flip in range(2):
                if not (k or flip):
                    continue
                at = 2 * k + flip
                to = (1 - layer if flip else layer, base + peer)
                slot = 2 * spot + layer
                send((away_gate if flip else gate).at[block], gate_in.at[slot], (send_g, recv_g), at, to)
                send((away_rest if flip else rest).at[block], rest_in.at[slot], (send_r, recv_r), at, to)
        mine = pl.ds(pl.multiple_of(spot * rows, rows), rows)
        gate_in[2 * spot + layer] = gate[mine, :]
        rest_in[2 * spot + layer] = rest[mine, :]
        half = D // 2
        gout_ref[:, layer * half : layer * half + half] = outw[...].astype(F32)
        for copy in copies + kept:
            copy.wait()
        gout_ref[:, (1 - layer) * half : (1 - layer) * half + half] = out_in[...].astype(F32)

    @pl.when(core == 0)
    def _():
        run(0, ga0, re0, ow0, a0, d0, a1, d1, ow1, ga1, re1)

    @pl.when(core == 1)
    def _():
        run(1, ga1, re1, ow1, a1, d1, a0, d0, ow0, ga0, re0)

    for p in range(2 * PLANE):
        wide = gate_in.shape[2]
        gin_ref[:, p * wide : p * wide + wide] = gate_in[p].astype(F32)
        wide = rest_in.shape[2]
        at = INNER + p * wide
        width = min(wide, PROJ - at)
        gin_ref[:, at : at + width] = rest_in[p].astype(F32)[:, :width]


def settle(gates, rests, outs, acts, grads, n):
    vmem = pl.BlockSpec(memory_space=pltpu.VMEM)
    anywhere = pl.BlockSpec(memory_space=pl.ANY)
    dma = pltpu.SemaphoreType.DMA
    rows = D // n
    eight = 2 * PLANE
    return pl.pallas_call(
        functools.partial(settle_kernel, n),
        out_shape=[
            sds(rows, PROJ, F32), sds(INNER // n, D, F32),
            jax.ShapeDtypeStruct((2, ROWS, D), BF16), jax.ShapeDtypeStruct((2, ROWS, D), F32),
        ],
        in_specs=[vmem] * 6 + [anywhere] * 4,
        out_specs=[vmem, vmem, anywhere, anywhere],
        scratch_shapes=[
            pltpu.VMEM((eight, rows, gates[0].shape[1]), BF16),
            pltpu.VMEM((eight, rows, rests[0].shape[1]), BF16),
            pltpu.VMEM((INNER // n, D // 2), BF16),
            dma((eight,)), dma((eight,)), dma((eight,)), dma((eight,)),
            dma((1,)), dma((1,)), dma((2,)), dma((2,)), dma((2,)),
        ],
        compiler_params=pltpu.CompilerParams(collective_id=3, has_side_effects=True, vmem_limit_bytes=40 * MIB),
    )(gates[0], rests[0], gates[1], rests[1], outs[0], outs[1], acts[0], acts[1], grads[0], grads[1])


def swap(value):
    return lax.ppermute(value, "section", [(0, 1), (1, 0)])


def shifted(value, distance, n):
    return lax.ppermute(value, "seq", [(i, i + distance) for i in range(n) if 0 <= i + distance < n])


def plane_route(k, n):
    return [(i, i - i % PLANE + (i + k) % PLANE) for i in range(n)]


def rms(value):
    return lax.rsqrt(jnp.mean(value * value, axis=-1, keepdims=True) + EPS)


def tied(value, *others):
    return lax.optimization_barrier((value, *others))[0]


def copies_of(value, n):
    return [value] + [lax.ppermute(value, "seq", plane_route(k, n)) for k in range(1, PLANE)]


def arrived(value, *lists):
    value, *rest = lax.optimization_barrier((value, *(copy for copies in lists for copy in copies)))
    return (value, *(jnp.stack(rest[k * PLANE : (k + 1) * PLANE]) for k in range(len(lists))))


def partial_grad(left, right):
    core = lax.axis_index("section")
    half = right.shape[2] // 2

    def part(side):
        cols = lax.dynamic_slice_in_dim(right, side * half, half, 2)
        return lax.dot_general(left, cols, (((0, 1), (0, 1)), ((), ())), preferred_element_type=F32)

    away = part(1 - core).astype(BF16)
    return (part(core) + swap(away).astype(F32)).astype(BF16)


def plane_rows(partial, n):
    columns = [[p + PLANE * z for z in range(n // PLANE)] for p in range(PLANE)]
    return lax.psum_scatter(partial, "seq", scatter_dimension=0, axis_index_groups=columns, tiled=True)


SIZES = [D, CONVD * CONV, CONVD, HEADS, HEADS, HEADS, INNER]


def split_small(flat):
    parts, at = [], 0
    for size in SIZES:
        parts.append(flat[at : at + size])
        at += size
    return parts


def unpack_params(flat):
    norm_g, conv_w, conv_b, dt_b, a_lg, skip_w, gate_g = split_small(flat)
    taps = jnp.concatenate(
        [conv_w.reshape(CONV, CONVD), conv_b[None], jnp.zeros((3, CONVD), F32)], axis=0
    )
    pad = jnp.zeros((128 - HEADS,), F32)
    hp = jnp.concatenate([dt_b, pad, a_lg, pad, jnp.zeros((6 * 128,), F32)]).reshape(8, 128)
    lp = jnp.concatenate(
        [jnp.repeat(skip_w, HEADDIM)[None], gate_g[None], jnp.zeros((6, INNER), F32)], axis=0
    )
    return norm_g, taps, hp, lp


def per_device(
    inputs, cotangent, norm_gain, in_weight, conv_weight, conv_bias, dt_bias, a_log, d_skip,
    gate_norm_gain, out_weight,
):
    n = lax.axis_size("seq")
    core = lax.axis_index("section")
    place = lax.axis_index("seq")
    first = core == 0
    own_in, own_out = in_weight[0].T, out_weight[0]
    other_in = swap(own_in)
    own_small = jnp.concatenate(
        [
            norm_gain[0], conv_weight[0].T.reshape(-1), conv_bias[0], dt_bias[0], a_log[0], d_skip[0],
            gate_norm_gain[0],
        ]
    )
    other_small = swap(own_small)
    flags = [(core == layer).astype(jnp.int32)[None] for layer in range(2)]
    params = [
        unpack_params(jnp.where(first, own_small, other_small)),
        unpack_params(jnp.where(first, other_small, own_small)),
    ]

    def mine(pair):
        return lax.dynamic_index_in_dim(pair, core, 0, keepdims=False)

    def normed_of(layer, h):
        return (h * rms(h) * params[layer][0]).astype(BF16)

    def project(layer, normed, before):
        proj, halo = project_mm(normed, normed_of(layer, before.astype(F32)), own_in, other_in, flags[layer], 1664)
        return proj, halo[8:, INNER : INNER + CONVD]

    def blocks(layer, proj, halo):
        _, taps, hp, _ = params[layer]
        return front(proj, halo, taps, hp)

    def finish(layer, h, proj, parts, carried):
        values, _, _, step, cum, cumt, _, c, _, g, _ = parts[:11]
        y, gated_low, owned = mix(g, step, cum, cumt, values, proj, c, carried, params[layer][3], n)
        return y, owned, h + mm(gated_low, own_out, other_out, flags[layer], False, 768)

    x_0 = mine(inputs)
    before_0 = shifted(x_0[ROWS - 16 :], 1, n)
    d_out_1 = mine(cotangent)
    h_0 = x_0.astype(F32)
    normed_0 = normed_of(0, h_0)
    normed_0, lows_1 = arrived(normed_0, copies_of(d_out_1, n))
    proj_0, halo_0 = project(0, normed_0, before_0)
    other_out = swap(tied(own_out, proj_0))
    parts_0 = blocks(0, proj_0, halo_0)
    carried_0 = exchange(parts_0[1], parts_0[2], n, False)
    normeds_0 = copies_of(tied(normed_0, carried_0), n)
    y_0, owned_0, out_0 = finish(0, h_0, proj_0, parts_0, carried_0)
    act_0 = out_0.astype(BF16)

    before_1 = shifted(act_0[ROWS - 16 :], 1, n)
    h_1 = act_0.astype(F32)
    normed_1 = normed_of(1, h_1)
    normeds_1 = copies_of(tied(normed_1, before_1), n)
    proj_1, halo_1 = project(1, normed_1, before_1)
    parts_1 = blocks(1, proj_1, halo_1)
    carried_1 = exchange(parts_1[1], parts_1[2], n, False)
    carried_1, normeds_0, normeds_1 = arrived(carried_1, normeds_0, normeds_1)
    y_1, owned_1, out_1 = finish(1, h_1, proj_1, parts_1, carried_1)
    act_1 = out_1.astype(BF16)

    def gate_side(layer, d_low, y, proj, parts, *spread):
        d_gated_low = mm(d_low, own_out, other_out, flags[layer], True, 1024)
        return gate_back(d_gated_low, y, proj, parts[4], parts[8], params[layer][3], *spread)

    def core_side(layer, proj, halo, parts, y, dy, carried, late, *spread):
        _, taps, hp, lp = params[layer]
        _, _, _, step, cum, cumt, b, c, _, _, gt = parts[:11]
        return core_back(proj, halo, taps, hp, step, cum, cumt, gt, b, c, y, dy, carried, late, lp, *spread)

    def conv_side(layer, back):
        rest, tail, head = back[:3]
        w = jnp.concatenate([params[layer][1], jnp.zeros((8, REST - CONVD), F32)], axis=1)
        a = shifted(head, -1, n)
        fix = jnp.concatenate(
            [
                jnp.zeros((13, REST), F32),
                w[0:1] * a[0:1],
                w[0:1] * a[1:2] + w[1:2] * a[0:1],
                w[0:1] * a[2:3] + w[1:2] * a[1:2] + w[2:3] * a[0:1],
            ],
            axis=0,
        )
        return lax.dynamic_update_slice(rest, (tail + fix).astype(BF16), (ROWS - 16, 0))

    def norm_side(layer, h, d_out, d_gate, rest):
        norm_g = params[layer][0]
        d_normed = back_mm(d_gate, rest, own_in, other_in, flags[layer], 512)
        r = rms(h)
        v = d_normed * norm_g
        d_h = d_out + r * (v - h * (r * r * jnp.mean(v * h, axis=-1, keepdims=True)))
        return d_h, jnp.sum(d_normed * h * r, axis=0)

    def small_of(norm_gain_grad, back, gate_gain):
        taps_all, heads = back[3][:, :CONVD], back[4]
        return jnp.concatenate(
            [
                norm_gain_grad, taps_all[:CONV].reshape(-1), taps_all[CONV],
                heads[0, :HEADS], heads[1, :HEADS], heads[2, :HEADS], gate_gain[0],
            ]
        )

    dy_1, d_gate_1, gain_1, d_carried_1, gateds_0 = gate_side(
        1, tied(d_out_1, carried_1), y_1, proj_1, parts_1, (owned_0,), 4
    )
    late_1 = exchange(d_carried_1, parts_1[2], n, True)
    back_1 = core_side(
        1, proj_1, halo_1, parts_1, y_1, dy_1, carried_1, late_1, (d_gate_1, owned_1), 5
    )
    gates_1, gateds_1 = back_1[5:]
    outw_1 = partial_grad(gateds_1, lows_1)
    gatew_1 = partial_grad(normeds_1, gates_1)
    rest_1 = conv_side(1, back_1)
    rest_1 = tied(rest_1, outw_1, gatew_1)
    outw_1, gatew_1 = plane_rows(outw_1, n), plane_rows(gatew_1, n)
    d_1, ng_1 = norm_side(1, h_1, d_out_1.astype(F32), d_gate_1, rest_1)

    d_out_0 = d_1.astype(BF16)
    dy_0, d_gate_0, gain_0, d_carried_0, rests_1 = gate_side(0, d_out_0, y_0, proj_0, parts_0, (rest_1,), 6)
    restw_1 = partial_grad(normeds_1, rests_1)
    late_0 = exchange(tied(d_carried_0, restw_1), parts_0[2], n, True)
    restw_1 = plane_rows(restw_1, n)
    lows_0 = copies_of(tied(d_out_0, late_0), n)
    back_0 = core_side(
        0, proj_0, halo_0, parts_0, y_0, dy_0, carried_0, late_0, (d_gate_0,), 7
    )
    gates_0, lows_0 = arrived(back_0[5], lows_0)
    gatew_0 = partial_grad(normeds_0, gates_0)
    outw_0 = plane_rows(partial_grad(gateds_0, lows_0), n)
    rest_0 = conv_side(0, back_0)
    rest_0 = tied(rest_0, gatew_0)
    gatew_0 = plane_rows(gatew_0, n)
    spot = place % PLANE
    width = REST // PLANE
    pieces = [lax.dynamic_slice_in_dim(rest_0, (spot + k) % PLANE * width, width, 1) for k in range(PLANE)]
    rests_0 = pieces[:1] + [lax.ppermute(pieces[k], "seq", plane_route(k, n)) for k in range(1, PLANE)]
    d_0, ng_0 = norm_side(0, h_0, d_out_0.astype(F32), d_gate_0, rest_0)
    ng_0, rests_0 = arrived(ng_0, rests_0)
    restw_0 = plane_rows(partial_grad(normeds_0, rests_0), n)

    g_in, g_out, acts, input_grads = settle(
        (gatew_0, gatew_1), (restw_0, restw_1), (outw_0, outw_1), (act_0, act_1), (d_0, d_1), n
    )
    small_0, small_1 = small_of(ng_0, back_0, gain_0), small_of(ng_1, back_1, gain_1)
    small = jnp.where(first, small_0, small_1) + swap(jnp.where(first, small_1, small_0))
    reach = 1
    while reach < n:
        small = small + lax.ppermute(small, "seq", [(i, i ^ reach) for i in range(n)])
        reach *= 2
    norm_g, conv_w, conv_b, dt_b, a_lg, skip_w, gate_g = split_small(small)

    def share(value):
        rows = value.shape[0] // n
        return lax.dynamic_slice_in_dim(value, place * rows, rows, 0)[None]

    conv_rows = CONVD // n
    conv_w = lax.dynamic_slice_in_dim(conv_w.reshape(CONV, CONVD), place * conv_rows, conv_rows, 1).T
    return (
        acts[None], input_grads[None], share(norm_g), g_in[None], conv_w[None], share(conv_b),
        dt_b[None], a_lg[None], skip_w[None], share(gate_g), g_out[None],
    )


def solution(mesh):
    in_specs = (
        P(None, "seq", None), P(None, "seq", None), P("section", None), P("section", None, None),
        P("section", None, None), P("section", None), P("section", None), P("section", None),
        P("section", None), P("section", None), P("section", None, None),
    )
    out_specs = (
        P("section", None, "seq", None), P("section", None, "seq", None), P("section", "seq"),
        P("section", "seq", None), P("section", "seq", None), P("section", "seq"), P("section", None),
        P("section", None), P("section", None), P("section", "seq"), P("section", "seq", None),
    )
    return jax.shard_map(per_device, mesh=mesh, in_specs=in_specs, out_specs=out_specs, check_vma=False)
```

```python
import functools

import jax
import jax.numpy as jnp
from jax import lax
from jax.experimental import pallas as pl
from jax.experimental.pallas import tpu as pltpu
from jax.sharding import PartitionSpec as P

D = 1536
INNER = 3072
STATE = 128
HEADS = 48
HEADDIM = 64
CONV = 4
CONVD = 3328
PROJ = 6448
ROWS = 256
WIDE = 256
STEPS = INNER // WIDE
HALF = ROWS // 2
PLANE = 4
LANES = INNER // PLANE
REST = 3584
EPS = 1e-05
MIB = 2**20
MESH = pl.DeviceIdType.MESH
F32 = jnp.float32
BF16 = jnp.bfloat16


def dot_nn(a, b):
    return lax.dot_general(a, b, (((1,), (0,)), ((), ())), preferred_element_type=F32)


def dot_tn(a, b):
    return lax.dot_general(a, b, (((0,), (0,)), ((), ())), preferred_element_type=F32)


def dot_nt(a, b):
    return lax.dot_general(a, b, (((1,), (1,)), ((), ())), preferred_element_type=F32)


def split3(v):
    high = v.astype(BF16)
    rest = v - high.astype(F32)
    mid = rest.astype(BF16)
    return high, mid, (rest - mid.astype(F32)).astype(BF16)


def split2(v):
    high = v.astype(BF16)
    return high, (v - high.astype(F32)).astype(BF16)


def fine(dot, a, b):
    return dot(a[0], b[0]) + (dot(a[0], b[1]) + dot(a[1], b[0]))


def halves(ref):
    return ref[:, 0:128], ref[:, 128:256]


def parts3(v):
    return jnp.concatenate(split3(v), axis=1)


def exact_left(ones, v):
    a, b, c = split3(v)
    return dot_nn(ones, a) + (dot_nn(ones, b) + dot_nn(ones, c))


def iota(shape, dim):
    return lax.broadcasted_iota(jnp.int32, shape, dim)


def expander(step):
    head_of = (WIDE // HEADDIM) * step + lax.shift_right_logical(iota((128, WIDE), 1), 6)
    ones = (iota((128, WIDE), 0) == head_of).astype(F32).astype(BF16)
    return jnp.concatenate([ones, ones, ones], axis=0)


def collector(step):
    head_of = (WIDE // HEADDIM) * step + lax.shift_right_logical(iota((WIDE, 128), 0), 6)
    return (iota((WIDE, 128), 1) == head_of).astype(F32).astype(BF16)


def collect(v, ones):
    a, b, c = split3(v)
    return dot_nn(a, ones) + (dot_nn(b, ones) + dot_nn(c, ones))


def triangle(lower):
    rows, cols = iota((ROWS, ROWS), 0), iota((ROWS, ROWS), 1)
    return ((rows >= cols) if lower else (rows <= cols)).astype(F32).astype(BF16)


def sigmoid(v):
    return 0.5 * jnp.tanh(0.5 * v) + 0.5


def extended(block, halo):
    return jnp.concatenate([halo, block], axis=0)


def conv_pre(ext, taps):
    out = taps[4:5] + taps[0:1] * ext[5 : 5 + ROWS]
    for k in range(1, CONV):
        out = out + taps[k : k + 1] * ext[5 + k : 5 + k + ROWS]
    return out


def conv_back(d_pre, taps):
    ext = jnp.concatenate([d_pre, jnp.zeros((8, d_pre.shape[1]), F32)], axis=0)
    out = taps[3:4] * d_pre
    for k in range(CONV - 1):
        out = out + taps[k : k + 1] * ext[3 - k : 3 - k + ROWS]
    return out


def tap_grads(d_pre, ext):
    rows = [jnp.sum(d_pre * ext[5 + k : 5 + k + ROWS], axis=0, keepdims=True) for k in range(CONV)]
    rows.append(jnp.sum(d_pre, axis=0, keepdims=True))
    rows.append(jnp.zeros((3, d_pre.shape[1]), F32))
    return jnp.concatenate(rows, axis=0)


def step_parts(raw_ref, hp_ref):
    real = iota((ROWS, 128), 1) < HEADS
    raw = jnp.where(real, raw_ref[...], 0.0) + hp_ref[0:1, :]
    step = jnp.maximum(raw, 0.0) + jnp.log1p(jnp.exp(-jnp.abs(raw)))
    step = jnp.where(real, step, 0.0)
    rate = jnp.where(real[0:1], -jnp.exp(hp_ref[1:2, :]), 0.0)
    return raw, step, rate


def mm_kernel(flag_ref, x_ref, own_ref, other_ref, o_ref, *, nt):
    dot = dot_nt if nt else dot_nn

    @pl.when(flag_ref[0] == 1)
    def _():
        o_ref[...] = dot(x_ref[...], own_ref[...])

    @pl.when(flag_ref[0] == 0)
    def _():
        o_ref[...] = dot(x_ref[...], other_ref[...])


def mm(x, own, other, flag, nt, tile):
    rows, depth = x.shape
    width = own.shape[0] if nt else own.shape[1]
    block = (tile, depth) if nt else (depth, tile)

    def place(j, keep):
        return (j * keep, 0) if nt else (0, j * keep)

    return pl.pallas_call(
        functools.partial(mm_kernel, nt=nt),
        grid_spec=pltpu.PrefetchScalarGridSpec(
            num_scalar_prefetch=1,
            grid=(pl.cdiv(width, tile),),
            in_specs=[
                pl.BlockSpec((rows, depth), lambda j, f: (0, 0)),
                pl.BlockSpec(block, lambda j, f: place(j, f[0])),
                pl.BlockSpec(block, lambda j, f: place(j, 1 - f[0])),
            ],
            out_specs=pl.BlockSpec((rows, tile), lambda j, f: (0, j)),
        ),
        out_shape=jax.ShapeDtypeStruct((rows, width), F32),
        compiler_params=pltpu.CompilerParams(vmem_limit_bytes=48 * MIB),
        cost_estimate=pl.CostEstimate(
            flops=2 * rows * depth * width, bytes_accessed=2 * depth * width, transcendentals=0
        ),
    )(flag, x, own, other)


def spread_copies(pairs, sems):
    send, recv, keep = sems
    section, q = lax.axis_index("section"), lax.axis_index("seq")
    spot = lax.rem(q, PLANE)
    base = q - spot
    away, own = [], []
    for at, (src, dst) in enumerate(pairs):
        width = dst.shape[2]
        for k in range(PLANE):
            peer = lax.rem(spot + k, PLANE)
            part = src.at[:, pl.ds(pl.multiple_of(peer * width, 128), width)]
            if k:
                away.append(
                    pltpu.make_async_remote_copy(
                        src_ref=part, dst_ref=dst.at[k], send_sem=send.at[3 * at + k - 1],
                        recv_sem=recv.at[3 * at + k - 1], device_id=(section, base + peer), device_id_type=MESH,
                    )
                )
            else:
                own.append(pltpu.make_async_copy(part, dst.at[0], keep.at[at]))
    return away, own


def spread_start(pairs, sems):
    section, q = lax.axis_index("section"), lax.axis_index("seq")
    spot = lax.rem(q, PLANE)
    barrier = pltpu.get_barrier_semaphore()
    for k in range(1, PLANE):
        peer = q - spot + lax.rem(spot + k, PLANE)
        pl.semaphore_signal(barrier, inc=1, device_id=(section, peer), device_id_type=MESH)
    pl.semaphore_wait(barrier, PLANE - 1)
    away, own = spread_copies(pairs, sems)
    for copy in away + own:
        copy.start()


def spread_wait(pairs, sems):
    away, own = spread_copies(pairs, sems)
    for copy in away + own:
        copy.wait()


def spread_specs(sources):
    anywhere = pl.BlockSpec(memory_space=pl.ANY)
    shapes = [jax.ShapeDtypeStruct((PLANE, v.shape[0], v.shape[1] // PLANE), v.dtype) for v in sources]
    dma = pltpu.SemaphoreType.DMA
    sems = [dma((3 * len(sources),)), dma((3 * len(sources),)), dma((len(sources),))] if sources else []
    return [anywhere] * len(sources), shapes, sems


def spreading(body, n_in, n_out, count, first, last):
    if not count:
        return body

    def kernel(*refs):
        ins, rest = refs[: n_in + count], refs[n_in + count :]
        outs, scratch = rest[: n_out + count], rest[n_out + count :]
        pairs = list(zip(ins[n_in:], outs[n_out:]))
        sems = scratch[-3:]

        @pl.when(first())
        def _():
            spread_start(pairs, sems)

        body(*ins[:n_in], *outs[:n_out], *scratch[:-3])

        @pl.when(last())
        def _():
            spread_wait(pairs, sems)

    return kernel


def call_params(collective_id):
    if collective_id is None:
        return grid_params()
    return pltpu.CompilerParams(
        vmem_limit_bytes=48 * MIB, collective_id=collective_id, has_side_effects=True
    )


def project_kernel(flag_ref, x_ref, own_ref, other_ref, o_ref, halo_ref):
    def product(w_ref):
        both = dot_nt(x_ref[...], w_ref[...])
        o_ref[...] = both[0:ROWS]
        halo_ref[...] = both[ROWS : ROWS + 16]

    @pl.when(flag_ref[0] == 1)
    def _():
        product(own_ref)

    @pl.when(flag_ref[0] == 0)
    def _():
        product(other_ref)


def project_mm(x, before, own, other, flag, tile):
    rows, depth = x.shape
    width = own.shape[0]
    x = jnp.concatenate([x, before], axis=0)
    return pl.pallas_call(
        project_kernel,
        grid_spec=pltpu.PrefetchScalarGridSpec(
            num_scalar_prefetch=1,
            grid=(pl.cdiv(width, tile),),
            in_specs=[
                pl.BlockSpec((rows + 16, depth), lambda j, f: (0, 0)),
                pl.BlockSpec((tile, depth), lambda j, f: (j * f[0], 0)),
                pl.BlockSpec((tile, depth), lambda j, f: (j * (1 - f[0]), 0)),
            ],
            out_specs=[
                pl.BlockSpec((rows, tile), lambda j, f: (0, j)),
                pl.BlockSpec((16, tile), lambda j, f: (0, j)),
            ],
        ),
        out_shape=[sds(rows, width, F32), sds(16, width, F32)],
        compiler_params=pltpu.CompilerParams(vmem_limit_bytes=48 * MIB),
        cost_estimate=pl.CostEstimate(
            flops=2 * rows * depth * width, bytes_accessed=2 * depth * width, transcendentals=0
        ),
    )(flag, x, own, other)


def back_kernel(flag_ref, gate_ref, rest_ref, own_ref, other_ref, o_ref):
    def product(w_ref):
        o_ref[...] = dot_nn(gate_ref[...], w_ref[0:INNER, :]) + dot_nn(
            rest_ref[:, 0 : PROJ - INNER], w_ref[INNER:PROJ, :]
        )

    @pl.when(flag_ref[0] == 1)
    def _():
        product(own_ref)

    @pl.when(flag_ref[0] == 0)
    def _():
        product(other_ref)


def back_mm(gate, rest, own, other, flag, tile):
    return pl.pallas_call(
        back_kernel,
        grid_spec=pltpu.PrefetchScalarGridSpec(
            num_scalar_prefetch=1,
            grid=(D // tile,),
            in_specs=[
                pl.BlockSpec((ROWS, INNER), lambda j, f: (0, 0)),
                pl.BlockSpec((ROWS, REST), lambda j, f: (0, 0)),
                pl.BlockSpec((PROJ, tile), lambda j, f: (0, j * f[0])),
                pl.BlockSpec((PROJ, tile), lambda j, f: (0, j * (1 - f[0]))),
            ],
            out_specs=pl.BlockSpec((ROWS, tile), lambda j, f: (0, j)),
        ),
        out_shape=sds(ROWS, D, F32),
        compiler_params=pltpu.CompilerParams(vmem_limit_bytes=48 * MIB),
        cost_estimate=pl.CostEstimate(
            flops=2 * ROWS * D * PROJ, bytes_accessed=2 * D * PROJ, transcendentals=0
        ),
    )(flag, gate, rest, own, other)


def front_kernel(
    x_ref, bc_ref, raw_ref, xh_ref, bch_ref, xw_ref, bcw_ref, hp_ref,
    val_ref, state_ref, dec_ref, step_ref, cum_ref, cumt_ref, b_ref, c_ref, ct_ref, g_ref, gt_ref, bt_ref,
):
    j = pl.program_id(0)

    @pl.when(j == 0)
    def _():
        _, step, rate = step_parts(raw_ref, hp_ref)
        step_ref[...] = parts3(step)
        cum = exact_left(triangle(True), rate * step)
        cum_ref[...] = parts3(cum)
        cumt_ref[...] = cum.T
        pre = conv_pre(extended(bc_ref[...], bch_ref[...]), bcw_ref[...])
        both = pre * sigmoid(pre)
        b, c = both[:, 0:128], both[:, 128:256]
        b_low, c_low = split2(b), split2(c)
        b_ref[...] = jnp.concatenate(b_low, axis=1)
        c_ref[...] = jnp.concatenate([c_low[0], c_low[1], c_low[0]], axis=1)
        ct_ref[...] = c.T.astype(BF16)
        bt_ref[...] = jnp.concatenate(split2(b.T), axis=0)
        seen = iota((ROWS, ROWS), 0) >= iota((ROWS, ROWS), 1)
        g = jnp.where(seen, fine(dot_nt, c_low, b_low), 0.0)
        g_ref[...] = g
        gt_ref[...] = g.T

    pre = conv_pre(extended(x_ref[...], xh_ref[...]), xw_ref[...])
    values = pre * sigmoid(pre)
    val_ref[...] = values
    heads = expander(j)
    cum = dot_nn(cum_ref[...], heads)
    last = cum[ROWS - 1 : ROWS]
    high, rest = split2(values * dot_nn(step_ref[...], heads) * jnp.exp(last - cum))
    twice = dot_nn(bt_ref[...], high)
    state_ref[...] = twice[0:128] + twice[128:256] + dot_nn(bt_ref[0:128, :], rest)
    dec_ref[...] = jnp.broadcast_to(jnp.exp(last), (8, WIDE))


def whole(shape):
    return pl.BlockSpec(shape, lambda j: (0, 0))


def lanes(rows, first=0):
    return pl.BlockSpec((rows, WIDE), lambda j: (0, first + j))


def fixed(rows, at, width=WIDE):
    return pl.BlockSpec((rows, width), lambda j: (0, at))


def sds(rows, cols, dtype):
    return jax.ShapeDtypeStruct((rows, cols), dtype)


def grid_params():
    return pltpu.CompilerParams(vmem_limit_bytes=48 * MIB)


def front(proj, halo, taps, hp, sources=(), collective_id=None):
    square = (ROWS, ROWS)
    specs, shapes, sems = spread_specs(sources)
    body = spreading(
        front_kernel, 8, 11, len(sources), lambda: pl.program_id(0) == 0, lambda: pl.program_id(0) == STEPS - 1
    )
    return pl.pallas_call(
        body,
        grid=(STEPS,),
        in_specs=[
            lanes(ROWS, STEPS), fixed(ROWS, 2 * STEPS), fixed(ROWS, 50, 128),
            lanes(8), fixed(8, STEPS), lanes(8), fixed(8, STEPS), whole((8, 128)), *specs,
        ],
        out_specs=[
            lanes(ROWS), lanes(128), lanes(8),
            whole((ROWS, 384)), whole((ROWS, 384)), whole((128, ROWS)),
            whole((ROWS, 256)), whole((ROWS, 384)), whole((128, ROWS)), whole(square), whole(square), *specs,
        ],
        out_shape=[
            sds(ROWS, INNER, F32), sds(128, INNER, F32), sds(8, INNER, F32),
            sds(ROWS, 384, BF16), sds(ROWS, 384, BF16), sds(128, ROWS, F32),
            sds(ROWS, 256, BF16), sds(ROWS, 384, BF16), sds(128, ROWS, BF16), sds(*square, F32), sds(*square, F32),
            *shapes,
        ],
        scratch_shapes=[pltpu.VMEM((256, ROWS), BF16), *sems],
        compiler_params=call_params(collective_id),
        cost_estimate=pl.CostEstimate(flops=10**9, bytes_accessed=10 * MIB, transcendentals=10**6),
    )(proj, proj, proj, halo, halo, taps, taps, hp, *sources)


def exchange_kernel(
    n, rev, s_ref, d_ref, o_ref, inbox, dbox, parts, decs, total, chain_out, chain_in, outbox,
    send_a, recv_a, send_d, recv_d, send_c, recv_c, send_o, recv_o,
):
    planes = n // PLANE
    section = lax.axis_index("section")
    q = lax.axis_index("seq")
    u = n - 1 - q if rev else q
    spot, level = lax.rem(u, PLANE), u // PLANE

    def device(at):
        return (section, n - 1 - at if rev else at)

    peers = [lax.rem(spot + k, PLANE) for k in range(1, PLANE)]
    barrier = pltpu.get_barrier_semaphore()
    for peer in peers:
        pl.semaphore_signal(barrier, inc=1, device_id=device(level * PLANE + peer), device_id_type=MESH)

    @pl.when(level > 0)
    def _():
        pl.semaphore_signal(barrier, inc=1, device_id=device(u - PLANE), device_id_type=MESH)

    pl.semaphore_wait(barrier, PLANE - 1 + (level < planes - 1).astype(jnp.int32))

    def group(at):
        return pl.ds(pl.multiple_of(at * LANES, LANES), LANES)

    first = []
    for k, peer in enumerate(peers):
        to = device(level * PLANE + peer)
        first.append(
            pltpu.make_async_remote_copy(
                src_ref=d_ref.at[:, group(peer)], dst_ref=dbox.at[spot],
                send_sem=send_d.at[k], recv_sem=recv_d.at[k], device_id=to, device_id_type=MESH,
            )
        )
        first.append(
            pltpu.make_async_remote_copy(
                src_ref=s_ref.at[:, group(peer)], dst_ref=inbox.at[spot],
                send_sem=send_a.at[k], recv_sem=recv_a.at[k], device_id=to, device_id_type=MESH,
            )
        )
    for copy in first:
        copy.start()
    inbox[spot] = s_ref[:, group(spot)]
    dbox[spot] = d_ref[:, group(spot)]
    for copy in first:
        copy.wait()

    cuts = LANES // 256
    for b in range(cuts):
        at = slice(b * 256, b * 256 + 256)
        state = inbox[0, :, at].astype(F32)
        decay = dbox[0, 0:1, at]
        for p in range(1, PLANE):
            parts[p, :, at] = state
            decs[p, 0:1, at] = decay
            d = dbox[p, 0:1, at]
            state = d * state + inbox[p, :, at].astype(F32)
            decay = decay * d
        total[:, at] = state
        decs[0, 0:1, at] = decay

    def chain(b):
        return pltpu.make_async_remote_copy(
            src_ref=chain_out.at[b], dst_ref=chain_in.at[b],
            send_sem=send_c.at[b], recv_sem=recv_c.at[b],
            device_id=device(lax.rem(u + PLANE, n)), device_id_type=MESH,
        )

    last = []
    for b in range(cuts):
        at = slice(b * 256, b * 256 + 256)

        @pl.when(level > 0)
        def _():
            chain(b).wait_recv()

        @pl.when(level == 0)
        def _():
            chain_in[b] = jnp.zeros((128, 256), chain_in.dtype)

        enter = chain_in[b].astype(F32)

        @pl.when(level < planes - 1)
        def _():
            chain_out[b] = (decs[0, 0:1, at] * enter + total[:, at]).astype(chain_out.dtype)
            chain(b).start()

        outbox[0, :, at] = enter.astype(outbox.dtype)
        for p in range(1, PLANE):
            outbox[p, :, at] = (decs[p, 0:1, at] * enter + parts[p, :, at]).astype(outbox.dtype)
        mine = pl.ds(pl.multiple_of(spot * LANES + b * 256, 256), 256)
        o_ref[:, mine] = outbox[spot, :, at]
        for k, peer in enumerate(peers):
            copy = pltpu.make_async_remote_copy(
                src_ref=outbox.at[peer, :, pl.ds(b * 256, 256)], dst_ref=o_ref.at[:, mine],
                send_sem=send_o.at[b * 3 + k], recv_sem=recv_o.at[b * 3 + k],
                device_id=device(level * PLANE + peer), device_id_type=MESH,
            )
            copy.start()
            last.append(copy)
    for copy in last:
        copy.wait()

    @pl.when(level < planes - 1)
    def _():
        for b in range(cuts):
            chain(b).wait_send()


def exchange(state, decay, n, rev):
    vmem = pl.BlockSpec(memory_space=pltpu.VMEM)
    dma = pltpu.SemaphoreType.DMA
    cuts = LANES // 256
    return pl.pallas_call(
        functools.partial(exchange_kernel, n, rev),
        out_shape=sds(128, INNER, state.dtype),
        in_specs=[vmem, vmem],
        out_specs=vmem,
        scratch_shapes=[
            pltpu.VMEM((PLANE, 128, LANES), state.dtype),
            pltpu.VMEM((PLANE, 8, LANES), F32),
            pltpu.VMEM((PLANE, 128, LANES), F32),
            pltpu.VMEM((PLANE, 8, LANES), F32),
            pltpu.VMEM((128, LANES), F32),
            pltpu.VMEM((cuts, 128, 256), state.dtype),
            pltpu.VMEM((cuts, 128, 256), state.dtype),
            pltpu.VMEM((PLANE, 128, LANES), state.dtype),
            dma((3,)), dma((3,)), dma((3,)), dma((3,)),
            dma((cuts,)), dma((cuts,)), dma((3 * cuts,)), dma((3 * cuts,)),
        ],
        compiler_params=pltpu.CompilerParams(
            collective_id=2 if rev else 1, has_side_effects=True, vmem_limit_bytes=32 * MIB
        ),
    )(state, decay)


def decay_block(later, earlier):
    return jnp.exp(jnp.minimum(later - earlier, 0.0))


def head_lanes(parts, i):
    at = (i // 2) * 128
    here = (iota((ROWS, 128), 1) < HEADDIM) if i % 2 == 0 else (iota((ROWS, 128), 1) >= HEADDIM)
    return [jnp.where(here, part[:, at : at + 128], jnp.zeros((), BF16)) for part in parts]


def mix_kernel(
    n, g_ref, step_ref, cum_ref, cumt_ref, val_ref, gate_ref, c_ref, car_ref, lp_ref, gain_ref,
    y_ref, low_ref, owned_ref, gated_ref, sum_ref,
):
    j = pl.program_id(0)
    heads = expander(j)
    cum = dot_nn(cum_ref[...], heads)
    values = val_ref[...]
    scaled = split2(values * dot_nn(step_ref[...], heads))
    car_high, car_rest = split2(car_ref[...])
    across = dot_nn(c_ref[...], jnp.concatenate([car_high, car_high, car_rest], axis=0))
    y = jnp.exp(cum) * across + lp_ref[0:1, :] * values
    sides = []
    for pair in range(WIDE // 128):
        top = jnp.zeros((HALF, 128), F32)
        bottom = jnp.zeros((HALF, 128), F32)
        for i in (2 * pair, 2 * pair + 1):
            row = cumt_ref[pl.ds((WIDE // HEADDIM) * j + i, 1), :]
            column = cum[:, i * HEADDIM : i * HEADDIM + 1]
            part = head_lanes(scaled, i)
            upper = split2(g_ref[0:HALF, 0:HALF] * decay_block(column[0:HALF], row[:, 0:HALF]))
            top = top + fine(dot_nn, upper, [v[0:HALF] for v in part])
            lower = split2(g_ref[HALF:ROWS, :] * decay_block(column[HALF:ROWS], row))
            bottom = bottom + fine(dot_nn, lower, part)
        sides.append(jnp.concatenate([top, bottom], axis=0))
    y = y + jnp.concatenate(sides, axis=1)
    y_ref[...] = y
    gate = gate_ref[...]
    gated = y * (gate * sigmoid(gate))
    gated_ref[j] = gated

    @pl.when(j == 0)
    def _():
        sum_ref[...] = jnp.zeros_like(sum_ref)

    sum_ref[...] += gated * gated

    @pl.when(j == STEPS - 1)
    def _():
        mean = jnp.sum(sum_ref[...], axis=1, keepdims=True) * (1.0 / INNER)
        scale = lax.rsqrt(mean + EPS)
        for k in range(STEPS):
            at = slice(k * WIDE, k * WIDE + WIDE)
            low_ref[:, at] = (gated_ref[k] * scale * gain_ref[1:2, at]).astype(BF16)
        width = INNER // n
        for q in range(n):
            to = (q % PLANE) * LANES + (q // PLANE) * width
            owned_ref[:, to : to + width] = low_ref[:, q * width : (q + 1) * width]


def mix(g, step, cum, cumt, values, proj, c, carried, lp, n):
    return pl.pallas_call(
        functools.partial(mix_kernel, n),
        grid=(STEPS,),
        in_specs=[
            whole((ROWS, ROWS)), whole((ROWS, 384)), whole((ROWS, 384)), whole((128, ROWS)),
            lanes(ROWS), lanes(ROWS), whole((ROWS, 384)), lanes(128), lanes(8),
            whole((8, INNER)),
        ],
        out_specs=[lanes(ROWS), whole((ROWS, INNER)), whole((ROWS, INNER))],
        out_shape=[sds(ROWS, INNER, F32), sds(ROWS, INNER, BF16), sds(ROWS, INNER, BF16)],
        scratch_shapes=[pltpu.VMEM((STEPS, ROWS, WIDE), F32), pltpu.VMEM((ROWS, WIDE), F32)],
        compiler_params=grid_params(),
        cost_estimate=pl.CostEstimate(flops=3 * 10**9, bytes_accessed=14 * MIB, transcendentals=4 * 10**6),
    )(g, step, cum, cumt, values, proj, c, carried, lp, lp)


def gate_back_kernel(
    dg_ref, y_ref, gate_ref, cum_ref, ct_ref, lp_ref, dy_ref, dgate_ref, gain_ref, dcar_ref,
    dg_all, y_all, gate_all, square_acc, cross_acc,
):
    phase, j = pl.program_id(0), pl.program_id(1)

    @pl.when(jnp.logical_and(phase == 0, j == 0))
    def _():
        square_acc[...] = jnp.zeros_like(square_acc)
        cross_acc[...] = jnp.zeros_like(cross_acc)

    @pl.when(phase == 0)
    def _():
        dg, y, gate = dg_ref[...], y_ref[...], gate_ref[...]
        dg_all[j], y_all[j], gate_all[j] = dg, y, gate
        gated = y * (gate * sigmoid(gate))
        square_acc[...] += gated * gated
        cross_acc[...] += dg * lp_ref[1:2, :] * gated

    @pl.when(phase == 1)
    def _():
        r = lax.rsqrt(jnp.sum(square_acc[...], axis=1, keepdims=True) * (1.0 / INNER) + EPS)
        m = jnp.sum(cross_acc[...], axis=1, keepdims=True) * (1.0 / INNER) * r * r
        dg, y, gate = dg_all[j], y_all[j], gate_all[j]
        s = sigmoid(gate)
        silu = gate * s
        gated = y * silu
        gain_ref[...] = jnp.broadcast_to(jnp.sum(dg * gated * r, axis=0, keepdims=True), (8, WIDE))
        d_gated = r * (dg * lp_ref[1:2, :] - gated * m)
        dy = d_gated * silu
        dy_ref[...] = dy
        dgate_ref[...] = (d_gated * y * (s + silu * (1.0 - s))).astype(BF16)
        cum = dot_nn(cum_ref[...], expander(j))
        dcar_ref[...] = dot_nn(ct_ref[...], (dy * jnp.exp(cum)).astype(BF16)).astype(BF16)


def gate_back(dg, y, proj, cum, ct, lp, sources=(), collective_id=None):
    def first(rows):
        return pl.BlockSpec((rows, WIDE), lambda p, j: (0, j * (1 - p) + (STEPS - 1) * p))

    def second(rows):
        return pl.BlockSpec((rows, WIDE), lambda p, j: (0, j * p))

    def both(shape):
        return pl.BlockSpec(shape, lambda p, j: (0, 0))

    def at_step(phase, j):
        return jnp.logical_and(pl.program_id(0) == phase, pl.program_id(1) == j)

    kept = pltpu.VMEM((STEPS, ROWS, WIDE), F32)
    specs, shapes, sems = spread_specs(sources)
    body = spreading(
        gate_back_kernel, 6, 4, len(sources), lambda: at_step(0, 0), lambda: at_step(1, STEPS - 1)
    )
    return pl.pallas_call(
        body,
        grid=(2, STEPS),
        in_specs=[
            first(ROWS), first(ROWS), first(ROWS), both((ROWS, 384)), both((128, ROWS)),
            pl.BlockSpec((8, WIDE), lambda p, j: (0, j)), *specs,
        ],
        out_specs=[second(ROWS), second(ROWS), second(8), second(128), *specs],
        out_shape=[
            sds(ROWS, INNER, F32), sds(ROWS, INNER, BF16), sds(8, INNER, F32), sds(128, INNER, BF16), *shapes,
        ],
        scratch_shapes=[kept, kept, kept, pltpu.VMEM((ROWS, WIDE), F32), pltpu.VMEM((ROWS, WIDE), F32), *sems],
        compiler_params=call_params(collective_id),
        cost_estimate=pl.CostEstimate(flops=10**9, bytes_accessed=16 * MIB, transcendentals=2 * 10**6),
    )(dg, y, proj, cum, ct, lp, *sources)


def core_back_kernel(
    x_ref, bc_ref, raw_ref, xh_ref, bch_ref, xw_ref, bcw_ref, hp_ref,
    step_ref, cum_ref, cumt_ref, gt_ref, b_ref, c_ref, y_ref, dy_ref, car_ref, late_ref, lp_ref,
    dx_ref, tail_ref, head_ref, taps_ref, hg_ref,
    dgt_acc, dc_acc, db_acc, dcum_acc, dstep_acc, rows_acc,
):
    j = pl.program_id(0)

    @pl.when(j == 0)
    def _():
        for acc in (dgt_acc, dc_acc, db_acc, dcum_acc, dstep_acc, rows_acc):
            acc[...] = jnp.zeros_like(acc)

    @pl.when(j < STEPS)
    def _():
        ext = extended(x_ref[...], xh_ref[...])
        pre = conv_pre(ext, xw_ref[...])
        sig = sigmoid(pre)
        values = pre * sig
        heads, to_heads = expander(j), collector(j)
        step = dot_nn(step_ref[...], heads)
        cum = dot_nn(cum_ref[...], heads)
        last = cum[ROWS - 1 : ROWS]
        scaled = values * step
        scaled_parts = split2(scaled)
        dy = dy_ref[...]
        dy_parts = split2(dy)
        sides = []
        for pair in range(WIDE // 128):
            top = jnp.zeros((HALF, 128), F32)
            bottom = jnp.zeros((HALF, 128), F32)
            at = slice(pair * 128, pair * 128 + 128)
            own = [part[:, at] for part in scaled_parts]
            for i in (2 * pair, 2 * pair + 1):
                row = cumt_ref[pl.ds((WIDE // HEADDIM) * j + i, 1), :]
                column = cum[:, i * HEADDIM : i * HEADDIM + 1]
                part = head_lanes(dy_parts, i)
                decay = decay_block(row, column[0:HALF])
                top = top + fine(dot_nn, split2(gt_ref[0:HALF, :] * decay), part)
                dgt_acc[0:HALF, :] += fine(dot_nt, [v[0:HALF] for v in own], part) * decay
                decay = decay_block(row[:, HALF:ROWS], column[HALF:ROWS])
                late_part = [v[HALF:ROWS] for v in part]
                bottom = bottom + fine(dot_nn, split2(gt_ref[HALF:ROWS, HALF:ROWS] * decay), late_part)
                dgt_acc[HALF:ROWS, HALF:ROWS] += fine(dot_nt, [v[HALF:ROWS] for v in own], late_part) * decay
            sides.append(jnp.concatenate([top, bottom], axis=0))
        car, late = car_ref[...], late_ref[...]
        to_end = jnp.exp(last - cum)
        d_ended = dot_nn(b_ref[:, 0:128], late)
        ended = scaled * to_end
        dc_acc[...] += fine(dot_nt, split2(dy * jnp.exp(cum)), split2(car))
        db_acc[...] += dot_nt(ended.astype(BF16), late)
        d_total = jnp.concatenate(sides, axis=1) + to_end * d_ended
        skip_w = lp_ref[0:1, :]
        dcum_acc[...] += collect(dy * (y_ref[...] - skip_w * values) - scaled * d_total, to_heads)
        dstep_acc[...] += collect(d_total * values, to_heads)
        at_last = jnp.exp(last) * jnp.sum(late.astype(F32) * car, axis=0, keepdims=True)
        at_last = at_last + jnp.sum(ended * d_ended, axis=0, keepdims=True)
        skip = jnp.sum(dy * values, axis=0, keepdims=True)
        rows_acc[...] += collect(jnp.concatenate([at_last, skip, jnp.zeros((6, WIDE), F32)], axis=0), to_heads)
        d_pre = (skip_w * dy + step * d_total) * (sig + values * (1.0 - sig))
        taps_ref[...] = tap_grads(d_pre, ext)
        head_ref[...] = d_pre[0:8]
        d_conv = conv_back(d_pre, xw_ref[...])
        dx_ref[...] = d_conv.astype(BF16)
        tail_ref[...] = d_conv[ROWS - 16 : ROWS]

    @pl.when(j == STEPS)
    def _():
        seen = iota((ROWS, ROWS), 1) >= iota((ROWS, ROWS), 0)
        d_gt = split2(jnp.where(seen, dgt_acc[...], 0.0))
        d_c = dc_acc[...] + fine(dot_tn, d_gt, halves(b_ref))
        d_b = db_acc[...] + fine(dot_nn, d_gt, halves(c_ref))
        ext_bc = extended(bc_ref[...], bch_ref[...])
        pre_bc = conv_pre(ext_bc, bcw_ref[...])
        sig_bc = sigmoid(pre_bc)
        d_pre_bc = jnp.concatenate([d_b, d_c], axis=1) * (sig_bc + pre_bc * sig_bc * (1.0 - sig_bc))
        taps_ref[...] = tap_grads(d_pre_bc, ext_bc)
        head_ref[...] = d_pre_bc[0:8]
        d_conv_bc = conv_back(d_pre_bc, bcw_ref[...])
        dx_ref[...] = d_conv_bc.astype(BF16)
        tail_ref[...] = d_conv_bc[ROWS - 16 : ROWS]

    @pl.when(j == STEPS + 1)
    def _():
        raw, step_all, rate = step_parts(raw_ref, hp_ref)
        end = iota((ROWS, 128), 0) == ROWS - 1
        d_cum_all = dcum_acc[...] + jnp.where(end, rows_acc[0:1, :], 0.0)
        d_log = exact_left(triangle(False), d_cum_all)
        d_step = dstep_acc[...] + rate * d_log
        d_raw = jnp.where(iota((ROWS, 128), 1) < HEADS, d_step * sigmoid(raw), 0.0)
        dx_ref[...] = jnp.concatenate([d_raw, jnp.zeros((ROWS, WIDE - 128), F32)], axis=1).astype(BF16)
        tail_ref[...] = dx_ref[ROWS - 16 : ROWS, :].astype(F32)
        head_ref[...] = jnp.zeros_like(head_ref)
        taps_ref[...] = jnp.zeros_like(taps_ref)
        hg_ref[...] = jnp.concatenate(
            [
                jnp.sum(d_raw, axis=0, keepdims=True),
                jnp.sum(d_log * rate * step_all, axis=0, keepdims=True),
                rows_acc[1:2, :],
                jnp.zeros((5, 128), F32),
            ],
            axis=0,
        )


def core_back(proj, halo, taps, hp, step, cum, cumt, gt, b, c, y, dy, carried, late, lp, sources=(), collective_id=None):
    acc = pltpu.VMEM((ROWS, 128), F32)

    def lanes(rows, first=0):
        return pl.BlockSpec((rows, WIDE), lambda j: (0, first + jnp.minimum(j, STEPS - 1)))

    def out(rows):
        return pl.BlockSpec((rows, WIDE), lambda j: (0, j))

    specs, shapes, sems = spread_specs(sources)
    body = spreading(
        core_back_kernel, 19, 5, len(sources),
        lambda: pl.program_id(0) == 0, lambda: pl.program_id(0) == STEPS + 1,
    )
    return pl.pallas_call(
        body,
        grid=(STEPS + 2,),
        in_specs=[
            lanes(ROWS, STEPS), fixed(ROWS, 2 * STEPS), fixed(ROWS, 50, 128),
            lanes(8), fixed(8, STEPS), lanes(8), fixed(8, STEPS), whole((8, 128)),
            whole((ROWS, 384)), whole((ROWS, 384)), whole((128, ROWS)), whole((ROWS, ROWS)),
            whole((ROWS, 256)), whole((ROWS, 384)),
            lanes(ROWS), lanes(ROWS), lanes(128), lanes(128), lanes(8), *specs,
        ],
        out_specs=[out(ROWS), out(16), out(8), out(8), whole((8, 128)), *specs],
        out_shape=[
            sds(ROWS, REST, BF16), sds(16, REST, F32), sds(8, REST, F32), sds(8, REST, F32), sds(8, 128, F32), *shapes,
        ],
        scratch_shapes=[pltpu.VMEM((ROWS, ROWS), F32), acc, acc, acc, acc, pltpu.VMEM((8, 128), F32), *sems],
        compiler_params=call_params(collective_id),
        cost_estimate=pl.CostEstimate(flops=8 * 10**9, bytes_accessed=14 * MIB, transcendentals=5 * 10**6),
    )(
        proj, proj, proj, halo, halo, taps, taps, hp,
        step, cum, cumt, gt, b, c, y, dy, carried, late, lp, *sources,
    )


def row_copies(layer, gate, rest, gate_in, rest_in, sems, spot, base, core, mine):
    send_g, recv_g, send_r, recv_r = sems
    rows = gate_in.shape[1]
    copies = []
    for k in range(1 if mine else 0, PLANE):
        peer = lax.rem(spot + k, PLANE)
        block = pl.ds(pl.multiple_of(peer * rows, rows), rows)
        at = 2 * k + core
        for src, dst, send, recv in ((gate, gate_in, send_g, recv_g), (rest, rest_in, send_r, recv_r)):
            copies.append(
                pltpu.make_async_remote_copy(
                    src_ref=src.at[block], dst_ref=dst.at[2 * spot + core], send_sem=send.at[at],
                    recv_sem=recv.at[at], device_id=(layer, base + peer), device_id_type=MESH,
                )
            )
    return copies


def keep_rows(layer, gate, rest, gate_in, rest_in, spot):
    rows = gate_in.shape[1]
    block = pl.ds(pl.multiple_of(spot * rows, rows), rows)
    gate_in[2 * spot + layer] = gate[block, :]
    rest_in[2 * spot + layer] = rest[block, :]


def wait_rows(layer, gate, rest, gate_in, rest_in, sems, spot, base):
    for core in range(2):
        for copy in row_copies(layer, gate, rest, gate_in, rest_in, sems, spot, base, core, core == layer):
            copy.wait_recv()


def early_kernel(n, gate, rest, gate_in, rest_in, send_g, recv_g, send_r, recv_r):
    core, q = lax.axis_index("section"), lax.axis_index("seq")
    spot = lax.rem(q, PLANE)
    base = q - spot
    sems = (send_g, recv_g, send_r, recv_r)
    barrier = pltpu.get_barrier_semaphore()

    @pl.when(core == 1)
    def _():
        for k in range(PLANE):
            for other in range(2 if k else 1):
                to = (other, base + lax.rem(spot + k, PLANE))
                pl.semaphore_signal(barrier, inc=1, device_id=to, device_id_type=MESH)

    pl.semaphore_wait(barrier, PLANE - core)
    for side in range(2):

        @pl.when(core == side)
        def _():
            copies = row_copies(1, gate, rest, gate_in, rest_in, sems, spot, base, side, side == 1)
            for copy in copies:
                copy.start()
            if side:
                keep_rows(1, gate, rest, gate_in, rest_in, spot)
            for copy in copies:
                copy.wait_send()
            if side:
                wait_rows(1, gate, rest, gate_in, rest_in, sems, spot, base)


def settle_early(gate, rest, n):
    vmem = pl.BlockSpec(memory_space=pltpu.VMEM)
    dma = pltpu.SemaphoreType.DMA
    rows, eight = D // n, 2 * PLANE
    return pl.pallas_call(
        functools.partial(early_kernel, n),
        out_shape=[
            jax.ShapeDtypeStruct((eight, rows, gate.shape[1]), BF16),
            jax.ShapeDtypeStruct((eight, rows, rest.shape[1]), BF16),
        ],
        in_specs=[vmem, vmem],
        out_specs=[vmem, vmem],
        scratch_shapes=[dma((eight,)), dma((eight,)), dma((eight,)), dma((eight,))],
        compiler_params=pltpu.CompilerParams(collective_id=8, has_side_effects=True, vmem_limit_bytes=32 * MIB),
    )(gate, rest)


def settle_kernel(
    n, gate, rest, gate_1, rest_1, ow0, ow1, a0, a1, d0, d1, gin_ref, gout_ref, acts_ref, grads_ref,
    gate_in, rest_in, out_in, send_g, recv_g, send_r, recv_r, send_o, recv_o, send_x, recv_x, keep_x,
):
    core = lax.axis_index("section")
    q = lax.axis_index("seq")
    spot = lax.rem(q, PLANE)
    base = q - spot
    sems = (send_g, recv_g, send_r, recv_r)
    barrier = pltpu.get_barrier_semaphore()
    for k in range(PLANE):
        for flip in range(2):
            if k or flip:
                to = (core ^ flip, base + lax.rem(spot + k, PLANE))
                pl.semaphore_signal(barrier, inc=1, device_id=to, device_id_type=MESH)
    pl.semaphore_wait(barrier, 2 * PLANE - 1)

    def fill(gates, rests):
        for p in range(2 * PLANE):
            wide = gates.shape[2]
            gin_ref[:, p * wide : p * wide + wide] = gates[p].astype(F32)
            wide = rests.shape[2]
            at = INNER + p * wide
            width = min(wide, PROJ - at)
            gin_ref[:, at : at + width] = rests[p].astype(F32)[:, :width]

    def run(layer, outw, act, grad, away_act, away_grad, away_outw):
        rows = row_copies(0, gate, rest, gate_in, rest_in, sems, spot, base, layer, layer == 0)
        for copy in rows:
            copy.start()
        copies = []

        def send(src, dst, sems, at):
            copy = pltpu.make_async_remote_copy(
                src_ref=src, dst_ref=dst, send_sem=sems[0].at[at], recv_sem=sems[1].at[at],
                device_id=(1 - layer, q), device_id_type=MESH,
            )
            copy.start()
            copies.append(copy)

        for at, (own, away, dst) in enumerate(((grad, away_grad, grads_ref), (act, away_act, acts_ref))):
            send(away, dst.at[layer], (send_x, recv_x), at)
            copies.append(pltpu.make_async_copy(own, dst.at[layer], keep_x.at[at]))
            copies[-1].start()
        send(away_outw, out_in, (send_o, recv_o), 0)
        half = D // 2
        gout_ref[:, layer * half : layer * half + half] = outw[...].astype(F32)
        if layer:
            fill(gate_1, rest_1)
        else:
            keep_rows(0, gate, rest, gate_in, rest_in, spot)
        for copy in rows:
            copy.wait_send()
        if not layer:
            wait_rows(0, gate, rest, gate_in, rest_in, sems, spot, base)
            fill(gate_in, rest_in)
        for copy in copies:
            copy.wait()
        gout_ref[:, (1 - layer) * half : (1 - layer) * half + half] = out_in[...].astype(F32)

    @pl.when(core == 0)
    def _():
        run(0, ow0, a0, d0, a1, d1, ow1)

    @pl.when(core == 1)
    def _():
        run(1, ow1, a1, d1, a0, d0, ow0)


def settle(gate, rest, early, outs, acts, grads, n):
    vmem = pl.BlockSpec(memory_space=pltpu.VMEM)
    anywhere = pl.BlockSpec(memory_space=pl.ANY)
    dma = pltpu.SemaphoreType.DMA
    rows = D // n
    eight = 2 * PLANE
    return pl.pallas_call(
        functools.partial(settle_kernel, n),
        out_shape=[
            sds(rows, PROJ, F32), sds(INNER // n, D, F32),
            jax.ShapeDtypeStruct((2, ROWS, D), BF16), jax.ShapeDtypeStruct((2, ROWS, D), F32),
        ],
        in_specs=[vmem] * 6 + [anywhere] * 4,
        out_specs=[vmem, vmem, anywhere, anywhere],
        scratch_shapes=[
            pltpu.VMEM((eight, rows, gate.shape[1]), BF16),
            pltpu.VMEM((eight, rows, rest.shape[1]), BF16),
            pltpu.VMEM((INNER // n, D // 2), BF16),
            dma((eight,)), dma((eight,)), dma((eight,)), dma((eight,)),
            dma((1,)), dma((1,)), dma((2,)), dma((2,)), dma((2,)),
        ],
        compiler_params=pltpu.CompilerParams(collective_id=3, has_side_effects=True, vmem_limit_bytes=40 * MIB),
    )(gate, rest, early[0], early[1], outs[0], outs[1], acts[0], acts[1], grads[0], grads[1])


def swap(value):
    return lax.ppermute(value, "section", [(0, 1), (1, 0)])


def shifted(value, distance, n):
    return lax.ppermute(value, "seq", [(i, i + distance) for i in range(n) if 0 <= i + distance < n])


def plane_route(k, n):
    return [(i, i - i % PLANE + (i + k) % PLANE) for i in range(n)]


def rms(value):
    return lax.rsqrt(jnp.mean(value * value, axis=-1, keepdims=True) + EPS)


def tied(value, *others):
    return lax.optimization_barrier((value, *others))[0]


def copies_of(value, n):
    return [value] + [lax.ppermute(value, "seq", plane_route(k, n)) for k in range(1, PLANE)]


def arrived(value, *lists):
    value, *rest = lax.optimization_barrier((value, *(copy for copies in lists for copy in copies)))
    return (value, *(jnp.stack(rest[k * PLANE : (k + 1) * PLANE]) for k in range(len(lists))))


def partial_grad(left, right):
    core = lax.axis_index("section")
    half = right.shape[2] // 2

    def part(side):
        cols = lax.dynamic_slice_in_dim(right, side * half, half, 2)
        return lax.dot_general(left, cols, (((0, 1), (0, 1)), ((), ())), preferred_element_type=F32)

    away = part(1 - core).astype(BF16)
    return (part(core) + swap(away).astype(F32)).astype(BF16)


def plane_rows(partial, n):
    columns = [[p + PLANE * z for z in range(n // PLANE)] for p in range(PLANE)]
    return lax.psum_scatter(partial, "seq", scatter_dimension=0, axis_index_groups=columns, tiled=True)


SIZES = [D, CONVD * CONV, CONVD, HEADS, HEADS, HEADS, INNER]


def split_small(flat):
    parts, at = [], 0
    for size in SIZES:
        parts.append(flat[at : at + size])
        at += size
    return parts


def unpack_params(flat):
    norm_g, conv_w, conv_b, dt_b, a_lg, skip_w, gate_g = split_small(flat)
    taps = jnp.concatenate(
        [conv_w.reshape(CONV, CONVD), conv_b[None], jnp.zeros((3, CONVD), F32)], axis=0
    )
    pad = jnp.zeros((128 - HEADS,), F32)
    hp = jnp.concatenate([dt_b, pad, a_lg, pad, jnp.zeros((6 * 128,), F32)]).reshape(8, 128)
    lp = jnp.concatenate(
        [jnp.repeat(skip_w, HEADDIM)[None], gate_g[None], jnp.zeros((6, INNER), F32)], axis=0
    )
    return norm_g, taps, hp, lp


def per_device(
    inputs, cotangent, norm_gain, in_weight, conv_weight, conv_bias, dt_bias, a_log, d_skip,
    gate_norm_gain, out_weight,
):
    n = lax.axis_size("seq")
    core = lax.axis_index("section")
    place = lax.axis_index("seq")
    first = core == 0
    own_in, own_out = in_weight[0].T, out_weight[0]
    other_in = swap(own_in)
    own_small = jnp.concatenate(
        [
            norm_gain[0], conv_weight[0].T.reshape(-1), conv_bias[0], dt_bias[0], a_log[0], d_skip[0],
            gate_norm_gain[0],
        ]
    )
    other_small = swap(own_small)
    flags = [(core == layer).astype(jnp.int32)[None] for layer in range(2)]
    params = [
        unpack_params(jnp.where(first, own_small, other_small)),
        unpack_params(jnp.where(first, other_small, own_small)),
    ]

    def mine(pair):
        return lax.dynamic_index_in_dim(pair, core, 0, keepdims=False)

    def normed_of(layer, h):
        return (h * rms(h) * params[layer][0]).astype(BF16)

    def project(layer, normed, before):
        proj, halo = project_mm(normed, normed_of(layer, before.astype(F32)), own_in, other_in, flags[layer], 1664)
        return proj, halo[8:, INNER : INNER + CONVD]

    def blocks(layer, proj, halo):
        _, taps, hp, _ = params[layer]
        return front(proj, halo, taps, hp)

    def finish(layer, h, proj, parts, carried):
        values, _, _, step, cum, cumt, _, c, _, g, _ = parts[:11]
        y, gated_low, owned = mix(g, step, cum, cumt, values, proj, c, carried, params[layer][3], n)
        return y, owned, gated_low

    def output(layer, h, gated_low):
        return (h + mm(gated_low, own_out, other_out, flags[layer], False, 768)).astype(BF16)

    x_0 = mine(inputs)
    before_0 = shifted(x_0[ROWS - 16 :], 1, n)
    d_out_1 = mine(cotangent)
    h_0 = x_0.astype(F32)
    normed_0 = normed_of(0, h_0)
    normed_0, lows_1 = arrived(normed_0, copies_of(d_out_1, n))
    proj_0, halo_0 = project(0, normed_0, before_0)
    other_out = swap(tied(own_out, proj_0))
    parts_0 = blocks(0, proj_0, halo_0)
    carried_0 = exchange(parts_0[1], parts_0[2], n, False)
    normeds_0 = copies_of(tied(normed_0, carried_0), n)
    y_0, owned_0, low_0 = finish(0, h_0, proj_0, parts_0, carried_0)
    act_0 = output(0, h_0, low_0)

    before_1 = shifted(act_0[ROWS - 16 :], 1, n)
    h_1 = act_0.astype(F32)
    normed_1 = normed_of(1, h_1)
    normeds_1 = copies_of(tied(normed_1, before_1), n)
    proj_1, halo_1 = project(1, normed_1, before_1)
    parts_1 = blocks(1, proj_1, halo_1)
    carried_1 = exchange(parts_1[1], parts_1[2], n, False)
    carried_1, normeds_0, normeds_1 = arrived(carried_1, normeds_0, normeds_1)
    y_1, owned_1, low_1 = finish(1, h_1, proj_1, parts_1, carried_1)

    def gate_side(layer, d_low, y, proj, parts, *spread):
        d_gated_low = mm(d_low, own_out, other_out, flags[layer], True, 1024)
        return gate_back(d_gated_low, y, proj, parts[4], parts[8], params[layer][3], *spread)

    def core_side(layer, proj, halo, parts, y, dy, carried, late, *spread):
        _, taps, hp, lp = params[layer]
        _, _, _, step, cum, cumt, b, c, _, _, gt = parts[:11]
        return core_back(proj, halo, taps, hp, step, cum, cumt, gt, b, c, y, dy, carried, late, lp, *spread)

    def conv_side(layer, back):
        rest, tail, head = back[:3]
        w = jnp.concatenate([params[layer][1], jnp.zeros((8, REST - CONVD), F32)], axis=1)
        a = shifted(head, -1, n)
        fix = jnp.concatenate(
            [
                jnp.zeros((13, REST), F32),
                w[0:1] * a[0:1],
                w[0:1] * a[1:2] + w[1:2] * a[0:1],
                w[0:1] * a[2:3] + w[1:2] * a[1:2] + w[2:3] * a[0:1],
            ],
            axis=0,
        )
        return lax.dynamic_update_slice(rest, (tail + fix).astype(BF16), (ROWS - 16, 0))

    def norm_side(layer, h, d_out, d_gate, rest):
        norm_g = params[layer][0]
        d_normed = back_mm(d_gate, rest, own_in, other_in, flags[layer], 512)
        r = rms(h)
        v = d_normed * norm_g
        d_h = d_out + r * (v - h * (r * r * jnp.mean(v * h, axis=-1, keepdims=True)))
        return d_h, jnp.sum(d_normed * h * r, axis=0)

    def small_of(norm_gain_grad, back, gate_gain):
        taps_all, heads = back[3][:, :CONVD], back[4]
        return jnp.concatenate(
            [
                norm_gain_grad, taps_all[:CONV].reshape(-1), taps_all[CONV],
                heads[0, :HEADS], heads[1, :HEADS], heads[2, :HEADS], gate_gain[0],
            ]
        )

    dy_1, d_gate_1, gain_1, d_carried_1, gateds_0 = gate_side(
        1, tied(d_out_1, carried_1), y_1, proj_1, parts_1, (owned_0,), 4
    )
    late_1 = exchange(d_carried_1, parts_1[2], n, True)
    back_1 = core_side(
        1, proj_1, halo_1, parts_1, y_1, dy_1, carried_1, late_1, (d_gate_1, owned_1), 5
    )
    gates_1, gateds_1 = back_1[5:]
    outw_1 = partial_grad(gateds_1, lows_1)
    gatew_1 = partial_grad(normeds_1, gates_1)
    rest_1 = conv_side(1, back_1)
    rest_1 = tied(rest_1, outw_1, gatew_1)
    outw_1, gatew_1 = plane_rows(outw_1, n), plane_rows(gatew_1, n)
    d_1, ng_1 = norm_side(1, h_1, d_out_1.astype(F32), d_gate_1, rest_1)

    d_out_0 = d_1.astype(BF16)
    dy_0, d_gate_0, gain_0, d_carried_0, rests_1 = gate_side(0, d_out_0, y_0, proj_0, parts_0, (rest_1,), 6)
    restw_1 = partial_grad(normeds_1, rests_1)
    late_0 = exchange(tied(d_carried_0, restw_1, outw_1, gatew_1), parts_0[2], n, True)
    restw_1 = plane_rows(tied(restw_1, late_0), n)
    lows_0 = copies_of(tied(d_out_0, late_0), n)
    back_0 = core_side(
        0, proj_0, halo_0, parts_0, y_0, dy_0, carried_0, late_0, (d_gate_0,), 7
    )
    gates_0, lows_0 = arrived(back_0[5], lows_0)
    gatew_0 = partial_grad(normeds_0, gates_0)
    outw_0 = plane_rows(partial_grad(gateds_0, lows_0), n)
    rest_0 = conv_side(0, back_0)
    rest_0 = tied(rest_0, gatew_0)
    gatew_0 = plane_rows(gatew_0, n)
    spot = place % PLANE
    width = REST // PLANE
    pieces = [lax.dynamic_slice_in_dim(rest_0, (spot + k) % PLANE * width, width, 1) for k in range(PLANE)]
    rests_0 = pieces[:1] + [lax.ppermute(pieces[k], "seq", plane_route(k, n)) for k in range(1, PLANE)]
    d_0, ng_0 = norm_side(0, h_0, d_out_0.astype(F32), d_gate_0, rest_0)
    ng_0, rests_0 = arrived(ng_0, rests_0)
    restw_0 = partial_grad(normeds_0, rests_0)
    act_1 = output(1, h_1, tied(low_1, restw_0))
    early = settle_early(tied(gatew_1, restw_0), restw_1, n)
    restw_0 = plane_rows(restw_0, n)

    g_in, g_out, acts, input_grads = settle(
        gatew_0, restw_0, early, (outw_0, outw_1), (act_0, act_1), (d_0, d_1), n
    )
    small_0, small_1 = small_of(ng_0, back_0, gain_0), small_of(ng_1, back_1, gain_1)
    small = jnp.where(first, small_0, small_1) + swap(jnp.where(first, small_1, small_0))
    reach = 1
    while reach < n:
        small = small + lax.ppermute(small, "seq", [(i, i ^ reach) for i in range(n)])
        reach *= 2
    norm_g, conv_w, conv_b, dt_b, a_lg, skip_w, gate_g = split_small(small)

    def share(value):
        rows = value.shape[0] // n
        return lax.dynamic_slice_in_dim(value, place * rows, rows, 0)[None]

    conv_rows = CONVD // n
    conv_w = lax.dynamic_slice_in_dim(conv_w.reshape(CONV, CONVD), place * conv_rows, conv_rows, 1).T
    return (
        acts[None], input_grads[None], share(norm_g), g_in[None], conv_w[None], share(conv_b),
        dt_b[None], a_lg[None], skip_w[None], share(gate_g), g_out[None],
    )


def solution(mesh):
    in_specs = (
        P(None, "seq", None), P(None, "seq", None), P("section", None), P("section", None, None),
        P("section", None, None), P("section", None), P("section", None), P("section", None),
        P("section", None), P("section", None), P("section", None, None),
    )
    out_specs = (
        P("section", None, "seq", None), P("section", None, "seq", None), P("section", "seq"),
        P("section", "seq", None), P("section", "seq", None), P("section", "seq"), P("section", None),
        P("section", None), P("section", None), P("section", "seq"), P("section", "seq", None),
    )
    return jax.shard_map(per_device, mesh=mesh, in_specs=in_specs, out_specs=out_specs, check_vma=False)
```

```python
import functools

import jax
import jax.numpy as jnp
from jax import lax
from jax.experimental import pallas as pl
from jax.experimental.pallas import tpu as pltpu
from jax.sharding import PartitionSpec as P

D = 1536
INNER = 3072
STATE = 128
HEADS = 48
HEADDIM = 64
CONV = 4
CONVD = 3328
PROJ = 6448
ROWS = 256
WIDE = 256
STEPS = INNER // WIDE
HALF = ROWS // 2
PLANE = 4
LANES = INNER // PLANE
REST = 3584
EPS = 1e-05
MIB = 2**20
MESH = pl.DeviceIdType.MESH
F32 = jnp.float32
BF16 = jnp.bfloat16


def dot_nn(a, b):
    return lax.dot_general(a, b, (((1,), (0,)), ((), ())), preferred_element_type=F32)


def dot_tn(a, b):
    return lax.dot_general(a, b, (((0,), (0,)), ((), ())), preferred_element_type=F32)


def dot_nt(a, b):
    return lax.dot_general(a, b, (((1,), (1,)), ((), ())), preferred_element_type=F32)


def split3(v):
    high = v.astype(BF16)
    rest = v - high.astype(F32)
    mid = rest.astype(BF16)
    return high, mid, (rest - mid.astype(F32)).astype(BF16)


def split2(v):
    high = v.astype(BF16)
    return high, (v - high.astype(F32)).astype(BF16)


def fine(dot, a, b):
    return dot(a[0], b[0]) + (dot(a[0], b[1]) + dot(a[1], b[0]))


def halves(ref):
    return ref[:, 0:128], ref[:, 128:256]


def parts3(v):
    return jnp.concatenate(split3(v), axis=1)


def exact_left(ones, v):
    a, b, c = split3(v)
    return dot_nn(ones, a) + (dot_nn(ones, b) + dot_nn(ones, c))


def iota(shape, dim):
    return lax.broadcasted_iota(jnp.int32, shape, dim)


def expander(step):
    head_of = (WIDE // HEADDIM) * step + lax.shift_right_logical(iota((128, WIDE), 1), 6)
    ones = (iota((128, WIDE), 0) == head_of).astype(F32).astype(BF16)
    return jnp.concatenate([ones, ones, ones], axis=0)


def collector(step):
    head_of = (WIDE // HEADDIM) * step + lax.shift_right_logical(iota((WIDE, 128), 0), 6)
    return (iota((WIDE, 128), 1) == head_of).astype(F32).astype(BF16)


def collect(v, ones):
    a, b, c = split3(v)
    return dot_nn(a, ones) + (dot_nn(b, ones) + dot_nn(c, ones))


def triangle(lower):
    rows, cols = iota((ROWS, ROWS), 0), iota((ROWS, ROWS), 1)
    return ((rows >= cols) if lower else (rows <= cols)).astype(F32).astype(BF16)


def sigmoid(v):
    return 0.5 * jnp.tanh(0.5 * v) + 0.5


def extended(block, halo):
    return jnp.concatenate([halo, block], axis=0)


def conv_pre(ext, taps):
    out = taps[4:5] + taps[0:1] * ext[5 : 5 + ROWS]
    for k in range(1, CONV):
        out = out + taps[k : k + 1] * ext[5 + k : 5 + k + ROWS]
    return out


def conv_back(d_pre, taps):
    ext = jnp.concatenate([d_pre, jnp.zeros((8, d_pre.shape[1]), F32)], axis=0)
    out = taps[3:4] * d_pre
    for k in range(CONV - 1):
        out = out + taps[k : k + 1] * ext[3 - k : 3 - k + ROWS]
    return out


def tap_grads(d_pre, ext):
    rows = [jnp.sum(d_pre * ext[5 + k : 5 + k + ROWS], axis=0, keepdims=True) for k in range(CONV)]
    rows.append(jnp.sum(d_pre, axis=0, keepdims=True))
    rows.append(jnp.zeros((3, d_pre.shape[1]), F32))
    return jnp.concatenate(rows, axis=0)


def step_parts(raw_ref, hp_ref):
    real = iota((ROWS, 128), 1) < HEADS
    raw = jnp.where(real, raw_ref[...], 0.0) + hp_ref[0:1, :]
    step = jnp.maximum(raw, 0.0) + jnp.log1p(jnp.exp(-jnp.abs(raw)))
    step = jnp.where(real, step, 0.0)
    rate = jnp.where(real[0:1], -jnp.exp(hp_ref[1:2, :]), 0.0)
    return raw, step, rate


def mm_kernel(flag_ref, x_ref, own_ref, other_ref, o_ref, *, nt):
    dot = dot_nt if nt else dot_nn

    @pl.when(flag_ref[0] == 1)
    def _():
        o_ref[...] = dot(x_ref[...], own_ref[...])

    @pl.when(flag_ref[0] == 0)
    def _():
        o_ref[...] = dot(x_ref[...], other_ref[...])


def mm(x, own, other, flag, nt, tile):
    rows, depth = x.shape
    width = own.shape[0] if nt else own.shape[1]
    block = (tile, depth) if nt else (depth, tile)

    def place(j, keep):
        return (j * keep, 0) if nt else (0, j * keep)

    return pl.pallas_call(
        functools.partial(mm_kernel, nt=nt),
        grid_spec=pltpu.PrefetchScalarGridSpec(
            num_scalar_prefetch=1,
            grid=(pl.cdiv(width, tile),),
            in_specs=[
                pl.BlockSpec((rows, depth), lambda j, f: (0, 0)),
                pl.BlockSpec(block, lambda j, f: place(j, f[0])),
                pl.BlockSpec(block, lambda j, f: place(j, 1 - f[0])),
            ],
            out_specs=pl.BlockSpec((rows, tile), lambda j, f: (0, j)),
        ),
        out_shape=jax.ShapeDtypeStruct((rows, width), F32),
        compiler_params=pltpu.CompilerParams(vmem_limit_bytes=48 * MIB),
        cost_estimate=pl.CostEstimate(
            flops=2 * rows * depth * width, bytes_accessed=2 * depth * width, transcendentals=0
        ),
    )(flag, x, own, other)


def spread_copies(pairs, sems):
    send, recv, keep = sems
    section, q = lax.axis_index("section"), lax.axis_index("seq")
    spot = lax.rem(q, PLANE)
    base = q - spot
    away, own = [], []
    for at, (src, dst) in enumerate(pairs):
        width = dst.shape[2]
        for k in range(PLANE):
            peer = lax.rem(spot + k, PLANE)
            part = src.at[:, pl.ds(pl.multiple_of(peer * width, 128), width)]
            if k:
                away.append(
                    pltpu.make_async_remote_copy(
                        src_ref=part, dst_ref=dst.at[k], send_sem=send.at[3 * at + k - 1],
                        recv_sem=recv.at[3 * at + k - 1], device_id=(section, base + peer), device_id_type=MESH,
                    )
                )
            else:
                own.append(pltpu.make_async_copy(part, dst.at[0], keep.at[at]))
    return away, own


def spread_start(pairs, sems):
    section, q = lax.axis_index("section"), lax.axis_index("seq")
    spot = lax.rem(q, PLANE)
    barrier = pltpu.get_barrier_semaphore()
    for k in range(1, PLANE):
        peer = q - spot + lax.rem(spot + k, PLANE)
        pl.semaphore_signal(barrier, inc=1, device_id=(section, peer), device_id_type=MESH)
    pl.semaphore_wait(barrier, PLANE - 1)
    away, own = spread_copies(pairs, sems)
    for copy in away + own:
        copy.start()


def spread_wait(pairs, sems):
    away, own = spread_copies(pairs, sems)
    for copy in away + own:
        copy.wait()


def spread_specs(sources):
    anywhere = pl.BlockSpec(memory_space=pl.ANY)
    shapes = [jax.ShapeDtypeStruct((PLANE, v.shape[0], v.shape[1] // PLANE), v.dtype) for v in sources]
    dma = pltpu.SemaphoreType.DMA
    sems = [dma((3 * len(sources),)), dma((3 * len(sources),)), dma((len(sources),))] if sources else []
    return [anywhere] * len(sources), shapes, sems


def spreading(body, n_in, n_out, count, first, last):
    if not count:
        return body

    def kernel(*refs):
        ins, rest = refs[: n_in + count], refs[n_in + count :]
        outs, scratch = rest[: n_out + count], rest[n_out + count :]
        pairs = list(zip(ins[n_in:], outs[n_out:]))
        sems = scratch[-3:]

        @pl.when(first())
        def _():
            spread_start(pairs, sems)

        body(*ins[:n_in], *outs[:n_out], *scratch[:-3])

        @pl.when(last())
        def _():
            spread_wait(pairs, sems)

    return kernel


def call_params(collective_id):
    if collective_id is None:
        return grid_params()
    return pltpu.CompilerParams(
        vmem_limit_bytes=48 * MIB, collective_id=collective_id, has_side_effects=True
    )


def project_kernel(flag_ref, x_ref, own_ref, other_ref, o_ref, halo_ref):
    def product(w_ref):
        both = dot_nt(x_ref[...], w_ref[...])
        o_ref[...] = both[0:ROWS]
        halo_ref[...] = both[ROWS : ROWS + 16]

    @pl.when(flag_ref[0] == 1)
    def _():
        product(own_ref)

    @pl.when(flag_ref[0] == 0)
    def _():
        product(other_ref)


def project_mm(x, before, own, other, flag, tile):
    rows, depth = x.shape
    width = own.shape[0]
    x = jnp.concatenate([x, before], axis=0)
    return pl.pallas_call(
        project_kernel,
        grid_spec=pltpu.PrefetchScalarGridSpec(
            num_scalar_prefetch=1,
            grid=(pl.cdiv(width, tile),),
            in_specs=[
                pl.BlockSpec((rows + 16, depth), lambda j, f: (0, 0)),
                pl.BlockSpec((tile, depth), lambda j, f: (j * f[0], 0)),
                pl.BlockSpec((tile, depth), lambda j, f: (j * (1 - f[0]), 0)),
            ],
            out_specs=[
                pl.BlockSpec((rows, tile), lambda j, f: (0, j)),
                pl.BlockSpec((16, tile), lambda j, f: (0, j)),
            ],
        ),
        out_shape=[sds(rows, width, F32), sds(16, width, F32)],
        compiler_params=pltpu.CompilerParams(vmem_limit_bytes=48 * MIB),
        cost_estimate=pl.CostEstimate(
            flops=2 * rows * depth * width, bytes_accessed=2 * depth * width, transcendentals=0
        ),
    )(flag, x, own, other)


def back_kernel(flag_ref, gate_ref, rest_ref, own_ref, other_ref, o_ref):
    def product(w_ref):
        o_ref[...] = dot_nn(gate_ref[...], w_ref[0:INNER, :]) + dot_nn(
            rest_ref[:, 0 : PROJ - INNER], w_ref[INNER:PROJ, :]
        )

    @pl.when(flag_ref[0] == 1)
    def _():
        product(own_ref)

    @pl.when(flag_ref[0] == 0)
    def _():
        product(other_ref)


def back_mm(gate, rest, own, other, flag, tile):
    return pl.pallas_call(
        back_kernel,
        grid_spec=pltpu.PrefetchScalarGridSpec(
            num_scalar_prefetch=1,
            grid=(D // tile,),
            in_specs=[
                pl.BlockSpec((ROWS, INNER), lambda j, f: (0, 0)),
                pl.BlockSpec((ROWS, REST), lambda j, f: (0, 0)),
                pl.BlockSpec((PROJ, tile), lambda j, f: (0, j * f[0])),
                pl.BlockSpec((PROJ, tile), lambda j, f: (0, j * (1 - f[0]))),
            ],
            out_specs=pl.BlockSpec((ROWS, tile), lambda j, f: (0, j)),
        ),
        out_shape=sds(ROWS, D, F32),
        compiler_params=pltpu.CompilerParams(vmem_limit_bytes=48 * MIB),
        cost_estimate=pl.CostEstimate(
            flops=2 * ROWS * D * PROJ, bytes_accessed=2 * D * PROJ, transcendentals=0
        ),
    )(flag, gate, rest, own, other)


def front_kernel(
    x_ref, bc_ref, raw_ref, xh_ref, bch_ref, xw_ref, bcw_ref, hp_ref,
    val_ref, state_ref, dec_ref, step_ref, cum_ref, cumt_ref, b_ref, c_ref, ct_ref, g_ref, gt_ref, bt_ref,
):
    j = pl.program_id(0)

    @pl.when(j == 0)
    def _():
        _, step, rate = step_parts(raw_ref, hp_ref)
        step_ref[...] = parts3(step)
        cum = exact_left(triangle(True), rate * step)
        cum_ref[...] = parts3(cum)
        cumt_ref[...] = cum.T
        pre = conv_pre(extended(bc_ref[...], bch_ref[...]), bcw_ref[...])
        both = pre * sigmoid(pre)
        b, c = both[:, 0:128], both[:, 128:256]
        b_low, c_low = split2(b), split2(c)
        b_ref[...] = jnp.concatenate(b_low, axis=1)
        c_ref[...] = jnp.concatenate([c_low[0], c_low[1], c_low[0]], axis=1)
        ct_ref[...] = c.T.astype(BF16)
        bt_ref[...] = jnp.concatenate(split2(b.T), axis=0)
        seen = iota((ROWS, ROWS), 0) >= iota((ROWS, ROWS), 1)
        g = jnp.where(seen, fine(dot_nt, c_low, b_low), 0.0)
        g_ref[...] = g
        gt_ref[...] = g.T

    pre = conv_pre(extended(x_ref[...], xh_ref[...]), xw_ref[...])
    values = pre * sigmoid(pre)
    val_ref[...] = values
    heads = expander(j)
    cum = dot_nn(cum_ref[...], heads)
    last = cum[ROWS - 1 : ROWS]
    high, rest = split2(values * dot_nn(step_ref[...], heads) * jnp.exp(last - cum))
    twice = dot_nn(bt_ref[...], high)
    state_ref[...] = twice[0:128] + twice[128:256] + dot_nn(bt_ref[0:128, :], rest)
    dec_ref[...] = jnp.broadcast_to(jnp.exp(last), (8, WIDE))


def whole(shape):
    return pl.BlockSpec(shape, lambda j: (0, 0))


def lanes(rows, first=0):
    return pl.BlockSpec((rows, WIDE), lambda j: (0, first + j))


def fixed(rows, at, width=WIDE):
    return pl.BlockSpec((rows, width), lambda j: (0, at))


def sds(rows, cols, dtype):
    return jax.ShapeDtypeStruct((rows, cols), dtype)


def grid_params():
    return pltpu.CompilerParams(vmem_limit_bytes=48 * MIB)


def front(proj, halo, taps, hp, sources=(), collective_id=None):
    square = (ROWS, ROWS)
    specs, shapes, sems = spread_specs(sources)
    body = spreading(
        front_kernel, 8, 11, len(sources), lambda: pl.program_id(0) == 0, lambda: pl.program_id(0) == STEPS - 1
    )
    return pl.pallas_call(
        body,
        grid=(STEPS,),
        in_specs=[
            lanes(ROWS, STEPS), fixed(ROWS, 2 * STEPS), fixed(ROWS, 50, 128),
            lanes(8), fixed(8, STEPS), lanes(8), fixed(8, STEPS), whole((8, 128)), *specs,
        ],
        out_specs=[
            lanes(ROWS), lanes(128), lanes(8),
            whole((ROWS, 384)), whole((ROWS, 384)), whole((128, ROWS)),
            whole((ROWS, 256)), whole((ROWS, 384)), whole((128, ROWS)), whole(square), whole(square), *specs,
        ],
        out_shape=[
            sds(ROWS, INNER, F32), sds(128, INNER, F32), sds(8, INNER, F32),
            sds(ROWS, 384, BF16), sds(ROWS, 384, BF16), sds(128, ROWS, F32),
            sds(ROWS, 256, BF16), sds(ROWS, 384, BF16), sds(128, ROWS, BF16), sds(*square, F32), sds(*square, F32),
            *shapes,
        ],
        scratch_shapes=[pltpu.VMEM((256, ROWS), BF16), *sems],
        compiler_params=call_params(collective_id),
        cost_estimate=pl.CostEstimate(flops=10**9, bytes_accessed=10 * MIB, transcendentals=10**6),
    )(proj, proj, proj, halo, halo, taps, taps, hp, *sources)


def exchange_kernel(
    n, rev, s_ref, d_ref, o_ref, inbox, dbox, parts, decs, total, chain_out, chain_in, outbox,
    send_a, recv_a, send_d, recv_d, send_c, recv_c, send_o, recv_o,
):
    planes = n // PLANE
    section = lax.axis_index("section")
    q = lax.axis_index("seq")
    u = n - 1 - q if rev else q
    spot, level = lax.rem(u, PLANE), u // PLANE

    def device(at):
        return (section, n - 1 - at if rev else at)

    peers = [lax.rem(spot + k, PLANE) for k in range(1, PLANE)]
    barrier = pltpu.get_barrier_semaphore()
    for peer in peers:
        pl.semaphore_signal(barrier, inc=1, device_id=device(level * PLANE + peer), device_id_type=MESH)

    @pl.when(level > 0)
    def _():
        pl.semaphore_signal(barrier, inc=1, device_id=device(u - PLANE), device_id_type=MESH)

    pl.semaphore_wait(barrier, PLANE - 1 + (level < planes - 1).astype(jnp.int32))

    def group(at):
        return pl.ds(pl.multiple_of(at * LANES, LANES), LANES)

    cuts = LANES // 256
    first = [[] for _ in range(cuts)]
    for k, peer in enumerate(peers):
        first[0].append(
            pltpu.make_async_remote_copy(
                src_ref=d_ref.at[:, group(peer)], dst_ref=dbox.at[spot],
                send_sem=send_d.at[k], recv_sem=recv_d.at[k],
                device_id=device(level * PLANE + peer), device_id_type=MESH,
            )
        )
    for b in range(cuts):
        for k, peer in enumerate(peers):
            part = pl.ds(pl.multiple_of(peer * LANES + b * 256, 256), 256)
            first[b].append(
                pltpu.make_async_remote_copy(
                    src_ref=s_ref.at[:, part], dst_ref=inbox.at[spot, :, pl.ds(b * 256, 256)],
                    send_sem=send_a.at[3 * b + k], recv_sem=recv_a.at[3 * b + k],
                    device_id=device(level * PLANE + peer), device_id_type=MESH,
                )
            )
    for copies in first:
        for copy in copies:
            copy.start()
    inbox[spot] = s_ref[:, group(spot)]
    dbox[spot] = d_ref[:, group(spot)]

    def chain(b):
        return pltpu.make_async_remote_copy(
            src_ref=chain_out.at[b], dst_ref=chain_in.at[b],
            send_sem=send_c.at[b], recv_sem=recv_c.at[b],
            device_id=device(lax.rem(u + PLANE, n)), device_id_type=MESH,
        )

    last = []
    for b in range(cuts):
        at = slice(b * 256, b * 256 + 256)
        for copy in first[b]:
            copy.wait()
        state = inbox[0, :, at].astype(F32)
        decay = dbox[0, 0:1, at]
        for p in range(1, PLANE):
            parts[p, :, at] = state
            decs[p, 0:1, at] = decay
            d = dbox[p, 0:1, at]
            state = d * state + inbox[p, :, at].astype(F32)
            decay = decay * d
        total[:, at] = state
        decs[0, 0:1, at] = decay

        @pl.when(level > 0)
        def _():
            chain(b).wait_recv()

        @pl.when(level == 0)
        def _():
            chain_in[b] = jnp.zeros((128, 256), chain_in.dtype)

        enter = chain_in[b].astype(F32)

        @pl.when(level < planes - 1)
        def _():
            chain_out[b] = (decs[0, 0:1, at] * enter + total[:, at]).astype(chain_out.dtype)
            chain(b).start()

        outbox[0, :, at] = enter.astype(outbox.dtype)
        for p in range(1, PLANE):
            outbox[p, :, at] = (decs[p, 0:1, at] * enter + parts[p, :, at]).astype(outbox.dtype)
        mine = pl.ds(pl.multiple_of(spot * LANES + b * 256, 256), 256)
        o_ref[:, mine] = outbox[spot, :, at]
        for k, peer in enumerate(peers):
            copy = pltpu.make_async_remote_copy(
                src_ref=outbox.at[peer, :, pl.ds(b * 256, 256)], dst_ref=o_ref.at[:, mine],
                send_sem=send_o.at[b * 3 + k], recv_sem=recv_o.at[b * 3 + k],
                device_id=device(level * PLANE + peer), device_id_type=MESH,
            )
            copy.start()
            last.append(copy)
    for copy in last:
        copy.wait()

    @pl.when(level < planes - 1)
    def _():
        for b in range(cuts):
            chain(b).wait_send()


def exchange(state, decay, n, rev):
    vmem = pl.BlockSpec(memory_space=pltpu.VMEM)
    dma = pltpu.SemaphoreType.DMA
    cuts = LANES // 256
    return pl.pallas_call(
        functools.partial(exchange_kernel, n, rev),
        out_shape=sds(128, INNER, state.dtype),
        in_specs=[vmem, vmem],
        out_specs=vmem,
        scratch_shapes=[
            pltpu.VMEM((PLANE, 128, LANES), state.dtype),
            pltpu.VMEM((PLANE, 8, LANES), F32),
            pltpu.VMEM((PLANE, 128, LANES), F32),
            pltpu.VMEM((PLANE, 8, LANES), F32),
            pltpu.VMEM((128, LANES), F32),
            pltpu.VMEM((cuts, 128, 256), state.dtype),
            pltpu.VMEM((cuts, 128, 256), state.dtype),
            pltpu.VMEM((PLANE, 128, LANES), state.dtype),
            dma((3 * cuts,)), dma((3 * cuts,)), dma((3,)), dma((3,)),
            dma((cuts,)), dma((cuts,)), dma((3 * cuts,)), dma((3 * cuts,)),
        ],
        compiler_params=pltpu.CompilerParams(
            collective_id=2 if rev else 1, has_side_effects=True, vmem_limit_bytes=32 * MIB
        ),
    )(state, decay)


def decay_block(later, earlier):
    return jnp.exp(jnp.minimum(later - earlier, 0.0))


def head_lanes(parts, i):
    at = (i // 2) * 128
    here = (iota((ROWS, 128), 1) < HEADDIM) if i % 2 == 0 else (iota((ROWS, 128), 1) >= HEADDIM)
    return [jnp.where(here, part[:, at : at + 128], jnp.zeros((), BF16)) for part in parts]


def mix_kernel(
    n, g_ref, step_ref, cum_ref, cumt_ref, val_ref, gate_ref, c_ref, car_ref, lp_ref, gain_ref,
    y_ref, low_ref, owned_ref, gated_ref, sum_ref,
):
    j = pl.program_id(0)
    heads = expander(j)
    cum = dot_nn(cum_ref[...], heads)
    values = val_ref[...]
    scaled = split2(values * dot_nn(step_ref[...], heads))
    car_high, car_rest = split2(car_ref[...])
    across = dot_nn(c_ref[...], jnp.concatenate([car_high, car_high, car_rest], axis=0))
    y = jnp.exp(cum) * across + lp_ref[0:1, :] * values
    sides = []
    for pair in range(WIDE // 128):
        top = jnp.zeros((HALF, 128), F32)
        bottom = jnp.zeros((HALF, 128), F32)
        for i in (2 * pair, 2 * pair + 1):
            row = cumt_ref[pl.ds((WIDE // HEADDIM) * j + i, 1), :]
            column = cum[:, i * HEADDIM : i * HEADDIM + 1]
            part = head_lanes(scaled, i)
            upper = split2(g_ref[0:HALF, 0:HALF] * decay_block(column[0:HALF], row[:, 0:HALF]))
            top = top + fine(dot_nn, upper, [v[0:HALF] for v in part])
            lower = split2(g_ref[HALF:ROWS, :] * decay_block(column[HALF:ROWS], row))
            bottom = bottom + fine(dot_nn, lower, part)
        sides.append(jnp.concatenate([top, bottom], axis=0))
    y = y + jnp.concatenate(sides, axis=1)
    y_ref[...] = y
    gate = gate_ref[...]
    gated = y * (gate * sigmoid(gate))
    gated_ref[j] = gated

    @pl.when(j == 0)
    def _():
        sum_ref[...] = jnp.zeros_like(sum_ref)

    sum_ref[...] += gated * gated

    @pl.when(j == STEPS - 1)
    def _():
        mean = jnp.sum(sum_ref[...], axis=1, keepdims=True) * (1.0 / INNER)
        scale = lax.rsqrt(mean + EPS)
        for k in range(STEPS):
            at = slice(k * WIDE, k * WIDE + WIDE)
            low_ref[:, at] = (gated_ref[k] * scale * gain_ref[1:2, at]).astype(BF16)
        width = INNER // n
        for q in range(n):
            to = (q % PLANE) * LANES + (q // PLANE) * width
            owned_ref[:, to : to + width] = low_ref[:, q * width : (q + 1) * width]


def mix(g, step, cum, cumt, values, proj, c, carried, lp, n):
    return pl.pallas_call(
        functools.partial(mix_kernel, n),
        grid=(STEPS,),
        in_specs=[
            whole((ROWS, ROWS)), whole((ROWS, 384)), whole((ROWS, 384)), whole((128, ROWS)),
            lanes(ROWS), lanes(ROWS), whole((ROWS, 384)), lanes(128), lanes(8),
            whole((8, INNER)),
        ],
        out_specs=[lanes(ROWS), whole((ROWS, INNER)), whole((ROWS, INNER))],
        out_shape=[sds(ROWS, INNER, F32), sds(ROWS, INNER, BF16), sds(ROWS, INNER, BF16)],
        scratch_shapes=[pltpu.VMEM((STEPS, ROWS, WIDE), F32), pltpu.VMEM((ROWS, WIDE), F32)],
        compiler_params=grid_params(),
        cost_estimate=pl.CostEstimate(flops=3 * 10**9, bytes_accessed=14 * MIB, transcendentals=4 * 10**6),
    )(g, step, cum, cumt, values, proj, c, carried, lp, lp)


def gate_back_kernel(
    dg_ref, y_ref, gate_ref, cum_ref, ct_ref, lp_ref, dy_ref, dgate_ref, gain_ref, dcar_ref,
    dg_all, y_all, gate_all, square_acc, cross_acc,
):
    phase, j = pl.program_id(0), pl.program_id(1)

    @pl.when(jnp.logical_and(phase == 0, j == 0))
    def _():
        square_acc[...] = jnp.zeros_like(square_acc)
        cross_acc[...] = jnp.zeros_like(cross_acc)

    @pl.when(phase == 0)
    def _():
        dg, y, gate = dg_ref[...], y_ref[...], gate_ref[...]
        dg_all[j], y_all[j], gate_all[j] = dg, y, gate
        gated = y * (gate * sigmoid(gate))
        square_acc[...] += gated * gated
        cross_acc[...] += dg * lp_ref[1:2, :] * gated

    @pl.when(phase == 1)
    def _():
        r = lax.rsqrt(jnp.sum(square_acc[...], axis=1, keepdims=True) * (1.0 / INNER) + EPS)
        m = jnp.sum(cross_acc[...], axis=1, keepdims=True) * (1.0 / INNER) * r * r
        dg, y, gate = dg_all[j], y_all[j], gate_all[j]
        s = sigmoid(gate)
        silu = gate * s
        gated = y * silu
        gain_ref[...] = jnp.broadcast_to(jnp.sum(dg * gated * r, axis=0, keepdims=True), (8, WIDE))
        d_gated = r * (dg * lp_ref[1:2, :] - gated * m)
        dy = d_gated * silu
        dy_ref[...] = dy
        dgate_ref[...] = (d_gated * y * (s + silu * (1.0 - s))).astype(BF16)
        cum = dot_nn(cum_ref[...], expander(j))
        dcar_ref[...] = dot_nn(ct_ref[...], (dy * jnp.exp(cum)).astype(BF16)).astype(BF16)


def gate_back(dg, y, proj, cum, ct, lp, sources=(), collective_id=None):
    def first(rows):
        return pl.BlockSpec((rows, WIDE), lambda p, j: (0, j * (1 - p) + (STEPS - 1) * p))

    def second(rows):
        return pl.BlockSpec((rows, WIDE), lambda p, j: (0, j * p))

    def both(shape):
        return pl.BlockSpec(shape, lambda p, j: (0, 0))

    def at_step(phase, j):
        return jnp.logical_and(pl.program_id(0) == phase, pl.program_id(1) == j)

    kept = pltpu.VMEM((STEPS, ROWS, WIDE), F32)
    specs, shapes, sems = spread_specs(sources)
    body = spreading(
        gate_back_kernel, 6, 4, len(sources), lambda: at_step(0, 0), lambda: at_step(1, STEPS - 1)
    )
    return pl.pallas_call(
        body,
        grid=(2, STEPS),
        in_specs=[
            first(ROWS), first(ROWS), first(ROWS), both((ROWS, 384)), both((128, ROWS)),
            pl.BlockSpec((8, WIDE), lambda p, j: (0, j)), *specs,
        ],
        out_specs=[second(ROWS), second(ROWS), second(8), second(128), *specs],
        out_shape=[
            sds(ROWS, INNER, F32), sds(ROWS, INNER, BF16), sds(8, INNER, F32), sds(128, INNER, BF16), *shapes,
        ],
        scratch_shapes=[kept, kept, kept, pltpu.VMEM((ROWS, WIDE), F32), pltpu.VMEM((ROWS, WIDE), F32), *sems],
        compiler_params=call_params(collective_id),
        cost_estimate=pl.CostEstimate(flops=10**9, bytes_accessed=16 * MIB, transcendentals=2 * 10**6),
    )(dg, y, proj, cum, ct, lp, *sources)


def core_back_kernel(
    x_ref, bc_ref, raw_ref, xh_ref, bch_ref, xw_ref, bcw_ref, hp_ref,
    step_ref, cum_ref, cumt_ref, gt_ref, b_ref, c_ref, y_ref, dy_ref, car_ref, late_ref, lp_ref,
    dx_ref, tail_ref, head_ref, taps_ref, hg_ref,
    dgt_acc, dc_acc, db_acc, dcum_acc, dstep_acc, rows_acc,
):
    j = pl.program_id(0)

    @pl.when(j == 0)
    def _():
        for acc in (dgt_acc, dc_acc, db_acc, dcum_acc, dstep_acc, rows_acc):
            acc[...] = jnp.zeros_like(acc)

    @pl.when(j < STEPS)
    def _():
        ext = extended(x_ref[...], xh_ref[...])
        pre = conv_pre(ext, xw_ref[...])
        sig = sigmoid(pre)
        values = pre * sig
        heads, to_heads = expander(j), collector(j)
        step = dot_nn(step_ref[...], heads)
        cum = dot_nn(cum_ref[...], heads)
        last = cum[ROWS - 1 : ROWS]
        scaled = values * step
        scaled_parts = split2(scaled)
        dy = dy_ref[...]
        dy_parts = split2(dy)
        sides = []
        for pair in range(WIDE // 128):
            top = jnp.zeros((HALF, 128), F32)
            bottom = jnp.zeros((HALF, 128), F32)
            at = slice(pair * 128, pair * 128 + 128)
            own = [part[:, at] for part in scaled_parts]
            for i in (2 * pair, 2 * pair + 1):
                row = cumt_ref[pl.ds((WIDE // HEADDIM) * j + i, 1), :]
                column = cum[:, i * HEADDIM : i * HEADDIM + 1]
                part = head_lanes(dy_parts, i)
                decay = decay_block(row, column[0:HALF])
                top = top + fine(dot_nn, split2(gt_ref[0:HALF, :] * decay), part)
                dgt_acc[0:HALF, :] += fine(dot_nt, [v[0:HALF] for v in own], part) * decay
                decay = decay_block(row[:, HALF:ROWS], column[HALF:ROWS])
                late_part = [v[HALF:ROWS] for v in part]
                bottom = bottom + fine(dot_nn, split2(gt_ref[HALF:ROWS, HALF:ROWS] * decay), late_part)
                dgt_acc[HALF:ROWS, HALF:ROWS] += fine(dot_nt, [v[HALF:ROWS] for v in own], late_part) * decay
            sides.append(jnp.concatenate([top, bottom], axis=0))
        car, late = car_ref[...], late_ref[...]
        to_end = jnp.exp(last - cum)
        d_ended = dot_nn(b_ref[:, 0:128], late)
        ended = scaled * to_end
        dc_acc[...] += fine(dot_nt, split2(dy * jnp.exp(cum)), split2(car))
        db_acc[...] += dot_nt(ended.astype(BF16), late)
        d_total = jnp.concatenate(sides, axis=1) + to_end * d_ended
        skip_w = lp_ref[0:1, :]
        dcum_acc[...] += collect(dy * (y_ref[...] - skip_w * values) - scaled * d_total, to_heads)
        dstep_acc[...] += collect(d_total * values, to_heads)
        at_last = jnp.exp(last) * jnp.sum(late.astype(F32) * car, axis=0, keepdims=True)
        at_last = at_last + jnp.sum(ended * d_ended, axis=0, keepdims=True)
        skip = jnp.sum(dy * values, axis=0, keepdims=True)
        rows_acc[...] += collect(jnp.concatenate([at_last, skip, jnp.zeros((6, WIDE), F32)], axis=0), to_heads)
        d_pre = (skip_w * dy + step * d_total) * (sig + values * (1.0 - sig))
        taps_ref[...] = tap_grads(d_pre, ext)
        head_ref[...] = d_pre[0:8]
        d_conv = conv_back(d_pre, xw_ref[...])
        dx_ref[...] = d_conv.astype(BF16)
        tail_ref[...] = d_conv[ROWS - 16 : ROWS]

    @pl.when(j == STEPS)
    def _():
        seen = iota((ROWS, ROWS), 1) >= iota((ROWS, ROWS), 0)
        d_gt = split2(jnp.where(seen, dgt_acc[...], 0.0))
        d_c = dc_acc[...] + fine(dot_tn, d_gt, halves(b_ref))
        d_b = db_acc[...] + fine(dot_nn, d_gt, halves(c_ref))
        ext_bc = extended(bc_ref[...], bch_ref[...])
        pre_bc = conv_pre(ext_bc, bcw_ref[...])
        sig_bc = sigmoid(pre_bc)
        d_pre_bc = jnp.concatenate([d_b, d_c], axis=1) * (sig_bc + pre_bc * sig_bc * (1.0 - sig_bc))
        taps_ref[...] = tap_grads(d_pre_bc, ext_bc)
        head_ref[...] = d_pre_bc[0:8]
        d_conv_bc = conv_back(d_pre_bc, bcw_ref[...])
        dx_ref[...] = d_conv_bc.astype(BF16)
        tail_ref[...] = d_conv_bc[ROWS - 16 : ROWS]

    @pl.when(j == STEPS + 1)
    def _():
        raw, step_all, rate = step_parts(raw_ref, hp_ref)
        end = iota((ROWS, 128), 0) == ROWS - 1
        d_cum_all = dcum_acc[...] + jnp.where(end, rows_acc[0:1, :], 0.0)
        d_log = exact_left(triangle(False), d_cum_all)
        d_step = dstep_acc[...] + rate * d_log
        d_raw = jnp.where(iota((ROWS, 128), 1) < HEADS, d_step * sigmoid(raw), 0.0)
        dx_ref[...] = jnp.concatenate([d_raw, jnp.zeros((ROWS, WIDE - 128), F32)], axis=1).astype(BF16)
        tail_ref[...] = dx_ref[ROWS - 16 : ROWS, :].astype(F32)
        head_ref[...] = jnp.zeros_like(head_ref)
        taps_ref[...] = jnp.zeros_like(taps_ref)
        hg_ref[...] = jnp.concatenate(
            [
                jnp.sum(d_raw, axis=0, keepdims=True),
                jnp.sum(d_log * rate * step_all, axis=0, keepdims=True),
                rows_acc[1:2, :],
                jnp.zeros((5, 128), F32),
            ],
            axis=0,
        )


def core_back(proj, halo, taps, hp, step, cum, cumt, gt, b, c, y, dy, carried, late, lp, sources=(), collective_id=None):
    acc = pltpu.VMEM((ROWS, 128), F32)

    def lanes(rows, first=0):
        return pl.BlockSpec((rows, WIDE), lambda j: (0, first + jnp.minimum(j, STEPS - 1)))

    def out(rows):
        return pl.BlockSpec((rows, WIDE), lambda j: (0, j))

    specs, shapes, sems = spread_specs(sources)
    body = spreading(
        core_back_kernel, 19, 5, len(sources),
        lambda: pl.program_id(0) == 0, lambda: pl.program_id(0) == STEPS + 1,
    )
    return pl.pallas_call(
        body,
        grid=(STEPS + 2,),
        in_specs=[
            lanes(ROWS, STEPS), fixed(ROWS, 2 * STEPS), fixed(ROWS, 50, 128),
            lanes(8), fixed(8, STEPS), lanes(8), fixed(8, STEPS), whole((8, 128)),
            whole((ROWS, 384)), whole((ROWS, 384)), whole((128, ROWS)), whole((ROWS, ROWS)),
            whole((ROWS, 256)), whole((ROWS, 384)),
            lanes(ROWS), lanes(ROWS), lanes(128), lanes(128), lanes(8), *specs,
        ],
        out_specs=[out(ROWS), out(16), out(8), out(8), whole((8, 128)), *specs],
        out_shape=[
            sds(ROWS, REST, BF16), sds(16, REST, F32), sds(8, REST, F32), sds(8, REST, F32), sds(8, 128, F32), *shapes,
        ],
        scratch_shapes=[pltpu.VMEM((ROWS, ROWS), F32), acc, acc, acc, acc, pltpu.VMEM((8, 128), F32), *sems],
        compiler_params=call_params(collective_id),
        cost_estimate=pl.CostEstimate(flops=8 * 10**9, bytes_accessed=14 * MIB, transcendentals=5 * 10**6),
    )(
        proj, proj, proj, halo, halo, taps, taps, hp,
        step, cum, cumt, gt, b, c, y, dy, carried, late, lp, *sources,
    )


def row_copies(layer, gate, rest, gate_in, rest_in, sems, spot, base, core, mine):
    send_g, recv_g, send_r, recv_r = sems
    rows = gate_in.shape[1]
    copies = []
    for k in range(1 if mine else 0, PLANE):
        peer = lax.rem(spot + k, PLANE)
        block = pl.ds(pl.multiple_of(peer * rows, rows), rows)
        at = 2 * k + core
        for src, dst, send, recv in ((gate, gate_in, send_g, recv_g), (rest, rest_in, send_r, recv_r)):
            copies.append(
                pltpu.make_async_remote_copy(
                    src_ref=src.at[block], dst_ref=dst.at[2 * spot + core], send_sem=send.at[at],
                    recv_sem=recv.at[at], device_id=(layer, base + peer), device_id_type=MESH,
                )
            )
    return copies


def keep_rows(layer, gate, rest, gate_in, rest_in, spot):
    rows = gate_in.shape[1]
    block = pl.ds(pl.multiple_of(spot * rows, rows), rows)
    gate_in[2 * spot + layer] = gate[block, :]
    rest_in[2 * spot + layer] = rest[block, :]


def wait_rows(layer, gate, rest, gate_in, rest_in, sems, spot, base):
    for core in range(2):
        for copy in row_copies(layer, gate, rest, gate_in, rest_in, sems, spot, base, core, core == layer):
            copy.wait_recv()


def early_kernel(n, gate, rest, gate_in, rest_in, send_g, recv_g, send_r, recv_r):
    core, q = lax.axis_index("section"), lax.axis_index("seq")
    spot = lax.rem(q, PLANE)
    base = q - spot
    sems = (send_g, recv_g, send_r, recv_r)
    barrier = pltpu.get_barrier_semaphore()

    @pl.when(core == 1)
    def _():
        for k in range(PLANE):
            for other in range(2 if k else 1):
                to = (other, base + lax.rem(spot + k, PLANE))
                pl.semaphore_signal(barrier, inc=1, device_id=to, device_id_type=MESH)

    pl.semaphore_wait(barrier, PLANE - core)
    for side in range(2):

        @pl.when(core == side)
        def _():
            copies = row_copies(1, gate, rest, gate_in, rest_in, sems, spot, base, side, side == 1)
            for copy in copies:
                copy.start()
            if side:
                keep_rows(1, gate, rest, gate_in, rest_in, spot)
            for copy in copies:
                copy.wait_send()
            if side:
                wait_rows(1, gate, rest, gate_in, rest_in, sems, spot, base)


def settle_early(gate, rest, n):
    vmem = pl.BlockSpec(memory_space=pltpu.VMEM)
    dma = pltpu.SemaphoreType.DMA
    rows, eight = D // n, 2 * PLANE
    return pl.pallas_call(
        functools.partial(early_kernel, n),
        out_shape=[
            jax.ShapeDtypeStruct((eight, rows, gate.shape[1]), BF16),
            jax.ShapeDtypeStruct((eight, rows, rest.shape[1]), BF16),
        ],
        in_specs=[vmem, vmem],
        out_specs=[vmem, vmem],
        scratch_shapes=[dma((eight,)), dma((eight,)), dma((eight,)), dma((eight,))],
        compiler_params=pltpu.CompilerParams(collective_id=8, has_side_effects=True, vmem_limit_bytes=32 * MIB),
    )(gate, rest)


def settle_kernel(
    n, gate, rest, gate_1, rest_1, ow0, ow1, a0, a1, d0, d1, gin_ref, gout_ref, acts_ref, grads_ref,
    gate_in, rest_in, out_in, send_g, recv_g, send_r, recv_r, send_o, recv_o, send_x, recv_x, keep_x,
):
    core = lax.axis_index("section")
    q = lax.axis_index("seq")
    spot = lax.rem(q, PLANE)
    base = q - spot
    sems = (send_g, recv_g, send_r, recv_r)
    barrier = pltpu.get_barrier_semaphore()
    for k in range(PLANE):
        for flip in range(2):
            if k or flip:
                to = (core ^ flip, base + lax.rem(spot + k, PLANE))
                pl.semaphore_signal(barrier, inc=1, device_id=to, device_id_type=MESH)
    pl.semaphore_wait(barrier, 2 * PLANE - 1)

    def fill(gates, rests):
        for p in range(2 * PLANE):
            wide = gates.shape[2]
            gin_ref[:, p * wide : p * wide + wide] = gates[p].astype(F32)
            wide = rests.shape[2]
            at = INNER + p * wide
            width = min(wide, PROJ - at)
            gin_ref[:, at : at + width] = rests[p].astype(F32)[:, :width]

    def run(layer, outw, act, grad, away_act, away_grad, away_outw):
        rows = row_copies(0, gate, rest, gate_in, rest_in, sems, spot, base, layer, layer == 0)
        for copy in rows:
            copy.start()
        copies = []

        def send(src, dst, sems, at):
            copy = pltpu.make_async_remote_copy(
                src_ref=src, dst_ref=dst, send_sem=sems[0].at[at], recv_sem=sems[1].at[at],
                device_id=(1 - layer, q), device_id_type=MESH,
            )
            copy.start()
            copies.append(copy)

        for at, (own, away, dst) in enumerate(((grad, away_grad, grads_ref), (act, away_act, acts_ref))):
            send(away, dst.at[layer], (send_x, recv_x), at)
            copies.append(pltpu.make_async_copy(own, dst.at[layer], keep_x.at[at]))
            copies[-1].start()
        send(away_outw, out_in, (send_o, recv_o), 0)
        half = D // 2
        gout_ref[:, layer * half : layer * half + half] = outw[...].astype(F32)
        if layer:
            fill(gate_1, rest_1)
        else:
            keep_rows(0, gate, rest, gate_in, rest_in, spot)
        for copy in rows:
            copy.wait_send()
        if not layer:
            wait_rows(0, gate, rest, gate_in, rest_in, sems, spot, base)
            fill(gate_in, rest_in)
        for copy in copies:
            copy.wait()
        gout_ref[:, (1 - layer) * half : (1 - layer) * half + half] = out_in[...].astype(F32)

    @pl.when(core == 0)
    def _():
        run(0, ow0, a0, d0, a1, d1, ow1)

    @pl.when(core == 1)
    def _():
        run(1, ow1, a1, d1, a0, d0, ow0)


def settle(gate, rest, early, outs, acts, grads, n):
    vmem = pl.BlockSpec(memory_space=pltpu.VMEM)
    anywhere = pl.BlockSpec(memory_space=pl.ANY)
    dma = pltpu.SemaphoreType.DMA
    rows = D // n
    eight = 2 * PLANE
    return pl.pallas_call(
        functools.partial(settle_kernel, n),
        out_shape=[
            sds(rows, PROJ, F32), sds(INNER // n, D, F32),
            jax.ShapeDtypeStruct((2, ROWS, D), BF16), jax.ShapeDtypeStruct((2, ROWS, D), F32),
        ],
        in_specs=[vmem] * 6 + [anywhere] * 4,
        out_specs=[vmem, vmem, anywhere, anywhere],
        scratch_shapes=[
            pltpu.VMEM((eight, rows, gate.shape[1]), BF16),
            pltpu.VMEM((eight, rows, rest.shape[1]), BF16),
            pltpu.VMEM((INNER // n, D // 2), BF16),
            dma((eight,)), dma((eight,)), dma((eight,)), dma((eight,)),
            dma((1,)), dma((1,)), dma((2,)), dma((2,)), dma((2,)),
        ],
        compiler_params=pltpu.CompilerParams(collective_id=3, has_side_effects=True, vmem_limit_bytes=40 * MIB),
    )(gate, rest, early[0], early[1], outs[0], outs[1], acts[0], acts[1], grads[0], grads[1])


def swap(value):
    return lax.ppermute(value, "section", [(0, 1), (1, 0)])


def shifted(value, distance, n):
    return lax.ppermute(value, "seq", [(i, i + distance) for i in range(n) if 0 <= i + distance < n])


def plane_route(k, n):
    return [(i, i - i % PLANE + (i + k) % PLANE) for i in range(n)]


def rms(value):
    return lax.rsqrt(jnp.mean(value * value, axis=-1, keepdims=True) + EPS)


def tied(value, *others):
    return lax.optimization_barrier((value, *others))[0]


def copies_of(value, n):
    return [value] + [lax.ppermute(value, "seq", plane_route(k, n)) for k in range(1, PLANE)]


def arrived(value, *lists):
    value, *rest = lax.optimization_barrier((value, *(copy for copies in lists for copy in copies)))
    return (value, *(jnp.stack(rest[k * PLANE : (k + 1) * PLANE]) for k in range(len(lists))))


def partial_grad(left, right):
    core = lax.axis_index("section")
    half = right.shape[2] // 2

    def part(side):
        cols = lax.dynamic_slice_in_dim(right, side * half, half, 2)
        return lax.dot_general(left, cols, (((0, 1), (0, 1)), ((), ())), preferred_element_type=F32)

    away = part(1 - core).astype(BF16)
    return (part(core) + swap(away).astype(F32)).astype(BF16)


def plane_rows(partial, n):
    columns = [[p + PLANE * z for z in range(n // PLANE)] for p in range(PLANE)]
    return lax.psum_scatter(partial, "seq", scatter_dimension=0, axis_index_groups=columns, tiled=True)


SIZES = [D, CONVD * CONV, CONVD, HEADS, HEADS, HEADS, INNER]


def split_small(flat):
    parts, at = [], 0
    for size in SIZES:
        parts.append(flat[at : at + size])
        at += size
    return parts


def unpack_params(flat):
    norm_g, conv_w, conv_b, dt_b, a_lg, skip_w, gate_g = split_small(flat)
    taps = jnp.concatenate(
        [conv_w.reshape(CONV, CONVD), conv_b[None], jnp.zeros((3, CONVD), F32)], axis=0
    )
    pad = jnp.zeros((128 - HEADS,), F32)
    hp = jnp.concatenate([dt_b, pad, a_lg, pad, jnp.zeros((6 * 128,), F32)]).reshape(8, 128)
    lp = jnp.concatenate(
        [jnp.repeat(skip_w, HEADDIM)[None], gate_g[None], jnp.zeros((6, INNER), F32)], axis=0
    )
    return norm_g, taps, hp, lp


def per_device(
    inputs, cotangent, norm_gain, in_weight, conv_weight, conv_bias, dt_bias, a_log, d_skip,
    gate_norm_gain, out_weight,
):
    n = lax.axis_size("seq")
    core = lax.axis_index("section")
    place = lax.axis_index("seq")
    first = core == 0
    own_in, own_out = in_weight[0].T, out_weight[0]
    other_in = swap(own_in)
    own_small = jnp.concatenate(
        [
            norm_gain[0], conv_weight[0].T.reshape(-1), conv_bias[0], dt_bias[0], a_log[0], d_skip[0],
            gate_norm_gain[0],
        ]
    )
    other_small = swap(own_small)
    flags = [(core == layer).astype(jnp.int32)[None] for layer in range(2)]
    params = [
        unpack_params(jnp.where(first, own_small, other_small)),
        unpack_params(jnp.where(first, other_small, own_small)),
    ]

    def mine(pair):
        return lax.dynamic_index_in_dim(pair, core, 0, keepdims=False)

    def normed_of(layer, h):
        return (h * rms(h) * params[layer][0]).astype(BF16)

    def project(layer, normed, before):
        proj, halo = project_mm(normed, normed_of(layer, before.astype(F32)), own_in, other_in, flags[layer], 1664)
        return proj, halo[8:, INNER : INNER + CONVD]

    def blocks(layer, proj, halo):
        _, taps, hp, _ = params[layer]
        return front(proj, halo, taps, hp)

    def finish(layer, h, proj, parts, carried):
        values, _, _, step, cum, cumt, _, c, _, g, _ = parts[:11]
        y, gated_low, owned = mix(g, step, cum, cumt, values, proj, c, carried, params[layer][3], n)
        return y, owned, gated_low

    def output(layer, h, gated_low):
        return (h + mm(gated_low, own_out, other_out, flags[layer], False, 768)).astype(BF16)

    x_0 = mine(inputs)
    before_0 = shifted(x_0[ROWS - 16 :], 1, n)
    d_out_1 = mine(cotangent)
    h_0 = x_0.astype(F32)
    normed_0 = normed_of(0, h_0)
    normed_0, lows_1 = arrived(normed_0, copies_of(d_out_1, n))
    proj_0, halo_0 = project(0, normed_0, before_0)
    other_out = swap(tied(own_out, proj_0))
    parts_0 = blocks(0, proj_0, halo_0)
    carried_0 = exchange(parts_0[1], parts_0[2], n, False)
    normeds_0 = copies_of(tied(normed_0, carried_0), n)
    y_0, owned_0, low_0 = finish(0, h_0, proj_0, parts_0, carried_0)
    act_0 = output(0, h_0, low_0)

    before_1 = shifted(act_0[ROWS - 16 :], 1, n)
    h_1 = act_0.astype(F32)
    normed_1 = normed_of(1, h_1)
    normeds_1 = copies_of(tied(normed_1, before_1), n)
    proj_1, halo_1 = project(1, normed_1, before_1)
    parts_1 = blocks(1, proj_1, halo_1)
    carried_1 = exchange(parts_1[1], parts_1[2], n, False)
    carried_1, normeds_0, normeds_1 = arrived(carried_1, normeds_0, normeds_1)
    y_1, owned_1, low_1 = finish(1, h_1, proj_1, parts_1, carried_1)

    def gate_side(layer, d_low, y, proj, parts, *spread):
        d_gated_low = mm(d_low, own_out, other_out, flags[layer], True, 1024)
        return gate_back(d_gated_low, y, proj, parts[4], parts[8], params[layer][3], *spread)

    def core_side(layer, proj, halo, parts, y, dy, carried, late, *spread):
        _, taps, hp, lp = params[layer]
        _, _, _, step, cum, cumt, b, c, _, _, gt = parts[:11]
        return core_back(proj, halo, taps, hp, step, cum, cumt, gt, b, c, y, dy, carried, late, lp, *spread)

    def conv_side(layer, back):
        rest, tail, head = back[:3]
        w = jnp.concatenate([params[layer][1], jnp.zeros((8, REST - CONVD), F32)], axis=1)
        a = shifted(head, -1, n)
        fix = jnp.concatenate(
            [
                jnp.zeros((13, REST), F32),
                w[0:1] * a[0:1],
                w[0:1] * a[1:2] + w[1:2] * a[0:1],
                w[0:1] * a[2:3] + w[1:2] * a[1:2] + w[2:3] * a[0:1],
            ],
            axis=0,
        )
        return lax.dynamic_update_slice(rest, (tail + fix).astype(BF16), (ROWS - 16, 0))

    def norm_side(layer, h, d_out, d_gate, rest):
        norm_g = params[layer][0]
        d_normed = back_mm(d_gate, rest, own_in, other_in, flags[layer], 512)
        r = rms(h)
        v = d_normed * norm_g
        d_h = d_out + r * (v - h * (r * r * jnp.mean(v * h, axis=-1, keepdims=True)))
        return d_h, jnp.sum(d_normed * h * r, axis=0)

    def small_of(norm_gain_grad, back, gate_gain):
        taps_all, heads = back[3][:, :CONVD], back[4]
        return jnp.concatenate(
            [
                norm_gain_grad, taps_all[:CONV].reshape(-1), taps_all[CONV],
                heads[0, :HEADS], heads[1, :HEADS], heads[2, :HEADS], gate_gain[0],
            ]
        )

    dy_1, d_gate_1, gain_1, d_carried_1, gateds_0 = gate_side(
        1, tied(d_out_1, carried_1), y_1, proj_1, parts_1, (owned_0,), 4
    )
    late_1 = exchange(d_carried_1, parts_1[2], n, True)
    back_1 = core_side(
        1, proj_1, halo_1, parts_1, y_1, dy_1, carried_1, late_1, (d_gate_1, owned_1), 5
    )
    gates_1, gateds_1 = back_1[5:]
    outw_1 = partial_grad(gateds_1, lows_1)
    gatew_1 = partial_grad(normeds_1, gates_1)
    rest_1 = conv_side(1, back_1)
    rest_1 = tied(rest_1, outw_1, gatew_1)
    outw_1, gatew_1 = plane_rows(outw_1, n), plane_rows(gatew_1, n)
    d_1, ng_1 = norm_side(1, h_1, d_out_1.astype(F32), d_gate_1, rest_1)

    d_out_0 = d_1.astype(BF16)
    dy_0, d_gate_0, gain_0, d_carried_0, rests_1 = gate_side(0, d_out_0, y_0, proj_0, parts_0, (rest_1,), 6)
    restw_1 = partial_grad(normeds_1, rests_1)
    late_0 = exchange(tied(d_carried_0, restw_1, outw_1, gatew_1), parts_0[2], n, True)
    restw_1 = plane_rows(tied(restw_1, late_0), n)
    lows_0 = copies_of(tied(d_out_0, late_0), n)
    back_0 = core_side(
        0, proj_0, halo_0, parts_0, y_0, dy_0, carried_0, late_0, (d_gate_0,), 7
    )
    gates_0, lows_0 = arrived(back_0[5], lows_0)
    gatew_0 = partial_grad(normeds_0, gates_0)
    outw_0 = plane_rows(partial_grad(gateds_0, lows_0), n)
    rest_0 = conv_side(0, back_0)
    rest_0 = tied(rest_0, gatew_0)
    gatew_0 = plane_rows(gatew_0, n)
    spot = place % PLANE
    width = REST // PLANE
    pieces = [lax.dynamic_slice_in_dim(rest_0, (spot + k) % PLANE * width, width, 1) for k in range(PLANE)]
    rests_0 = pieces[:1] + [lax.ppermute(pieces[k], "seq", plane_route(k, n)) for k in range(1, PLANE)]
    d_0, ng_0 = norm_side(0, h_0, d_out_0.astype(F32), d_gate_0, rest_0)
    ng_0, rests_0 = arrived(ng_0, rests_0)
    restw_0 = partial_grad(normeds_0, rests_0)
    act_1 = output(1, h_1, tied(low_1, restw_0))
    early = settle_early(tied(gatew_1, restw_0), restw_1, n)
    restw_0 = plane_rows(restw_0, n)

    g_in, g_out, acts, input_grads = settle(
        gatew_0, restw_0, early, (outw_0, outw_1), (act_0, act_1), (d_0, d_1), n
    )
    small_0, small_1 = small_of(ng_0, back_0, gain_0), small_of(ng_1, back_1, gain_1)
    small = jnp.where(first, small_0, small_1) + swap(jnp.where(first, small_1, small_0))
    reach = 1
    while reach < n:
        small = small + lax.ppermute(small, "seq", [(i, i ^ reach) for i in range(n)])
        reach *= 2
    norm_g, conv_w, conv_b, dt_b, a_lg, skip_w, gate_g = split_small(small)

    def share(value):
        rows = value.shape[0] // n
        return lax.dynamic_slice_in_dim(value, place * rows, rows, 0)[None]

    conv_rows = CONVD // n
    conv_w = lax.dynamic_slice_in_dim(conv_w.reshape(CONV, CONVD), place * conv_rows, conv_rows, 1).T
    return (
        acts[None], input_grads[None], share(norm_g), g_in[None], conv_w[None], share(conv_b),
        dt_b[None], a_lg[None], skip_w[None], share(gate_g), g_out[None],
    )


def solution(mesh):
    in_specs = (
        P(None, "seq", None), P(None, "seq", None), P("section", None), P("section", None, None),
        P("section", None, None), P("section", None), P("section", None), P("section", None),
        P("section", None), P("section", None), P("section", None, None),
    )
    out_specs = (
        P("section", None, "seq", None), P("section", None, "seq", None), P("section", "seq"),
        P("section", "seq", None), P("section", "seq", None), P("section", "seq"), P("section", None),
        P("section", None), P("section", None), P("section", "seq"), P("section", "seq", None),
    )
    return jax.shard_map(per_device, mesh=mesh, in_specs=in_specs, out_specs=out_specs, check_vma=False)
```
